32 devices in a mesh: section: 2 (over core), wide: 8 (over z, x), fc: 2 (over y).
Axes of the slice: x: 2, y: 2, z: 4, core: 2. Of those that a mesh axis runs over, the one named last changes fastest.
Arguments:
- map_p2: float32 [8, 48, 96, 256], P('wide', 'section', None, 'fc'), may hold values from -6 to 6
- map_p3: float32 [8, 24, 48, 256], P('wide', 'section', None, 'fc'), may hold values from -6 to 6
- map_p4: float32 [8, 12, 24, 256], P('wide', 'section', None, 'fc'), may hold values from -6 to 6
- map_p5: float32 [8, 6, 12, 256], P('wide', 'section', None, 'fc'), may hold values from -6 to 6
- boxes: float32 [4096, 4], P('wide'), may hold values from 0.2 to 0.8
- levels: int32 [4096], P('wide'), may hold values from 0 to 3
- classes: int32 [4096], P('wide'), may hold values from 0 to 80
- sampled: int32 [4096], P('wide'), may hold values 0 or 1
- counts: int32 [8], P('wide'), may hold values from 1 to 512, as said below
- targets: float32 [4096, 4], P('wide'), may hold values from -6 to 6
- first_weight: float32 [12544, 1024], P('fc', ('section', 'wide')), may hold values from -0.0546875 to 0.0546875
- second_weight: float32 [1024, 1024], P('fc', ('section', 'wide')), may hold values from -0.1875 to 0.1875
- out_weight: float32 [1024, 401], P(('section', 'wide', 'fc')), may hold values from -0.75 to 0.75
- hidden_bias: float32 [1024, 2], P(('section', 'wide', 'fc')), may hold values from -2 to 2
- out_bias: float32 [401], replicated, may hold values from -2 to 2
- first_moment: float32 [12544, 1024], P('fc', ('section', 'wide')), may hold values from -0.0034179688 to 0.0034179688
- second_moment: float32 [1024, 1024], P('fc', ('section', 'wide')), may hold values from -0.0068359375 to 0.0068359375
- out_moment: float32 [1024, 401], P(('section', 'wide', 'fc')), may hold values from -0.0625 to 0.0625
- hidden_moment: float32 [1024, 2], P(('section', 'wide', 'fc')), may hold values from -0.0234375 to 0.0234375
- bias_moment: float32 [401], replicated, may hold values from -0.3125 to 0.3125
- first_average: float32 [12544, 1024], P('fc', ('section', 'wide')), may hold values from -0.0546875 to 0.0546875
- second_average: float32 [1024, 1024], P('fc', ('section', 'wide')), may hold values from -0.1875 to 0.1875
- out_average: float32 [1024, 401], P(('section', 'wide', 'fc')), may hold values from -0.75 to 0.75
- hidden_average: float32 [1024, 2], P(('section', 'wide', 'fc')), may hold values from -2 to 2
- bias_average: float32 [401], replicated, may hold values from -2 to 2
Outputs:
- loss_sum: float32 [], replicated
- roi_count: float32 [], replicated
- grad_p2: float32 [8, 48, 96, 256], P('wide', 'section', None, 'fc')
- grad_p3: float32 [8, 24, 48, 256], P('wide', 'section', None, 'fc')
- grad_p4: float32 [8, 12, 24, 256], P('wide', 'section', None, 'fc')
- grad_p5: float32 [8, 6, 12, 256], P('wide', 'section', None, 'fc')
- first_new: float32 [12544, 1024], P('fc', ('section', 'wide'))
- first_moment_new: float32 [12544, 1024], P('fc', ('section', 'wide'))
- first_average_new: float32 [12544, 1024], P('fc', ('section', 'wide'))
- second_new: float32 [1024, 1024], P('fc', ('section', 'wide'))
- second_moment_new: float32 [1024, 1024], P('fc', ('section', 'wide'))
- second_average_new: float32 [1024, 1024], P('fc', ('section', 'wide'))
- out_new: float32 [1024, 401], P(('section', 'wide', 'fc'))
- out_moment_new: float32 [1024, 401], P(('section', 'wide', 'fc'))
- out_average_new: float32 [1024, 401], P(('section', 'wide', 'fc'))
- hidden_new: float32 [1024, 2], P(('section', 'wide', 'fc'))
- hidden_moment_new: float32 [1024, 2], P(('section', 'wide', 'fc'))
- hidden_average_new: float32 [1024, 2], P(('section', 'wide', 'fc'))
- bias_new: float32 [401], replicated
- bias_moment_new: float32 [401], replicated
- bias_average_new: float32 [401], replicated
The draws below stay inside these ranges and needn't reach their ends.
Inputs may be any that keep to these rules, and one draw needn't show every extreme that they name: The live slots of each image are its first counts slots; one image uses all 512.
All inputs are finite; a program needn't handle non-finite values. No bound on the sum of `sampled` on one device may be relied on, other than what follows from the above.
Results may differ from the reference program's by a relative error of at most 0.02.
Values may be sent and summed in bfloat16 or wider, within the bound.
No kernel may reach another device: no remote copies, remote signals or barrier semaphores. Data moves between devices by JAX's collectives and lax.ppermute only.
A program may use at most 640 MiB of HBM per device.

```python
import math
import jax
import jax.numpy as jnp
import numpy as np
from jax import lax

C = 256
HID = 1024
CLASSES = 81
H2 = 48
W2 = 96
R_DEV = 512
IMAGES = 8
ROIS = 4096


def draw_counts(key, part):
    key = jax.random.fold_in(key, 7)
    images = jnp.arange(IMAGES, dtype=jnp.int32)
    floor_count = R_DEV // 3 + images * (R_DEV - R_DEV // 3) // max(IMAGES - 1, 1)
    jitter = jax.random.randint(key, (IMAGES,), 0, R_DEV // 8 + 1)
    drawn = jnp.maximum(floor_count - jitter, 1)
    return jnp.where(images == IMAGES - 1, R_DEV, drawn).astype(jnp.int32)


def with_ends(values, rng, least, top_value):
    shape = values.shape
    index_at = [jax.random.randint(jax.random.fold_in(rng, axis), (), 0, shape[axis]) for axis in range(len(shape))]
    values = values.at[tuple(index_at)].set(least)
    longest = shape.index(max(shape))
    index_at[longest] = (index_at[longest] + 1) % shape[longest]
    return values.at[tuple(index_at)].set(top_value)


def block_scale(own_key, shape, cuts, least, largest):
    factor_of = 1.0
    for axis_at, blocks in cuts:
        heights = jax.random.uniform(jax.random.fold_in(jax.random.fold_in(own_key, 6), axis_at), (blocks,), jnp.float32, least / len(cuts), largest / len(cuts))
        factor_of = factor_of * jnp.repeat(jnp.exp(heights), shape[axis_at] // blocks).reshape((-1,) + (1,) * (len(shape) - 1 - axis_at))
    return factor_of


def rank_bounds(number_of, skew):
    weights = [(1 << 20) // math.isqrt(standing ** skew) + 1 for standing in range(1, number_of + 1)]
    deviation = 1 + sum(weights) // (1 << 30)
    return np.cumsum(np.array([max(1, weight // deviation) for weight in weights]))


def ranked_ids(rng, dims, count, lean):
    table = rank_bounds(count, lean)
    ticket = jax.random.randint(jax.random.fold_in(rng, 1), dims, 0, int(table[count - 1]))
    rank = jnp.searchsorted(jnp.asarray(table, jnp.int32), ticket, side="right")
    return jax.random.permutation(jax.random.fold_in(rng, 2), count)[rank].astype(jnp.int32)


def noise(rng, dims, spread, limit, cuts=(), kind=jnp.bfloat16):
    entries = jax.random.normal(rng, dims, jnp.float32) * spread
    if len(cuts) > 0:
        entries = block_scale(rng, dims, cuts, -0.22, 0.18) * entries
    return jnp.clip(entries, min=-limit, max=limit).astype(kind)


def setup_inputs(seed: int = 0) -> dict:
    key_list = jax.random.split(jax.random.key(seed), 26)
    map_p2 = noise(key_list[0], (IMAGES, H2, W2, C), 1.0, 6.0, ((0, 8), (1, 2), (3, 2)), jnp.float32)
    map_p3 = noise(key_list[1], (IMAGES, H2 // 2, W2 // 2, C), 1.0, 6.0, ((0, 8), (1, 2), (3, 2)), jnp.float32)
    map_p4 = noise(key_list[2], (IMAGES, H2 // 4, W2 // 4, C), 1.0, 6.0, ((0, 8), (1, 2), (3, 2)), jnp.float32)
    map_p5 = noise(key_list[3], (IMAGES, H2 // 8, W2 // 8, C), 1.0, 6.0, ((0, 8), (1, 2), (3, 2)), jnp.float32)
    boxes = jnp.clip(0.2 + 0.6 * jax.random.uniform(key_list[4], (ROIS, 4), jnp.float32) ** block_scale(key_list[4], (ROIS, 4), ((0, 8),), -0.2, 0.2), 0.2, 0.8)
    levels = with_ends(ranked_ids(key_list[5], (ROIS,), 4, 2), jax.random.fold_in(key_list[5], 3), 0, 3).astype(jnp.int32)
    classes = with_ends(jax.random.randint(key_list[6], (ROIS,), 0, CLASSES), jax.random.fold_in(key_list[6], 1), 0, CLASSES - 1).astype(jnp.int32)
    sampled = with_ends((jax.random.randint(key_list[7], (ROIS,), 0, 4) < 3).astype(jnp.int32), jax.random.fold_in(key_list[7], 1), 0, 1)
    counts = draw_counts(jax.random.fold_in(key_list[25], 71), 0)
    targets = noise(key_list[9], (ROIS, 4), 1.0, 6.0, ((0, 8),), jnp.float32)
    first_weight = noise(key_list[10], (C * 49, HID), (C * 49) ** -0.5, 0.0546875, ((0, 2), (1, 16)), jnp.float32)
    second_weight = noise(key_list[11], (HID, HID), HID ** -0.5, 0.1875, ((0, 2), (1, 16)), jnp.float32)
    out_weight = noise(key_list[12], (HID, 5 * CLASSES - 4), (HID // 16) ** -0.5, 0.75, ((0, 32),), jnp.float32)
    hidden_bias = noise(key_list[13], (HID, 2), 0.3, 2.0, ((0, 32),), jnp.float32)
    out_bias = noise(key_list[14], (5 * CLASSES - 4,), 0.3, 2.0, (), jnp.float32)
    first_moment = noise(key_list[15], (C * 49, HID), (0.015 / ROIS ** 0.5), 0.0034179688, ((0, 2), (1, 16)), jnp.float32)
    second_moment = noise(key_list[16], (HID, HID), (0.03 / ROIS ** 0.5), 0.0068359375, ((0, 2), (1, 16)), jnp.float32)
    out_moment = noise(key_list[17], (HID, 5 * CLASSES - 4), (0.3 / ROIS ** 0.5), 0.0625, ((0, 32),), jnp.float32)
    hidden_moment = noise(key_list[18], (HID, 2), (0.1 / ROIS ** 0.5), 0.0234375, ((0, 32),), jnp.float32)
    bias_moment = noise(key_list[19], (5 * CLASSES - 4,), 0.02, 0.3125, (), jnp.float32)
    first_average = noise(key_list[20], (C * 49, HID), (C * 49) ** -0.5, 0.0546875, ((0, 2), (1, 16)), jnp.float32)
    second_average = noise(key_list[21], (HID, HID), HID ** -0.5, 0.1875, ((0, 2), (1, 16)), jnp.float32)
    out_average = noise(key_list[22], (HID, 5 * CLASSES - 4), (HID // 16) ** -0.5, 0.75, ((0, 32),), jnp.float32)
    hidden_average = noise(key_list[23], (HID, 2), 0.3, 2.0, ((0, 32),), jnp.float32)
    bias_average = noise(key_list[24], (5 * CLASSES - 4,), 0.3, 2.0, (), jnp.float32)
    return dict(map_p2=map_p2, map_p3=map_p3, map_p4=map_p4, map_p5=map_p5, boxes=boxes, levels=levels, classes=classes, sampled=sampled, counts=counts, targets=targets, first_weight=first_weight, second_weight=second_weight, out_weight=out_weight, hidden_bias=hidden_bias, out_bias=out_bias, first_moment=first_moment, second_moment=second_moment, out_moment=out_moment, hidden_moment=hidden_moment, bias_moment=bias_moment, first_average=first_average, second_average=second_average, out_average=out_average, hidden_average=hidden_average, bias_average=bias_average)


@jax.custom_vjp
def low(v):
    return lax.optimization_barrier(v.astype(jnp.bfloat16)).astype(jnp.float32)

@jax.custom_vjp
def low_back(v):
    return v

def low_keep(v):
    return (low(v), None)

def low_pass(kept, grad):
    return (grad,)

def back_keep(v):
    return (v, None)

def back_low(kept, grad):
    return (low(grad),)
low.defvjp(low_keep, low_pass)
low_back.defvjp(back_keep, back_low)
MOMENTUM = 0.9
AVERAGE = 0.7
DECAY = 0.0001
SMOOTH = 0.5

def sample_cells(boxes, level, height, width, parts):
    shapes = [(height >> depth, width >> depth) for depth in range(4)]
    held = [rows // parts for rows, cols in shapes]
    starts = [0]
    for depth in range(3):
        starts.append(starts[-1] + held[depth] * shapes[depth][1])
    half_total = starts[3] + held[3] * shapes[3][1]
    matches = level[:, None] == jnp.arange(4, dtype=jnp.int32)[None, :]

    def choose(values):
        table = jnp.asarray(values, dtype=jnp.int32)[None, :]
        return lax.optimization_barrier(jnp.sum(jnp.where(matches, table, 0), axis=1)).astype(jnp.int32)
    level_rows = choose([rows for rows, cols in shapes])
    level_cols = choose([cols for rows, cols in shapes])
    level_held = choose(held)
    level_start = choose(starts)
    fraction = (jnp.arange(7, dtype=jnp.float32)[:, None] + (jnp.arange(2, dtype=jnp.float32)[None, :] + 0.5) * 0.5) / 7.0

    def corners(center, extent, count):
        reach = (count - 1).astype(jnp.float32)
        anchor = (center - 0.25 * extent) * reach
        length = 0.5 * extent * reach
        points = anchor[:, None, None] + length[:, None, None] * fraction[None]
        lower = jnp.clip(jnp.floor(points), 0.0, (count - 2).astype(jnp.float32)[:, None, None])
        upper_weight = points - lower
        index = lower.astype(jnp.int32)[..., None] + jnp.arange(2, dtype=jnp.int32)
        weight = jnp.stack([1.0 - upper_weight, upper_weight], axis=-1)
        return (index, weight)
    row_index, row_weight = corners(boxes[:, 0], boxes[:, 2], level_rows)
    col_index, col_weight = corners(boxes[:, 1], boxes[:, 3], level_cols)
    held_b = level_held[:, None, None, None]
    owner = (row_index // held_b).astype(jnp.int32)
    local_row = row_index - owner * held_b
    row_cells = owner * half_total + level_start[:, None, None, None] + local_row * level_cols[:, None, None, None]
    cells = row_cells[:, :, :, :, None, None, None] + col_index[:, None, None, None, :, :, :]
    weights = 0.25 * row_weight[:, :, :, :, None, None, None] * col_weight[:, None, None, None, :, :, :]
    return (cells.astype(jnp.int32), weights)

def crop_rows(table, cells, weights):
    values = table[cells]
    summed = jnp.einsum('rijakmbc,rijakmb->rcik', values, weights, precision=lax.Precision.HIGHEST)
    return summed.reshape(summed.shape[0], -1)

def row_losses(logits, classes, live, targets):
    scores = logits[:, :CLASSES]
    deltas = logits[:, CLASSES:].reshape(logits.shape[0], CLASSES - 1, 4)
    matches = classes[:, None] == jnp.arange(CLASSES, dtype=jnp.int32)[None, :]
    entropy = jax.nn.logsumexp(scores, axis=1) - lax.optimization_barrier(jnp.sum(jnp.where(matches, scores, 0.0), axis=1))
    chosen_class = classes[:, None] == jnp.arange(1, CLASSES, dtype=jnp.int32)[None, :]
    chosen = lax.optimization_barrier(jnp.sum(jnp.where(chosen_class[:, :, None], deltas, 0.0), axis=1))
    offset = chosen - targets
    magnitude = jnp.abs(offset)
    smooth = jnp.where(magnitude < SMOOTH, 0.5 * offset * offset / SMOOTH, magnitude - 0.5 * SMOOTH)
    foreground = (classes > 0).astype(logits.dtype)
    return live * (entropy + foreground * lax.optimization_barrier(jnp.sum(smooth, axis=1)))

def renew(weight, moment, average, grad, rate):
    step_value = grad + DECAY * weight
    moment_new = MOMENTUM * moment + step_value
    weight_new = weight - rate * (step_value + MOMENTUM * moment_new)
    average_new = AVERAGE * average + (1.0 - AVERAGE) * weight_new
    return (weight_new, moment_new, average_new)

def reference(map_p2, map_p3, map_p4, map_p5, boxes, levels, classes, sampled, counts, targets, first_weight, second_weight, out_weight, hidden_bias, out_bias, first_moment, second_moment, out_moment, hidden_moment, bias_moment, first_average, second_average, out_average, hidden_average, bias_average):
    slots = jnp.arange(ROIS, dtype=jnp.int32) % R_DEV
    live = ((slots < jnp.repeat(counts, R_DEV)) & (sampled > 0)).astype(map_p2.dtype)
    total = jnp.sum(live)
    cells, weights = sample_cells(boxes, levels, H2, W2, 1)
    cells = cells.reshape((IMAGES, R_DEV) + cells.shape[1:])
    weights = weights.reshape((IMAGES, R_DEV) + weights.shape[1:])
    highest = lax.Precision.HIGHEST

    def loss_of(maps, first, second, outw, hbias, obias):
        tables = jnp.concatenate([level_map.reshape(IMAGES, -1, C) for level_map in maps], axis=1)
        crops = lax.map(jax.checkpoint(lambda item: crop_rows(item[0], item[1], item[2])), (tables, cells, weights))
        inputs = low_back(low(crops.reshape(ROIS, C * 49)))
        pre_first = jnp.dot(inputs, low(first), precision=highest, preferred_element_type=inputs.dtype) + low(hbias[:, 0])
        act_first = low(jax.nn.gelu(low_back(pre_first)))
        pre_second = jnp.dot(act_first, low(second), precision=highest, preferred_element_type=inputs.dtype) + low(hbias[:, 1])
        act_second = low(jax.nn.gelu(low_back(pre_second)))
        logits = low_back(jnp.dot(act_second, low(outw), precision=highest, preferred_element_type=inputs.dtype) + obias)
        return jnp.sum(row_losses(logits, classes, live, targets))
    maps = [map_p2, map_p3, map_p4, map_p5]
    loss_sum, pull = jax.vjp(loss_of, maps, first_weight, second_weight, out_weight, hidden_bias, out_bias)
    grads = pull(1.0 / total)
    map_grads = grads[0]
    rate = 0.15 * math.sqrt(ROIS)
    first_out = renew(first_weight, first_moment, first_average, grads[1], rate)
    second_out = renew(second_weight, second_moment, second_average, grads[2], rate)
    out_out = renew(out_weight, out_moment, out_average, grads[3], rate)
    hidden_out = renew(hidden_bias, hidden_moment, hidden_average, grads[4], rate)
    bias_out = renew(out_bias, bias_moment, bias_average, grads[5], 4.0)
    return (loss_sum, total, map_grads[0], map_grads[1], map_grads[2], map_grads[3], first_out[0], first_out[1], first_out[2], second_out[0], second_out[1], second_out[2], out_out[0], out_out[1], out_out[2], hidden_out[0], hidden_out[1], hidden_out[2], bias_out[0], bias_out[1], bias_out[2])
```

```python
import functools
import math

import jax
import jax.numpy as jnp
from jax import lax
from jax.experimental import pallas as pl
from jax.experimental.pallas import tpu as pltpu
from jax.sharding import PartitionSpec as P

CLASSES = 81
BINS = 7
CELLS = BINS * BINS
WINDOW = 24
GROUP = 16
CHAINS = 4
PADDED = 512
MOMENTUM = 0.9
AVERAGE = 0.7
DECAY = 0.0001
SMOOTH = 0.5

F32 = jnp.float32
BF16 = jnp.bfloat16
VMEM_LIMIT = 52 * 2**20


def smem():
    return pl.BlockSpec(memory_space=pltpu.SMEM)


def vmem():
    return pl.BlockSpec(memory_space=pltpu.VMEM)


def limits():
    return pltpu.CompilerParams(vmem_limit_bytes=VMEM_LIMIT)


def level_plan(height, width):
    shapes = [(height >> depth, width >> depth) for depth in range(4)]
    strides = [max(rows, WINDOW) for rows, cols in shapes]
    bases = [0]
    for depth in range(4):
        bases.append(bases[-1] + strides[depth] * shapes[depth][1])
    total = -(-(bases[-1] + 2 * WINDOW) // GROUP) * GROUP
    return shapes, strides, bases[:4], total


def half_starts(shapes):
    starts = [0]
    for rows, cols in shapes:
        starts.append(starts[-1] + rows // 2 * cols)
    return starts


def table_kernel(height, width, place, own, other, table):
    shapes, strides, bases, total = level_plan(height, width)
    starts = half_starts(shapes)
    table[...] = jnp.zeros_like(table)

    def fill(source, bottom):
        for depth, (rows, cols) in enumerate(shapes):
            half = rows // 2

            def column(x, carry, depth=depth, half=half, cols=cols):
                cells = source[pl.ds(starts[depth] + x, half, stride=cols), :]
                table[pl.ds(bases[depth] + x * strides[depth] + bottom * half, half), :] = cells
                return carry

            lax.fori_loop(0, cols, column, 0, unroll=4)

    bottom = place[0]
    fill(own, bottom)
    fill(other, 1 - bottom)


def build_table(place, own, other, height, width):
    total = level_plan(height, width)[3]
    return pl.pallas_call(
        functools.partial(table_kernel, height, width),
        out_shape=jax.ShapeDtypeStruct((total, own.shape[1]), F32),
        in_specs=[smem(), vmem(), vmem()],
        out_specs=vmem(),
        compiler_params=limits(),
        name="build_table",
    )(place, own, other)


def box_parameters(boxes, levels, height, width):
    shapes, strides, bases, total = level_plan(height, width)
    rows = boxes.shape[0]

    def choose(values, kind):
        out = jnp.full((rows,), values[3], kind)
        for depth in range(3):
            out = jnp.where(levels == depth, jnp.asarray(values[depth], kind), out)
        return out

    reach_y = choose([h - 1 for h, w in shapes], F32)
    reach_x = choose([w - 1 for h, w in shapes], F32)
    stride = choose(strides, jnp.int32)
    base = choose(bases, jnp.int32)
    fraction = (
        (
            jnp.arange(BINS, dtype=F32)[:, None]
            + (jnp.arange(2, dtype=F32)[None, :] + 0.5) * 0.5
        )
        / 7.0
    ).reshape(2 * BINS, 1)
    top = (boxes[:, 0] - 0.25 * boxes[:, 2]) * reach_y
    length_y = 0.5 * boxes[:, 2] * reach_y
    left = (boxes[:, 1] - 0.25 * boxes[:, 3]) * reach_x
    length_x = 0.5 * boxes[:, 3] * reach_x
    first = jnp.clip(jnp.floor(top + length_y * fraction[0, 0]), 0.0, reach_y - 1.0)
    points = left[None] + length_x[None] * fraction
    lower = jnp.clip(jnp.floor(points), 0.0, (reach_x - 1.0)[None])
    upper_weight = points - lower
    address = (base + first.astype(jnp.int32))[None] + lower.astype(jnp.int32) * stride[None]
    row_values = jnp.stack([top, length_y, first, reach_y - 1.0])
    return address.reshape(-1), upper_weight.reshape(-1), row_values.reshape(-1), stride


def row_weights(top, length, first, last, index, offset):
    total = None
    for place in (0.25, 0.75):
        points = top + length * ((index + place) / 7.0)
        lower = jnp.minimum(jnp.maximum(jnp.floor(points), 0.0), last)
        upper_weight = points - lower
        distance = offset - (lower - first)
        part = jnp.where(
            distance == 0.0, 1.0 - upper_weight, jnp.where(distance == 1.0, upper_weight, 0.0)
        )
        total = part if total is None else total + part
    return total * 0.25


def crop_kernel(rows, address, weight, row_values, stride, table, out, turned):
    depth = 256
    lane = lax.broadcasted_iota(jnp.int32, (8, depth), 1)
    offset = (lane % WINDOW).astype(F32)
    index = lax.broadcasted_iota(jnp.int32, (8, depth), 0).astype(F32)
    inside = (
        lax.broadcasted_iota(jnp.int32, (8 * BINS, depth), 0) // 8
        == lax.broadcasted_iota(jnp.int32, (8 * BINS, depth), 1) // WINDOW
    )

    def group(step, carry):
        for part in range(GROUP):
            row = step * GROUP + part
            weights = row_weights(
                row_values[row],
                row_values[rows + row],
                row_values[2 * rows + row],
                row_values[3 * rows + row],
                index,
                offset,
            )
            left = jnp.where(inside, jnp.concatenate([weights] * BINS, axis=0), 0.0).astype(BF16)
            step_x = stride[row]
            columns = []
            for k in range(BINS):
                total = None
                for m in range(2):
                    place = address[(2 * k + m) * rows + row]
                    upper = weight[(2 * k + m) * rows + row]
                    first = table[pl.ds(place, WINDOW), :]
                    second = table[pl.ds(place + step_x, WINDOW), :]
                    value = first + upper * (second - first)
                    total = value if total is None else total + value
                columns.append(total)
            columns.append(jnp.zeros((depth - BINS * WINDOW, 128), F32))
            right = jnp.concatenate(columns, axis=0).astype(BF16)
            crop = jnp.dot(left, right, preferred_element_type=F32)
            for k in range(BINS):
                turned[pl.ds(part + k * BINS * GROUP, BINS, stride=GROUP), :] = crop[
                    8 * k : 8 * k + BINS
                ]
        start = pl.multiple_of(step * GROUP, GROUP)
        for cell in range(CELLS):
            out[pl.ds(start, GROUP), cell * 128 : (cell + 1) * 128] = turned[
                cell * GROUP : (cell + 1) * GROUP, :
            ].astype(BF16)
        return carry

    lax.fori_loop(0, rows // GROUP, group, 0)


def crop_forward(parameters, table):
    rows = parameters[3].shape[0]
    return pl.pallas_call(
        functools.partial(crop_kernel, rows),
        out_shape=jax.ShapeDtypeStruct((rows, CELLS * 128), BF16),
        in_specs=[smem()] * 4 + [vmem()],
        out_specs=vmem(),
        scratch_shapes=[pltpu.VMEM((CELLS * GROUP, 128), F32)],
        compiler_params=limits(),
        name="crop_forward",
    )(*parameters, table)


def spread_kernel(
    rows, height, width, place, address, weight, row_values, stride, grad, own, other, turned, half, *tables
):
    shapes, strides, bases, total = level_plan(height, width)
    starts = half_starts(shapes)
    lane = lax.broadcasted_iota(jnp.int32, (WINDOW, 128), 1)
    index = (lane % 8).astype(F32)
    offset = lax.broadcasted_iota(jnp.int32, (WINDOW, 128), 0).astype(F32)
    long_row = lax.broadcasted_iota(jnp.int32, (BINS * WINDOW, 128), 0)
    long_lane = lax.broadcasted_iota(jnp.int32, (BINS * WINDOW, 128), 1)
    inside = (long_row // WINDOW == long_lane // 8) & (long_lane % 8 < BINS)
    for table in tables:
        table[...] = jnp.zeros_like(table)
    turned[pl.ds(CELLS * GROUP, GROUP), :] = jnp.zeros((GROUP, 128), F32)

    def group(step, carry):
        start = pl.multiple_of(step * GROUP, GROUP)
        for cell in range(CELLS):
            turned[cell * GROUP : (cell + 1) * GROUP, :] = grad[
                pl.ds(start, GROUP), cell * 128 : (cell + 1) * 128
            ].astype(F32)
        for head in range(0, GROUP, CHAINS):
            results = []
            for part in range(head, head + CHAINS):
                row = step * GROUP + part
                weights = row_weights(
                    row_values[row],
                    row_values[rows + row],
                    row_values[2 * rows + row],
                    row_values[3 * rows + row],
                    index,
                    offset,
                )
                left = jnp.where(inside, jnp.concatenate([weights] * BINS, axis=0), 0.0).astype(
                    BF16
                )
                pieces = [
                    turned[pl.ds(part + k * BINS * GROUP, 8, stride=GROUP), :] for k in range(BINS)
                ]
                pieces.append(jnp.zeros((128 - 8 * BINS, 128), F32))
                right = jnp.concatenate(pieces, axis=0).astype(BF16)
                results.append(jnp.dot(left, right, preferred_element_type=F32))
            for k in range(BINS):
                for m in range(2):
                    for chain in range(CHAINS):
                        row = step * GROUP + head + chain
                        table = tables[chain]
                        at = address[(2 * k + m) * rows + row]
                        next_at = at + stride[row]
                        value = results[chain][k * WINDOW : (k + 1) * WINDOW]
                        upper = value * weight[(2 * k + m) * rows + row]
                        first = table[pl.ds(at, WINDOW), :] + (value - upper)
                        second = table[pl.ds(next_at, WINDOW), :] + upper
                        table[pl.ds(at, WINDOW), :] = first
                        table[pl.ds(next_at, WINDOW), :] = second
        return carry

    lax.fori_loop(0, rows // GROUP, group, 0)

    def summed(step, carry):
        span = pl.ds(pl.multiple_of(step * GROUP, GROUP), GROUP)
        value = tables[0][span, :]
        for table in tables[1:]:
            value = value + table[span, :]
        tables[0][span, :] = value
        return carry

    lax.fori_loop(0, total // GROUP, summed, 0)

    def collect(target, bottom):
        for depth, (level_rows, cols) in enumerate(shapes):
            count = level_rows // 2

            def column(x, carry, depth=depth, count=count, cols=cols):
                cells = tables[0][pl.ds(bases[depth] + x * strides[depth] + bottom * count, count), :]
                target[pl.ds(starts[depth] + x, count, stride=cols), :] = cells
                return carry

            lax.fori_loop(0, cols, column, 0, unroll=4)

    bottom = place[0]
    collect(own, bottom)
    collect(half, 1 - bottom)
    other[...] = half[...].astype(BF16)


def crop_backward(place, parameters, grad, height, width):
    rows = parameters[3].shape[0]
    shapes, strides, bases, total = level_plan(height, width)
    cells = half_starts(shapes)[-1]
    return pl.pallas_call(
        functools.partial(spread_kernel, rows, height, width),
        out_shape=(
            jax.ShapeDtypeStruct((cells, 128), F32),
            jax.ShapeDtypeStruct((cells, 128), BF16),
        ),
        in_specs=[smem()] * 5 + [vmem()],
        out_specs=(vmem(), vmem()),
        scratch_shapes=[
            pltpu.VMEM(((CELLS + 1) * GROUP, 128), F32),
            pltpu.VMEM((cells, 128), F32),
        ]
        + [pltpu.VMEM((total, 128), F32)] * CHAINS,
        compiler_params=limits(),
        name="crop_backward",
    )(place, *parameters, grad)


def natural_row(cell):
    k, i = divmod(cell, BINS)
    return i * BINS + k


def turn_kernel(weight, out, turned):
    held = weight.shape[0]
    for tile in range(CELLS):
        turned[tile * 128 : (tile + 1) * 128, 0:held] = jnp.transpose(
            weight[:, tile * 128 : (tile + 1) * 128]
        )
    for cell in range(CELLS):
        block = turned[pl.ds(natural_row(cell), 128, stride=CELLS), :]
        out[:, cell * 128 : (cell + 1) * 128] = jnp.transpose(block)[0:held].astype(BF16)


def turn_weight(weight):
    return pl.pallas_call(
        turn_kernel,
        out_shape=jax.ShapeDtypeStruct(weight.shape, BF16),
        in_specs=[vmem()],
        out_specs=vmem(),
        scratch_shapes=[pltpu.VMEM((weight.shape[1], 128), F32)],
        compiler_params=limits(),
        name="turn_weight",
    )(weight)


def renew(weight, moment, average, grad, rate):
    step_value = grad + DECAY * weight
    moment_new = MOMENTUM * moment + step_value
    weight_new = weight - rate * (step_value + MOMENTUM * moment_new)
    average_new = AVERAGE * average + (1.0 - AVERAGE) * weight_new
    return (weight_new, moment_new, average_new)


def renew_kernel(rate, count, *refs):
    terms = refs[:count]
    weight, moment, average, weight_new, moment_new, average_new, turned = refs[count:]
    held = weight.shape[0]
    for cell in range(CELLS):
        span = slice(cell * 128, (cell + 1) * 128)
        grad = terms[0][:, span].astype(F32)
        for term in terms[1:]:
            grad = grad + term[:, span].astype(F32)
        turned[pl.ds(natural_row(cell), 128, stride=CELLS), 0:held] = jnp.transpose(grad)
    for tile in range(CELLS):
        span = slice(tile * 128, (tile + 1) * 128)
        grad = jnp.transpose(turned[span, :])[0:held]
        new = renew(weight[:, span], moment[:, span], average[:, span], grad, rate)
        weight_new[:, span], moment_new[:, span], average_new[:, span] = new


def renew_first(terms, weight, moment, average, rate):
    return pl.pallas_call(
        functools.partial(renew_kernel, rate, len(terms)),
        out_shape=(jax.ShapeDtypeStruct(weight.shape, F32),) * 3,
        in_specs=[vmem()] * (len(terms) + 3),
        out_specs=(vmem(),) * 3,
        scratch_shapes=[pltpu.VMEM((weight.shape[1], 128), F32)],
        compiler_params=limits(),
        name="renew_first",
    )(*terms, weight, moment, average)


def gelu_parts(value):
    root = math.sqrt(2.0 / math.pi)
    square = value * value
    bend = jnp.tanh(root * (value + 0.044715 * square * value))
    half = 0.5 * (1.0 + bend)
    slope = half + 0.5 * value * (1.0 - bend * bend) * (
        root * (1.0 + 3.0 * 0.044715 * square)
    )
    return value * half, slope


def dot(left, right):
    return jnp.dot(left, right, preferred_element_type=F32)


def dot_last(left, right):
    return lax.dot_general(left, right, (((1,), (1,)), ((), ())), preferred_element_type=F32)


def middle_kernel(
    blocks,
    order,
    pre_own,
    pre_other,
    biases,
    second_turned,
    second,
    out_turned,
    out_weight,
    out_bias,
    slots,
    grad_own,
    grad_other,
    act_first,
    act_second,
    grad_second,
    grad_logits,
    losses,
    pre_first,
    slope_first,
    slope_second,
    grad_first,
):
    hidden, rows = pre_first.shape
    half = hidden // 2
    size = half // blocks
    own_start = order[blocks] * half
    other_start = (1 - order[blocks]) * half
    for block in range(blocks):
        span = slice(block * size, (block + 1) * size)
        at = pl.multiple_of(own_start + order[block] * size, size)
        pre_first[pl.ds(at, size), :] = pre_own[span, :]
        at = pl.multiple_of(other_start + order[block] * size, size)
        pre_first[pl.ds(at, size), :] = pre_other[span, :]
    act, slope = gelu_parts(pre_first[...] + biases[:, 0:1])
    slope_first[...] = slope
    act_first[...] = act.astype(BF16)
    pre_second = dot(second_turned[...], act_first[...]) + biases[:, 1:2]
    act, slope = gelu_parts(pre_second)
    slope_second[...] = slope
    act_second[...] = act.astype(BF16)
    logits = dot(out_turned[...], act_second[...]) + out_bias[...]

    row = lax.broadcasted_iota(jnp.int32, logits.shape, 0)
    live = slots[0:1, :]
    scale = slots[1:2, :]
    chosen = slots[2:3, :].astype(jnp.int32)
    foreground = jnp.where(chosen > 0, 1.0, 0.0)
    is_score = row < CLASSES
    top = jnp.max(jnp.where(is_score, logits, -jnp.inf), axis=0, keepdims=True)
    power = jnp.where(is_score, jnp.exp(logits - top), 0.0)
    total = jnp.sum(power, axis=0, keepdims=True)
    matches = row == chosen
    picked = jnp.sum(jnp.where(matches, logits, 0.0), axis=0, keepdims=True)
    value = jnp.log(total) + top - picked
    grad = power / total - jnp.where(matches, 1.0, 0.0)
    delta_row = CLASSES + 4 * (chosen - 1)
    smooth_total = jnp.zeros_like(live)
    for part in range(4):
        mine = (row == delta_row + part) & (chosen > 0)
        offset = jnp.sum(jnp.where(mine, logits, 0.0), axis=0, keepdims=True) - slots[
            3 + part : 4 + part, :
        ]
        size_of = jnp.abs(offset)
        near = size_of < SMOOTH
        smooth_total = smooth_total + jnp.where(
            near, 0.5 * offset * offset / SMOOTH, size_of - 0.5 * SMOOTH
        )
        slope = jnp.where(near, offset / SMOOTH, jnp.where(offset > 0.0, 1.0, -1.0))
        grad = jnp.where(mine, slope, grad)
    losses[...] = live * (value + foreground * smooth_total)
    grad_logits[...] = (grad * (live * scale)).astype(BF16)
    grad_second[...] = (dot(out_weight[...], grad_logits[...]) * slope_second[...]).astype(BF16)
    grad_first[...] = dot(second[...], grad_second[...]) * slope_first[...]
    for block in range(blocks):
        span = slice(block * size, (block + 1) * size)
        at = pl.multiple_of(own_start + order[block] * size, size)
        grad_own[span, :] = grad_first[pl.ds(at, size), :].astype(BF16)
        at = pl.multiple_of(other_start + order[block] * size, size)
        grad_other[span, :] = grad_first[pl.ds(at, size), :].astype(BF16)


def middle(blocks, order, pre_own, pre_other, biases, second_turned, second, out_turned, out_weight, out_bias, slots):
    half, rows = pre_own.shape
    hidden = 2 * half
    low = lambda *shape: jax.ShapeDtypeStruct(shape, BF16)
    return pl.pallas_call(
        functools.partial(middle_kernel, blocks),
        out_shape=(
            low(half, rows),
            low(half, rows),
            low(hidden, rows),
            low(hidden, rows),
            low(hidden, rows),
            low(PADDED, rows),
            jax.ShapeDtypeStruct((1, rows), F32),
        ),
        in_specs=[smem()] + [vmem()] * 9,
        out_specs=(vmem(),) * 7,
        scratch_shapes=[pltpu.VMEM((hidden, rows), F32)] * 4,
        compiler_params=limits(),
        name="middle",
    )(order, pre_own, pre_other, biases, second_turned, second, out_turned, out_weight, out_bias, slots)


def small_grads_kernel(
    parts, held, act_first, act_second, grad_second, grad_first, grad_logits, second_out, out_out, bias_out
):
    rows = act_first.shape[1]
    depth = act_first.shape[0] // parts
    for part in range(parts):
        value = dot_last(grad_second[...], act_first[part * depth : (part + 1) * depth, :]).astype(BF16)
        for block in range(value.shape[0] // held):
            start = (block * parts + part) * held
            second_out[start : start + held, :] = value[block * held : (block + 1) * held]
    column = lax.broadcasted_iota(jnp.int32, (rows, PADDED), 1)
    width = 5 * CLASSES - 4
    value = dot_last(act_second[...], grad_logits[...])
    value = value + dot(grad_first[...], jnp.where(column == width, 1.0, 0.0).astype(BF16))
    value = value + dot(grad_second[...], jnp.where(column == width + 1, 1.0, 0.0).astype(BF16))
    out_out[...] = value
    bias_out[...] = jnp.sum(grad_logits[...].astype(F32), axis=1, keepdims=True)


def small_grads(parts, held, act_first, act_second, grad_second, grad_first, grad_logits):
    hidden = act_first.shape[0]
    return pl.pallas_call(
        functools.partial(small_grads_kernel, parts, held),
        out_shape=(
            jax.ShapeDtypeStruct((hidden * parts, hidden // parts), BF16),
            jax.ShapeDtypeStruct((hidden, PADDED), F32),
            jax.ShapeDtypeStruct((PADDED, 1), F32),
        ),
        in_specs=[vmem()] * 5,
        out_specs=(vmem(),) * 3,
        compiler_params=limits(),
        name="small_grads",
    )(act_first, act_second, grad_second, grad_first, grad_logits)


def pair_swap(value, count):
    return lax.ppermute(value, "wide", [(at, at ^ 1) for at in range(count)])


def line_step(value, count):
    return lax.ppermute(value, "wide", [(at, (at + 2) % count) for at in range(count)])


def swap(value, axis):
    return lax.ppermute(value, axis, [(0, 1), (1, 0)])


def gather_ring(shard, count):
    line = count // 2
    pieces = []
    moving = shard
    for step in range(line):
        later = line_step(moving, count) if step < line - 1 else None
        pieces.append(moving)
        pieces.append(pair_swap(moving, count))
        moving = later
    return pieces


def scatter_ring(blocks, count):
    line = count // 2
    moving = None
    for step in list(range(1, line)) + [0]:
        crossed = pair_swap(blocks[2 * step + 1], count)
        terms = [blocks[2 * step], crossed]
        if moving is not None:
            terms.append(moving)
        if step == 0:
            return terms
        total = terms[0].astype(F32)
        for term in terms[1:]:
            total = total + term.astype(F32)
        moving = line_step(total.astype(BF16), count)


def body(
    map_p2,
    map_p3,
    map_p4,
    map_p5,
    boxes,
    levels,
    classes,
    sampled,
    counts,
    targets,
    first_weight,
    second_weight,
    out_weight,
    hidden_bias,
    out_bias,
    first_moment,
    second_moment,
    out_moment,
    hidden_moment,
    bias_moment,
    first_average,
    second_average,
    out_average,
    hidden_average,
    bias_average,
):
    n_section = lax.axis_size("section")
    n_fc = lax.axis_size("fc")
    n_wide = lax.axis_size("wide")
    section = lax.axis_index("section")
    fc = lax.axis_index("fc")
    wide = lax.axis_index("wide")
    everywhere = ("section", "wide", "fc")
    maps = [map_p2, map_p3, map_p4, map_p5]
    channels = map_p2.shape[3]
    height = map_p2.shape[1] * n_section
    width = map_p2.shape[2]
    rows_dev = boxes.shape[0]
    rows_own = rows_dev // (n_section * n_fc)
    held = first_weight.shape[1]
    classes_out = out_weight.shape[1]
    place = section.astype(jnp.int32).reshape(1)

    turned = turn_weight(first_weight.T)
    ring = n_wide <= 16
    if ring:
        pieces = gather_ring(turned, n_wide)
        blocks = n_wide
        line, pair = (wide // 2, wide % 2)
        order = jnp.stack(
            [
                ((line - step) % (n_wide // 2)) * 2 + (pair ^ side)
                for step in range(n_wide // 2)
                for side in range(2)
            ]
            + [section]
        ).astype(jnp.int32)
    else:
        pieces = [lax.all_gather(turned, "wide", axis=0, tiled=True)]
        blocks = 1
        order = jnp.stack([jnp.zeros_like(section), section]).astype(jnp.int32)

    live = ((jnp.arange(rows_dev, dtype=jnp.int32) < counts[0]) & (sampled > 0)).astype(F32)
    live_count = jnp.sum(live)
    high = jnp.floor(live_count / 32.0)
    count_columns = jnp.broadcast_to(
        jnp.stack([high, live_count - 32.0 * high])[None], (out_weight.shape[0], 2)
    )
    small = lax.all_gather(
        jnp.concatenate([out_weight, hidden_bias, count_columns], axis=1).astype(BF16),
        everywhere,
        axis=0,
        tiled=True,
    )
    counted = jnp.sum(small[:, classes_out + 2 : classes_out + 4].astype(F32), axis=0)
    total = (32.0 * counted[0] + counted[1]) / (out_weight.shape[0] * n_section * n_fc)
    w_out = jnp.pad(small[:, :classes_out], ((0, 0), (0, PADDED - classes_out)))
    biases = small[:, classes_out : classes_out + 2].astype(F32)
    w_second = lax.all_gather(
        second_weight.T.astype(BF16), everywhere, axis=0, tiled=True
    ).reshape(-1, n_fc, held, second_weight.shape[0])
    w_second_turned = jnp.transpose(w_second, (0, 2, 1, 3)).reshape(
        -1, n_fc * second_weight.shape[0]
    )
    hidden = w_second_turned.shape[0]
    slot_values = jnp.concatenate(
        [
            live[None],
            classes.astype(F32)[None],
            targets.T,
        ],
        axis=0,
    )

    def own_slots(values, axis):
        start = section * (n_fc * rows_own)
        mine = lax.dynamic_slice_in_dim(values, start + fc * rows_own, rows_own, axis)
        theirs = lax.dynamic_slice_in_dim(values, start + (1 - fc) * rows_own, rows_own, axis)
        return mine, theirs

    boxes_mine, boxes_theirs = own_slots(boxes, 0)
    levels_mine, levels_theirs = own_slots(levels, 0)
    slots_mine = own_slots(slot_values, 1)[0]
    slots_mine = jnp.concatenate(
        [slots_mine[0:1], jnp.full((1, rows_own), 1.0, F32) / total, slots_mine[1:]], axis=0
    )
    slots_mine = jnp.pad(slots_mine, ((0, 1), (0, 0)))

    half_own = jnp.concatenate([level_map.reshape(-1, channels) for level_map in maps], axis=0)
    table = build_table(place, half_own, swap(half_own, "section"), height, width)
    crops_mine = crop_forward(box_parameters(boxes_mine, levels_mine, height, width), table)
    passed_mine = swap(crops_mine, "section")
    crops_theirs = crop_forward(box_parameters(boxes_theirs, levels_theirs, height, width), table)
    passed_theirs = swap(crops_theirs, "section")
    inputs = jnp.concatenate([crops_mine, passed_mine, crops_theirs, passed_theirs], axis=0)
    rows_fc = n_section * rows_own

    sums = []
    for piece in pieces:
        term = dot_last(piece, inputs)
        sums.append(term[:, :rows_fc] + swap(term[:, rows_fc:], "fc"))
    pre = jnp.concatenate(sums, axis=0)
    pre_own = pre[:, :rows_own]
    pre_other = swap(pre[:, rows_own:], "section")

    grad_own, grad_other, act_first, act_second, grad_second, grad_logits, losses = middle(
        blocks,
        order,
        pre_own,
        pre_other,
        biases,
        w_second_turned,
        w_second_turned.T,
        w_out.T,
        w_out,
        jnp.pad(out_bias, (0, PADDED - classes_out))[:, None],
        slots_mine,
    )
    grad_mine = jnp.concatenate([grad_own, swap(grad_other, "section")], axis=1)
    grad_all = jnp.concatenate([grad_mine, swap(grad_mine, "fc")], axis=1)

    first_terms = dot(grad_all, inputs).astype(BF16)
    rate = 0.15 * math.sqrt(rows_dev * n_wide)
    if ring:
        first_sums = scatter_ring(
            [first_terms[at * held : (at + 1) * held] for at in range(n_wide)], n_wide
        )
    else:
        first_sums = [lax.psum_scatter(first_terms, "wide", scatter_dimension=0, tiled=True)]

    w_first = jnp.concatenate(pieces, axis=0)
    grad_inputs = lax.dot_general(
        grad_all, w_first, (((0,), (0,)), ((), ())), preferred_element_type=F32
    )
    to_keep = jnp.concatenate(
        [grad_inputs[:rows_own], grad_inputs[rows_fc : rows_fc + rows_own]], axis=0
    )
    to_send = jnp.concatenate(
        [grad_inputs[rows_own:rows_fc], grad_inputs[rows_fc + rows_own :]], axis=0
    ).astype(BF16)
    grad_crops = (to_keep + swap(to_send, "section").astype(F32)).astype(BF16)
    map_own, map_other = crop_backward(
        place,
        box_parameters(
            jnp.concatenate([boxes_mine, boxes_theirs], axis=0),
            jnp.concatenate([levels_mine, levels_theirs], axis=0),
            height,
            width,
        ),
        grad_crops,
        height,
        width,
    )
    own_grad = map_own + swap(map_other, "section").astype(F32)
    map_grads = []
    start_cell = 0
    for level_map in maps:
        cell_count = level_map.shape[1] * level_map.shape[2]
        map_grads.append(own_grad[start_cell : start_cell + cell_count].reshape(level_map.shape))
        start_cell = start_cell + cell_count

    half = hidden // n_section
    first_bias_rows = jnp.concatenate([grad_own, grad_other], axis=0)
    size = half // blocks
    unordered = jnp.zeros_like(first_bias_rows)
    for block in range(blocks):
        for side, where in ((0, section), (1, 1 - section)):
            unordered = lax.dynamic_update_slice_in_dim(
                unordered,
                first_bias_rows[side * half + block * size : side * half + (block + 1) * size],
                where * half + order[block] * size,
                0,
            )
    second_terms, out_terms, bias_terms = small_grads(
        n_fc, held, act_first, act_second, grad_second, unordered, grad_logits
    )
    second_sum = lax.psum_scatter(second_terms, everywhere, scatter_dimension=0, tiled=True)
    out_sum = lax.psum_scatter(out_terms, everywhere, scatter_dimension=0, tiled=True)
    vector = jnp.concatenate([bias_terms[:classes_out, 0], jnp.sum(losses).reshape(1)])
    vector = lax.psum(vector, everywhere)

    first_out = renew_first(first_sums, first_weight.T, first_moment.T, first_average.T, rate)
    second_out = renew(
        second_weight, second_moment, second_average, second_sum.astype(F32).T, rate
    )
    out_out = renew(out_weight, out_moment, out_average, out_sum[:, :classes_out], rate)
    hidden_out = renew(
        hidden_bias,
        hidden_moment,
        hidden_average,
        out_sum[:, classes_out : classes_out + 2],
        rate,
    )
    bias_out = renew(out_bias, bias_moment, bias_average, vector[:classes_out], 4.0)
    return (
        vector[classes_out],
        total,
        map_grads[0],
        map_grads[1],
        map_grads[2],
        map_grads[3],
        first_out[0].T,
        first_out[1].T,
        first_out[2].T,
        *second_out,
        *out_out,
        *hidden_out,
        *bias_out,
    )


def solution(mesh):
    maps = P("wide", "section", None, "fc")
    wide_weight = P("fc", ("section", "wide"))
    tall_weight = P(("section", "wide", "fc"), None)
    in_specs = (
        (maps,) * 4
        + (P("wide", None), P("wide"), P("wide"), P("wide"), P("wide"), P("wide", None))
        + (wide_weight, wide_weight, tall_weight, tall_weight, P()) * 3
    )
    out_specs = (
        (P(), P())
        + (maps,) * 4
        + (wide_weight,) * 6
        + (tall_weight,) * 6
        + (P(),) * 3
    )
    return jax.shard_map(body, mesh=mesh, in_specs=in_specs, out_specs=out_specs, check_vma=False)
```

```python
import functools
import math

import jax
import jax.numpy as jnp
from jax import lax
from jax.experimental import pallas as pl
from jax.experimental.pallas import tpu as pltpu
from jax.sharding import PartitionSpec as P

CLASSES = 81
BINS = 7
CELLS = BINS * BINS
WINDOW = 24
GROUP = 16
CHAINS = 4
PADDED = 512
MOMENTUM = 0.9
AVERAGE = 0.7
DECAY = 0.0001
SMOOTH = 0.5

F32 = jnp.float32
BF16 = jnp.bfloat16
VMEM_LIMIT = 52 * 2**20


def smem():
    return pl.BlockSpec(memory_space=pltpu.SMEM)


def vmem():
    return pl.BlockSpec(memory_space=pltpu.VMEM)


def lasting(microseconds):
    return pl.CostEstimate(
        flops=0, bytes_accessed=int(microseconds * 3.6e6), transcendentals=0
    )


def limits():
    return pltpu.CompilerParams(vmem_limit_bytes=VMEM_LIMIT)


def level_plan(height, width):
    shapes = [(height >> depth, width >> depth) for depth in range(4)]
    strides = [max(rows, WINDOW) for rows, cols in shapes]
    bases = [0]
    for depth in range(4):
        bases.append(bases[-1] + strides[depth] * shapes[depth][1])
    total = -(-(bases[-1] + 2 * WINDOW) // GROUP) * GROUP
    return shapes, strides, bases[:4], total


def half_starts(shapes):
    starts = [0]
    for rows, cols in shapes:
        starts.append(starts[-1] + rows // 2 * cols)
    return starts


def table_kernel(height, width, place, own, other, table):
    shapes, strides, bases, total = level_plan(height, width)
    starts = half_starts(shapes)
    table[...] = jnp.zeros_like(table)

    def fill(source, bottom):
        for depth, (rows, cols) in enumerate(shapes):
            half = rows // 2

            def column(x, carry, depth=depth, half=half, cols=cols):
                cells = source[pl.ds(starts[depth] + x, half, stride=cols), :]
                table[pl.ds(bases[depth] + x * strides[depth] + bottom * half, half), :] = cells
                return carry

            lax.fori_loop(0, cols, column, 0, unroll=4)

    bottom = place[0]
    fill(own, bottom)
    fill(other, 1 - bottom)


def build_table(place, own, other, height, width):
    total = level_plan(height, width)[3]
    return pl.pallas_call(
        functools.partial(table_kernel, height, width),
        out_shape=jax.ShapeDtypeStruct((total, own.shape[1]), F32),
        in_specs=[smem(), vmem(), vmem()],
        out_specs=vmem(),
        compiler_params=limits(),
        cost_estimate=lasting(5.0),
        name="build_table",
    )(place, own, other)


def box_parameters(boxes, levels, height, width):
    shapes, strides, bases, total = level_plan(height, width)
    rows = boxes.shape[0]

    def choose(values, kind):
        out = jnp.full((rows,), values[3], kind)
        for depth in range(3):
            out = jnp.where(levels == depth, jnp.asarray(values[depth], kind), out)
        return out

    reach_y = choose([h - 1 for h, w in shapes], F32)
    reach_x = choose([w - 1 for h, w in shapes], F32)
    stride = choose(strides, jnp.int32)
    base = choose(bases, jnp.int32)
    fraction = (
        (
            jnp.arange(BINS, dtype=F32)[:, None]
            + (jnp.arange(2, dtype=F32)[None, :] + 0.5) * 0.5
        )
        / 7.0
    ).reshape(2 * BINS, 1)
    top = (boxes[:, 0] - 0.25 * boxes[:, 2]) * reach_y
    length_y = 0.5 * boxes[:, 2] * reach_y
    left = (boxes[:, 1] - 0.25 * boxes[:, 3]) * reach_x
    length_x = 0.5 * boxes[:, 3] * reach_x
    first = jnp.clip(jnp.floor(top + length_y * fraction[0, 0]), 0.0, reach_y - 1.0)
    points = left[None] + length_x[None] * fraction
    lower = jnp.clip(jnp.floor(points), 0.0, (reach_x - 1.0)[None])
    upper_weight = points - lower
    address = (base + first.astype(jnp.int32))[None] + lower.astype(jnp.int32) * stride[None]
    row_values = jnp.stack([top, length_y, first, reach_y - 1.0])
    return address.reshape(-1), upper_weight.reshape(-1), row_values.reshape(-1), stride


def row_weights(top, length, first, last, index, offset):
    total = None
    for place in (0.25, 0.75):
        points = top + length * ((index + place) / 7.0)
        lower = jnp.minimum(jnp.maximum(jnp.floor(points), 0.0), last)
        upper_weight = points - lower
        distance = offset - (lower - first)
        part = jnp.where(
            distance == 0.0, 1.0 - upper_weight, jnp.where(distance == 1.0, upper_weight, 0.0)
        )
        total = part if total is None else total + part
    return total * 0.25


def box_rows(row_values, row, all_rows):
    return [row_values[part * all_rows + row] for part in range(4)]


def crop_kernel(rows, first, address, weight, row_values, stride, table, out, turned):
    depth = 256
    all_rows = stride.shape[0]
    lane = lax.broadcasted_iota(jnp.int32, (8, depth), 1)
    offset = (lane % WINDOW).astype(F32)
    index = lax.broadcasted_iota(jnp.int32, (8, depth), 0).astype(F32)
    inside = (
        lax.broadcasted_iota(jnp.int32, (8 * BINS, depth), 0) // 8
        == lax.broadcasted_iota(jnp.int32, (8 * BINS, depth), 1) // WINDOW
    )

    def group(step, carry):
        for part in range(GROUP):
            row = first + step * GROUP + part
            weights = row_weights(*box_rows(row_values, row, all_rows), index, offset)
            left = jnp.where(inside, jnp.concatenate([weights] * BINS, axis=0), 0.0).astype(BF16)
            step_x = stride[row]
            columns = []
            for k in range(BINS):
                total = None
                for m in range(2):
                    place = address[(2 * k + m) * all_rows + row]
                    upper = weight[(2 * k + m) * all_rows + row]
                    near = table[pl.ds(place, WINDOW), :]
                    far = table[pl.ds(place + step_x, WINDOW), :]
                    value = near + upper * (far - near)
                    total = value if total is None else total + value
                columns.append(total)
            columns.append(jnp.zeros((depth - BINS * WINDOW, 128), F32))
            right = jnp.concatenate(columns, axis=0).astype(BF16)
            crop = jnp.dot(left, right, preferred_element_type=F32)
            for k in range(BINS):
                turned[pl.ds(part + k * BINS * GROUP, BINS, stride=GROUP), :] = crop[
                    8 * k : 8 * k + BINS
                ]
        start = pl.multiple_of(step * GROUP, GROUP)
        for cell in range(CELLS):
            out[pl.ds(start, GROUP), cell * 128 : (cell + 1) * 128] = turned[
                cell * GROUP : (cell + 1) * GROUP, :
            ].astype(BF16)
        return carry

    lax.fori_loop(0, rows // GROUP, group, 0)


def crop_forward(parameters, table, first, rows):
    return pl.pallas_call(
        functools.partial(crop_kernel, rows, first),
        out_shape=jax.ShapeDtypeStruct((rows, CELLS * 128), BF16),
        in_specs=[smem()] * 4 + [vmem()],
        out_specs=vmem(),
        scratch_shapes=[pltpu.VMEM((CELLS * GROUP, 128), F32)],
        compiler_params=limits(),
        cost_estimate=lasting(0.07 * rows),
        name="crop_forward",
    )(*parameters, table)


def spread_kernel(rows, first, height, width, last, place, address, weight, row_values, stride, keep, passed, *refs):
    shapes, strides, bases, total = level_plan(height, width)
    starts = half_starts(shapes)
    all_rows = stride.shape[0]
    if last:
        before, own, other, turned, half, *tables = refs
    else:
        out, turned, *tables = refs
    lane = lax.broadcasted_iota(jnp.int32, (WINDOW, 128), 1)
    index = (lane % 8).astype(F32)
    offset = lax.broadcasted_iota(jnp.int32, (WINDOW, 128), 0).astype(F32)
    long_row = lax.broadcasted_iota(jnp.int32, (BINS * WINDOW, 128), 0)
    long_lane = lax.broadcasted_iota(jnp.int32, (BINS * WINDOW, 128), 1)
    inside = (long_row // WINDOW == long_lane // 8) & (long_lane % 8 < BINS)
    for table in tables:
        table[...] = jnp.zeros_like(table)
    turned[pl.ds(CELLS * GROUP, GROUP), :] = jnp.zeros((GROUP, 128), F32)

    def group(step, carry):
        start = pl.multiple_of(step * GROUP, GROUP)
        for cell in range(CELLS):
            span = slice(cell * 128, (cell + 1) * 128)
            turned[cell * GROUP : (cell + 1) * GROUP, :] = keep[pl.ds(start, GROUP), span].astype(
                F32
            ) + passed[pl.ds(start, GROUP), span].astype(F32)
        for head in range(0, GROUP, CHAINS):
            results = []
            for part in range(head, head + CHAINS):
                row = first + step * GROUP + part
                weights = row_weights(*box_rows(row_values, row, all_rows), index, offset)
                left = jnp.where(inside, jnp.concatenate([weights] * BINS, axis=0), 0.0).astype(
                    BF16
                )
                pieces = [
                    turned[pl.ds(part + k * BINS * GROUP, 8, stride=GROUP), :] for k in range(BINS)
                ]
                pieces.append(jnp.zeros((128 - 8 * BINS, 128), F32))
                right = jnp.concatenate(pieces, axis=0).astype(BF16)
                results.append(jnp.dot(left, right, preferred_element_type=F32))
            for k in range(BINS):
                for m in range(2):
                    for chain in range(CHAINS):
                        row = first + step * GROUP + head + chain
                        table = tables[chain]
                        at = address[(2 * k + m) * all_rows + row]
                        next_at = at + stride[row]
                        value = results[chain][k * WINDOW : (k + 1) * WINDOW]
                        upper = value * weight[(2 * k + m) * all_rows + row]
                        near = table[pl.ds(at, WINDOW), :] + (value - upper)
                        far = table[pl.ds(next_at, WINDOW), :] + upper
                        table[pl.ds(at, WINDOW), :] = near
                        table[pl.ds(next_at, WINDOW), :] = far
        return carry

    lax.fori_loop(0, rows // GROUP, group, 0)
    result = tables[0] if last else out

    def summed(step, carry):
        span = pl.ds(pl.multiple_of(step * GROUP, GROUP), GROUP)
        value = tables[0][span, :]
        for table in tables[1:]:
            value = value + table[span, :]
        if last:
            value = value + before[span, :]
        result[span, :] = value
        return carry

    lax.fori_loop(0, total // GROUP, summed, 0)
    if not last:
        return

    def collect(target, bottom):
        for depth, (level_rows, cols) in enumerate(shapes):
            count = level_rows // 2

            def column(x, carry, depth=depth, count=count, cols=cols):
                cells = result[pl.ds(bases[depth] + x * strides[depth] + bottom * count, count), :]
                target[pl.ds(starts[depth] + x, count, stride=cols), :] = cells
                return carry

            lax.fori_loop(0, cols, column, 0, unroll=4)

    bottom = place[0]
    collect(own, bottom)
    collect(half, 1 - bottom)
    other[...] = half[...].astype(BF16)


def crop_backward(place, parameters, keep, passed, first, height, width, before=None):
    rows = keep.shape[0]
    shapes, strides, bases, total = level_plan(height, width)
    cells = half_starts(shapes)[-1]
    last = before is not None
    turned = pltpu.VMEM(((CELLS + 1) * GROUP, 128), F32)
    tables = [pltpu.VMEM((total, 128), F32)] * CHAINS
    if last:
        out_shape = (
            jax.ShapeDtypeStruct((cells, 128), F32),
            jax.ShapeDtypeStruct((cells, 128), BF16),
        )
        scratch = [turned, pltpu.VMEM((cells, 128), F32)] + tables
    else:
        out_shape = jax.ShapeDtypeStruct((total, 128), F32)
        scratch = [turned] + tables
    return pl.pallas_call(
        functools.partial(spread_kernel, rows, first, height, width, last),
        out_shape=out_shape,
        in_specs=[smem()] * 5 + [vmem()] * (3 if last else 2),
        out_specs=(vmem(),) * 2 if last else vmem(),
        scratch_shapes=scratch,
        compiler_params=limits(),
        cost_estimate=lasting(0.12 * rows),
        name="crop_backward",
    )(place, *parameters, keep, passed, *([before] if last else []))


def natural_row(cell):
    k, i = divmod(cell, BINS)
    return i * BINS + k


def turn_kernel(weight, out, turned):
    held = weight.shape[0]
    for tile in range(CELLS):
        turned[tile * 128 : (tile + 1) * 128, 0:held] = jnp.transpose(
            weight[:, tile * 128 : (tile + 1) * 128]
        )
    for cell in range(CELLS):
        block = turned[pl.ds(natural_row(cell), 128, stride=CELLS), :]
        out[:, cell * 128 : (cell + 1) * 128] = jnp.transpose(block)[0:held].astype(BF16)


def turn_weight(weight):
    return pl.pallas_call(
        turn_kernel,
        out_shape=jax.ShapeDtypeStruct(weight.shape, BF16),
        in_specs=[vmem()],
        out_specs=vmem(),
        scratch_shapes=[pltpu.VMEM((weight.shape[1], 128), F32)],
        compiler_params=limits(),
        cost_estimate=lasting(2.7),
        name="turn_weight",
    )(weight)


def renew(weight, moment, average, grad, rate):
    step_value = grad + DECAY * weight
    moment_new = MOMENTUM * moment + step_value
    weight_new = weight - rate * (step_value + MOMENTUM * moment_new)
    average_new = AVERAGE * average + (1.0 - AVERAGE) * weight_new
    return (weight_new, moment_new, average_new)


def renew_kernel(rate, count, *refs):
    terms = refs[:count]
    weight, moment, average, weight_new, moment_new, average_new, turned = refs[count:]
    held = weight.shape[0]
    for cell in range(CELLS):
        span = slice(cell * 128, (cell + 1) * 128)
        grad = terms[0][:, span].astype(F32)
        for term in terms[1:]:
            grad = grad + term[:, span].astype(F32)
        turned[pl.ds(natural_row(cell), 128, stride=CELLS), 0:held] = jnp.transpose(grad)
    for tile in range(CELLS):
        span = slice(tile * 128, (tile + 1) * 128)
        grad = jnp.transpose(turned[span, :])[0:held]
        new = renew(weight[:, span], moment[:, span], average[:, span], grad, rate)
        weight_new[:, span], moment_new[:, span], average_new[:, span] = new


def renew_first(terms, weight, moment, average, rate):
    return pl.pallas_call(
        functools.partial(renew_kernel, rate, len(terms)),
        out_shape=(jax.ShapeDtypeStruct(weight.shape, F32),) * 3,
        in_specs=[vmem()] * (len(terms) + 3),
        out_specs=(vmem(),) * 3,
        scratch_shapes=[pltpu.VMEM((weight.shape[1], 128), F32)],
        compiler_params=limits(),
        cost_estimate=lasting(6.5),
        name="renew_first",
    )(*terms, weight, moment, average)


def gelu_parts(value):
    root = math.sqrt(2.0 / math.pi)
    square = value * value
    bend = jnp.tanh(root * (value + 0.044715 * square * value))
    half = 0.5 * (1.0 + bend)
    slope = half + 0.5 * value * (1.0 - bend * bend) * (
        root * (1.0 + 3.0 * 0.044715 * square)
    )
    return value * half, slope


def dot(left, right):
    return jnp.dot(left, right, preferred_element_type=F32)


def dot_last(left, right):
    return lax.dot_general(left, right, (((1,), (1,)), ((), ())), preferred_element_type=F32)


def middle_kernel(
    blocks,
    order,
    pre_own,
    pre_other,
    biases,
    second_turned,
    second,
    out_turned,
    out_weight,
    out_bias,
    slots,
    grad_own,
    grad_other,
    act_first,
    act_second,
    grad_second,
    grad_logits,
    losses,
    pre_first,
    slope_first,
    slope_second,
    grad_first,
):
    hidden, rows = pre_first.shape
    half = hidden // 2
    size = half // blocks
    own_start = order[blocks] * half
    other_start = (1 - order[blocks]) * half
    for block in range(blocks):
        span = slice(block * size, (block + 1) * size)
        at = pl.multiple_of(own_start + order[block] * size, size)
        pre_first[pl.ds(at, size), :] = pre_own[span, :]
        at = pl.multiple_of(other_start + order[block] * size, size)
        pre_first[pl.ds(at, size), :] = pre_other[span, :]
    act, slope = gelu_parts(pre_first[...] + biases[:, 0:1])
    slope_first[...] = slope
    act_first[...] = act.astype(BF16)
    pre_second = (
        dot(second_turned[0], act_first[0:half, :])
        + dot(second_turned[1], act_first[half:hidden, :])
        + biases[:, 1:2]
    )
    act, slope = gelu_parts(pre_second)
    slope_second[...] = slope
    act_second[...] = act.astype(BF16)
    logits = dot(out_turned[...], act_second[...]) + out_bias[...]

    row = lax.broadcasted_iota(jnp.int32, logits.shape, 0)
    live = slots[0:1, :]
    scale = slots[1:2, :]
    chosen = slots[2:3, :].astype(jnp.int32)
    foreground = jnp.where(chosen > 0, 1.0, 0.0)
    is_score = row < CLASSES
    top = jnp.max(jnp.where(is_score, logits, -jnp.inf), axis=0, keepdims=True)
    power = jnp.where(is_score, jnp.exp(logits - top), 0.0)
    total = jnp.sum(power, axis=0, keepdims=True)
    matches = row == chosen
    picked = jnp.sum(jnp.where(matches, logits, 0.0), axis=0, keepdims=True)
    value = jnp.log(total) + top - picked
    grad = power / total - jnp.where(matches, 1.0, 0.0)
    delta_row = CLASSES + 4 * (chosen - 1)
    smooth_total = jnp.zeros_like(live)
    for part in range(4):
        mine = (row == delta_row + part) & (chosen > 0)
        offset = jnp.sum(jnp.where(mine, logits, 0.0), axis=0, keepdims=True) - slots[
            3 + part : 4 + part, :
        ]
        size_of = jnp.abs(offset)
        near = size_of < SMOOTH
        smooth_total = smooth_total + jnp.where(
            near, 0.5 * offset * offset / SMOOTH, size_of - 0.5 * SMOOTH
        )
        slope = jnp.where(near, offset / SMOOTH, jnp.where(offset > 0.0, 1.0, -1.0))
        grad = jnp.where(mine, slope, grad)
    losses[...] = live * (value + foreground * smooth_total)
    grad_logits[...] = (grad * (live * scale)).astype(BF16)
    grad_second[...] = (dot(out_weight[...], grad_logits[...]) * slope_second[...]).astype(BF16)
    grad_first[...] = dot(second[...], grad_second[...]) * slope_first[...]
    for block in range(blocks):
        span = slice(block * size, (block + 1) * size)
        at = pl.multiple_of(own_start + order[block] * size, size)
        grad_own[span, :] = grad_first[pl.ds(at, size), :].astype(BF16)
        at = pl.multiple_of(other_start + order[block] * size, size)
        grad_other[span, :] = grad_first[pl.ds(at, size), :].astype(BF16)


def middle(blocks, order, pre_own, pre_other, biases, second_turned, second, out_turned, out_weight, out_bias, slots):
    half, rows = pre_own.shape
    hidden = 2 * half
    low = lambda *shape: jax.ShapeDtypeStruct(shape, BF16)
    return pl.pallas_call(
        functools.partial(middle_kernel, blocks),
        out_shape=(
            low(half, rows),
            low(half, rows),
            low(hidden, rows),
            low(hidden, rows),
            low(hidden, rows),
            low(PADDED, rows),
            jax.ShapeDtypeStruct((1, rows), F32),
        ),
        in_specs=[smem()] + [vmem()] * 9,
        out_specs=(vmem(),) * 7,
        scratch_shapes=[pltpu.VMEM((hidden, rows), F32)] * 4,
        compiler_params=limits(),
        cost_estimate=lasting(6.5),
        name="middle",
    )(order, pre_own, pre_other, biases, second_turned, second, out_turned, out_weight, out_bias, slots)


def small_grads_kernel(
    blocks,
    order,
    act_first,
    act_second,
    grad_second,
    grad_own,
    grad_other,
    grad_logits,
    own,
    other,
    bias_out,
    second_sum,
    out_sum,
):
    hidden, rows = act_first.shape
    half = hidden // 2
    size = half // blocks
    section, fc = order[blocks], order[blocks + 1]
    for side in range(2):
        second_sum[side] = dot_last(
            grad_second[...], act_first[side * half : (side + 1) * half, :]
        ).astype(BF16)
    width = 5 * CLASSES - 4
    column = lax.broadcasted_iota(jnp.int32, (rows, PADDED), 1)
    value = dot_last(act_second[...], grad_logits[...])
    value = value + dot(grad_second[...], jnp.where(column == width + 1, 1.0, 0.0).astype(BF16))
    out_sum[...] = value
    ones = jnp.where(column == width, 1.0, 0.0).astype(BF16)
    for block in range(blocks):
        span = slice(block * size, (block + 1) * size)
        for values, where in ((grad_own, section), (grad_other, 1 - section)):
            at = pl.ds(pl.multiple_of(where * half + order[block] * size, size), size)
            out_sum[at, :] = out_sum[at, :] + dot(values[span, :], ones)
    bias_out[...] = jnp.sum(grad_logits[...].astype(F32), axis=1, keepdims=True)
    part = size // 2
    for target, where in ((own, section), (other, 1 - section)):
        for near in range(2):
            lane = fc if near == 0 else 1 - fc
            for block in range(blocks):
                start = pl.multiple_of(where * half + order[block] * size, size)
                target[near, block * size : (block + 1) * size, 0:half] = second_sum[
                    lane, pl.ds(start, size), :
                ]
                at = pl.ds(pl.multiple_of(start + lane * part, part), part)
                for side in range(2):
                    target[
                        near,
                        block * size + side * part : block * size + (side + 1) * part,
                        half : half + PADDED // 2,
                    ] = out_sum[at, side * (PADDED // 2) : (side + 1) * (PADDED // 2)].astype(BF16)


def small_grads(blocks, order, act_first, act_second, grad_second, grad_own, grad_other, grad_logits):
    hidden = act_first.shape[0]
    half = hidden // 2
    low = jax.ShapeDtypeStruct((2, half, half + PADDED // 2), BF16)
    return pl.pallas_call(
        functools.partial(small_grads_kernel, blocks),
        out_shape=(low, low, jax.ShapeDtypeStruct((PADDED, 1), F32)),
        in_specs=[smem()] + [vmem()] * 6,
        out_specs=(vmem(),) * 3,
        scratch_shapes=[
            pltpu.VMEM((2, hidden, half), BF16),
            pltpu.VMEM((hidden, PADDED), F32),
        ],
        compiler_params=limits(),
        cost_estimate=lasting(4.0),
        name="small_grads",
    )(order, act_first, act_second, grad_second, grad_own, grad_other, grad_logits)


def assemble_kernel(blocks, order, own, other, second_turned, second, out_weight, out_turned):
    hidden = second.shape[0]
    half = hidden // 2
    size = half // blocks
    part = size // 2
    section, fc = order[blocks], order[blocks + 1]
    for source, where in ((own, section), (other, 1 - section)):
        for near in range(2):
            lane = fc if near == 0 else 1 - fc
            for block in range(blocks):
                start = pl.multiple_of(where * half + order[block] * size, size)
                second_turned[lane, pl.ds(start, size), :] = source[
                    near, block * size : (block + 1) * size, 0:half
                ]
                at = pl.ds(pl.multiple_of(start + lane * part, part), part)
                for side in range(2):
                    out_weight[at, side * (PADDED // 2) : (side + 1) * (PADDED // 2)] = source[
                        near,
                        block * size + side * part : block * size + (side + 1) * part,
                        half : half + PADDED // 2,
                    ]
    for side in range(2):
        second[side * half : (side + 1) * half, :] = jnp.transpose(second_turned[side])
    out_turned[...] = jnp.transpose(out_weight[...])


def assemble(blocks, order, own, other):
    half = own.shape[1]
    hidden = 2 * half
    low = lambda *shape: jax.ShapeDtypeStruct(shape, BF16)
    return pl.pallas_call(
        functools.partial(assemble_kernel, blocks),
        out_shape=(low(2, hidden, half), low(hidden, hidden), low(hidden, PADDED), low(PADDED, hidden)),
        in_specs=[smem()] + [vmem()] * 2,
        out_specs=(vmem(),) * 4,
        compiler_params=limits(),
        cost_estimate=lasting(5.0),
        name="assemble",
    )(order, own, other)


def lane_blocks(lanes):
    for parts in (7, 1):
        if lanes % (128 * parts) == 0:
            return parts, lanes // parts


def weight_grad_kernel(count, grad, first, second, third, fourth, *outs):
    inputs = jnp.concatenate([first[...], second[...], third[...], fourth[...]], axis=0)
    value = dot(grad[...], inputs).astype(BF16)
    size = value.shape[0] // count
    for at in range(count):
        outs[at][...] = value[at * size : (at + 1) * size]


def weight_grad(count, grad, inputs):
    rows, lanes = inputs[0].shape
    parts, size = lane_blocks(lanes)
    held = grad.shape[0] // count
    return pl.pallas_call(
        functools.partial(weight_grad_kernel, count),
        out_shape=(jax.ShapeDtypeStruct((held, lanes), BF16),) * count,
        grid=(parts,),
        in_specs=[pl.BlockSpec(grad.shape, lambda step: (0, 0))]
        + [pl.BlockSpec((rows, size), lambda step: (0, step))] * 4,
        out_specs=(pl.BlockSpec((held, size), lambda step: (0, step)),) * count,
        compiler_params=limits(),
        cost_estimate=lasting(2.0 + 0.4 * count),
        name="weight_grad",
    )(grad, *inputs)


def input_grad_kernel(count, grad, *refs):
    weight = jnp.concatenate([ref[...] for ref in refs[:count]], axis=0)
    value = dot(grad[...], weight).astype(BF16)
    rows = value.shape[0] // 4
    for at, out in enumerate(refs[count:]):
        out[...] = value[at * rows : (at + 1) * rows]


def input_grad(grad, pieces):
    lanes = pieces[0].shape[1]
    parts, size = lane_blocks(lanes)
    rows = grad.shape[0] // 4
    return pl.pallas_call(
        functools.partial(input_grad_kernel, len(pieces)),
        out_shape=(jax.ShapeDtypeStruct((rows, lanes), BF16),) * 4,
        grid=(parts,),
        in_specs=[pl.BlockSpec(grad.shape, lambda step: (0, 0))]
        + [pl.BlockSpec((piece.shape[0], size), lambda step: (0, step)) for piece in pieces],
        out_specs=(pl.BlockSpec((rows, size), lambda step: (0, step)),) * 4,
        compiler_params=limits(),
        cost_estimate=lasting(5.0),
        name="input_grad",
    )(grad, *pieces)


def pair_swap(value, count):
    return lax.ppermute(value, "wide", [(at, at ^ 1) for at in range(count)])


def line_step(value, count, steps=1):
    return lax.ppermute(value, "wide", [(at, (at + 2 * steps) % count) for at in range(count)])


def swap(value, axis):
    return lax.ppermute(value, axis, [(0, 1), (1, 0)])


def after(value, *others):
    return lax.optimization_barrier((value, *others))[0]


def add(*terms):
    total = terms[0].astype(F32)
    for term in terms[1:]:
        total = total + term.astype(F32)
    return total.astype(BF16)


def gather_small(piece, count):
    line = count // 2
    held = [piece] + [line_step(piece, count, steps) for steps in range(1, line)]
    held = jnp.concatenate(held, axis=0)
    plane = jnp.concatenate([held, pair_swap(held, count)], axis=0)
    own = jnp.stack([plane, swap(plane, "fc")])
    return own, swap(own, "section")


def scatter_small(own, other, count):
    line = count // 2
    both = add(own, swap(other, "section"))
    plane = add(both[0], swap(both[1], "fc"))
    half = plane.shape[0] // 2
    held = add(plane[:half], pair_swap(plane[half:], count))
    size = half // line
    terms = [held[:size].astype(F32)]
    for steps in range(1, line):
        part = held[steps * size : (steps + 1) * size]
        terms.append(line_step(part, count, -steps).astype(F32))
    return functools.reduce(jnp.add, terms)


def gather_ring(shard, count):
    line = count // 2
    half = shard.shape[0] // 2
    straight = [shard]
    crossed = []
    for step in range(line - 1):
        straight.append(line_step(straight[step], count))
        crossed.append(pair_swap(straight[step], count))
    tail = [
        pair_swap(straight[-1][:half], count),
        line_step(crossed[-1][half:], count),
    ]
    return straight, crossed, tail


def scatter_ring(straight, crossed, count):
    line = count // 2
    half = straight[0].shape[0] // 2
    tail = line_step(crossed[1][half:], count)
    head = pair_swap(crossed[1][:half], count)
    moving = jnp.concatenate(
        [add(straight[1][:half], head), straight[1][half:]], axis=0
    )
    last = head
    for step in list(range(2, line)) + [0]:
        block = crossed[step]
        if step == 2:
            block = jnp.concatenate([block[:half], add(block[half:], tail)], axis=0)
        passed = pair_swap(after(block, last), count)
        last = passed
        moving = line_step(moving, count)
        if step == 0:
            return [straight[0], passed, moving]
        moving = add(straight[step], passed, moving)


def split_tall(terms, n_wide):
    sections, places, half, columns = terms.shape
    held = half // n_wide
    second = terms[..., : columns - PADDED // 2].reshape(sections, places, n_wide, held, -1)
    out = terms[..., columns - PADDED // 2 :].reshape(sections, places, 2, half // 2, PADDED // 2)
    out = jnp.transpose(out, (0, 1, 3, 2, 4)).reshape(sections, half, PADDED)
    out = out.reshape(sections, n_wide, places, held // places, 2, PADDED // 2)
    out = jnp.transpose(out, (0, 2, 1, 4, 3, 5)).reshape(sections, places, n_wide, held, -1)
    return jnp.concatenate([second, out], axis=-1)


def body(
    map_p2,
    map_p3,
    map_p4,
    map_p5,
    boxes,
    levels,
    classes,
    sampled,
    counts,
    targets,
    first_weight,
    second_weight,
    out_weight,
    hidden_bias,
    out_bias,
    first_moment,
    second_moment,
    out_moment,
    hidden_moment,
    bias_moment,
    first_average,
    second_average,
    out_average,
    hidden_average,
    bias_average,
):
    n_section = lax.axis_size("section")
    n_fc = lax.axis_size("fc")
    n_wide = lax.axis_size("wide")
    section = lax.axis_index("section")
    fc = lax.axis_index("fc")
    wide = lax.axis_index("wide")
    everywhere = ("section", "wide", "fc")
    maps = [map_p2, map_p3, map_p4, map_p5]
    channels = map_p2.shape[3]
    height = map_p2.shape[1] * n_section
    width = map_p2.shape[2]
    rows_dev = boxes.shape[0]
    rows_own = rows_dev // (n_section * n_fc)
    held = first_weight.shape[1]
    classes_out = out_weight.shape[1]
    place = section.astype(jnp.int32).reshape(1)

    ring = 4 <= n_wide <= 16
    line = n_wide // 2
    rows_tall = out_weight.shape[0]
    rows_fc = n_section * rows_own

    live = ((jnp.arange(rows_dev, dtype=jnp.int32) < counts[0]) & (sampled > 0)).astype(F32)
    live_count = jnp.sum(live)
    high = jnp.floor(live_count / 32.0)
    count_columns = jnp.broadcast_to(
        jnp.stack([high, live_count - 32.0 * high])[None], (rows_tall, 2)
    )
    tall = jnp.concatenate([out_weight, hidden_bias, count_columns], axis=1)
    tall = jnp.pad(tall, ((0, 0), (0, PADDED - tall.shape[1])))
    tall = jnp.concatenate([tall[:, : PADDED // 2], tall[:, PADDED // 2 :]], axis=0)
    piece = jnp.concatenate([second_weight.T, tall], axis=1).astype(BF16)
    if ring:
        order = jnp.stack(
            [
                ((wide // 2 - step) % line) * 2 + ((wide % 2) ^ side)
                for side in range(2)
                for step in range(line)
            ]
            + [section, fc]
        ).astype(jnp.int32)
        blocks = n_wide
        small_own, small_other = gather_small(piece, n_wide)
        w_second_turned, w_second, w_out, w_out_turned = assemble(
            blocks, order, small_own, small_other
        )
    else:
        order = jnp.stack([jnp.zeros_like(section), section, fc]).astype(jnp.int32)
        blocks = 1
        small = lax.all_gather(piece, everywhere, axis=0, tiled=True)
        small = small.reshape(-1, n_fc, held, piece.shape[1])
        w_second_turned = jnp.transpose(
            small[..., : second_weight.shape[0]], (1, 0, 2, 3)
        ).reshape(n_fc, -1, second_weight.shape[0])
        w_second = jnp.transpose(w_second_turned, (0, 2, 1)).reshape(
            -1, w_second_turned.shape[1]
        )
        w_out = small[..., second_weight.shape[0] :].reshape(-1, 2, rows_tall, PADDED // 2)
        w_out = jnp.transpose(w_out, (0, 2, 1, 3)).reshape(-1, PADDED)
        w_out_turned = w_out.T
    hidden = w_out.shape[0]
    biases = w_out[:, classes_out : classes_out + 2].astype(F32)
    counted = jnp.sum(w_out[:, classes_out + 2 : classes_out + 4].astype(F32), axis=0)
    total = (32.0 * counted[0] + counted[1]) / (rows_tall * n_section * n_fc)

    turned = turn_weight(first_weight.T)
    if ring:
        straight, crossed, tail = gather_ring(turned, n_wide)
    else:
        straight, crossed, tail = (
            [lax.all_gather(turned, "wide", axis=0, tiled=True)],
            [],
            [],
        )
    pieces = straight + crossed + tail

    def own_slots(values, axis):
        start = section * (n_fc * rows_own)
        mine = lax.dynamic_slice_in_dim(values, start + fc * rows_own, rows_own, axis)
        theirs = lax.dynamic_slice_in_dim(values, start + (1 - fc) * rows_own, rows_own, axis)
        return jnp.concatenate([mine, theirs], axis)

    parameters = box_parameters(own_slots(boxes, 0), own_slots(levels, 0), height, width)
    slot_values = jnp.concatenate([live[None], classes.astype(F32)[None], targets.T], axis=0)
    slots = own_slots(slot_values, 1)[:, :rows_own]
    slots = jnp.concatenate(
        [slots[0:1], jnp.full((1, rows_own), 1.0, F32) / total, slots[1:]], axis=0
    )
    slots = jnp.pad(slots, ((0, 1), (0, 0)))

    half_own = jnp.concatenate([level_map.reshape(-1, channels) for level_map in maps], axis=0)
    table = build_table(place, half_own, swap(half_own, "section"), height, width)
    crops_mine = crop_forward(parameters, table, 0, rows_own)
    passed_mine = swap(crops_mine, "section")
    crops_theirs = crop_forward(parameters, table, rows_own, rows_own)
    passed_theirs = swap(crops_theirs, "section")
    inputs = [crops_mine, passed_mine, crops_theirs, passed_theirs]
    inputs_all = jnp.concatenate(inputs, axis=0)

    def first_layer(parts):
        terms = [dot_last(part, inputs_all) for part in parts]
        mine = jnp.concatenate([term[:, :rows_fc] for term in terms], axis=0)
        theirs = jnp.concatenate([term[:, rows_fc:] for term in terms], axis=0)
        return mine + swap(theirs, "fc")

    if ring:
        early = first_layer(straight[:-1] + crossed[:-1])
        late = first_layer([straight[-1], crossed[-1]])
        end = first_layer(tail)
        cut = (line - 1) * held
        pre = jnp.concatenate([early[:cut], late[:held], early[cut:], late[held:], end], axis=0)
    else:
        pre = first_layer(pieces)
    pre_own = pre[:, :rows_own]
    pre_other = swap(pre[:, rows_own:], "section")

    grad_own, grad_other, act_first, act_second, grad_second, grad_logits, losses = middle(
        blocks,
        order,
        pre_own,
        pre_other,
        biases,
        w_second_turned,
        w_second,
        w_out_turned,
        w_out,
        jnp.pad(out_bias, (0, PADDED - classes_out))[:, None],
        slots,
    )
    grad_mine = jnp.concatenate([grad_own, swap(grad_other, "section")], axis=1)

    rate = 0.15 * math.sqrt(rows_dev * n_wide)
    if ring:
        def all_slots(parts):
            mine = jnp.concatenate([grad_mine[at * held : (at + 1) * held] for at in parts], axis=0)
            return jnp.concatenate([mine, swap(mine, "fc")], axis=1)

        first_at = [1, line + 1]
        rest_at = [at for at in range(n_wide) if at not in first_at]
        first_grads = all_slots(first_at)
        rest_grads = all_slots(rest_at)
        terms = dict(zip(first_at, weight_grad(2, first_grads, inputs)))
        terms.update(zip(rest_at, weight_grad(len(rest_at), rest_grads, inputs)))
        first_sums = scatter_ring(
            [terms[at] for at in range(line)], [terms[line + at] for at in range(line)], n_wide
        )
        grad_all = jnp.concatenate(
            [
                rest_grads[:held],
                first_grads[:held],
                rest_grads[held : (line) * held],
                first_grads[held:],
                rest_grads[line * held :],
            ],
            axis=0,
        )
    else:
        grad_all = jnp.concatenate([grad_mine, swap(grad_mine, "fc")], axis=1)
        first_sums = [
            lax.psum_scatter(
                weight_grad(1, grad_all, inputs)[0], "wide", scatter_dimension=0, tiled=True
            )
        ]

    keep_mine, send_mine, keep_theirs, send_theirs = input_grad(grad_all.T, pieces)
    back_mine = swap(send_mine, "section")
    back_theirs = swap(send_theirs, "section")
    before = crop_backward(place, parameters, keep_mine, back_mine, 0, height, width)
    map_own, map_other = crop_backward(
        place, parameters, keep_theirs, back_theirs, rows_own, height, width, before
    )
    own_grad = map_own + swap(map_other, "section").astype(F32)
    map_grads = []
    start_cell = 0
    for level_map in maps:
        cell_count = level_map.shape[1] * level_map.shape[2]
        map_grads.append(own_grad[start_cell : start_cell + cell_count].reshape(level_map.shape))
        start_cell = start_cell + cell_count

    terms_own, terms_other, bias_terms = small_grads(
        blocks, order, act_first, act_second, grad_second, grad_own, grad_other, grad_logits
    )
    if ring:
        small_sum = scatter_small(terms_own, terms_other, n_wide)
    else:
        terms = jnp.stack(
            [jnp.where(section == at, terms_own, terms_other) for at in range(n_section)]
        )
        terms = jnp.where(fc == 0, terms, terms[:, ::-1])
        terms = jnp.transpose(split_tall(terms, n_wide), (0, 2, 1, 3, 4))
        small_sum = lax.psum_scatter(
            terms.reshape(-1, terms.shape[-1]), everywhere, scatter_dimension=0, tiled=True
        ).astype(F32)
    second_sum = small_sum[:, : second_weight.shape[0]]
    tall_sum = small_sum[:, second_weight.shape[0] :]
    tall_sum = jnp.concatenate([tall_sum[:rows_tall], tall_sum[rows_tall:]], axis=1)
    vector = jnp.concatenate([bias_terms[:classes_out, 0], jnp.sum(losses).reshape(1)])
    if ring:
        vector = jnp.pad(vector, (0, PADDED - vector.shape[0])).reshape(4, 128)
        for move in (
            lambda value: swap(value, "section"),
            lambda value: swap(value, "fc"),
            lambda value: pair_swap(value, n_wide),
        ):
            vector = vector + move(vector)
        vector = functools.reduce(
            jnp.add, [vector] + [line_step(vector, n_wide, steps) for steps in range(1, line)]
        ).reshape(-1)
    else:
        vector = lax.psum(vector, everywhere)

    first_out = renew_first(first_sums, first_weight.T, first_moment.T, first_average.T, rate)
    second_out = renew(second_weight, second_moment, second_average, second_sum.T, rate)
    out_out = renew(out_weight, out_moment, out_average, tall_sum[:, :classes_out], rate)
    hidden_out = renew(
        hidden_bias,
        hidden_moment,
        hidden_average,
        tall_sum[:, classes_out : classes_out + 2],
        rate,
    )
    bias_out = renew(out_bias, bias_moment, bias_average, vector[:classes_out], 4.0)
    return (
        vector[classes_out],
        total,
        map_grads[0],
        map_grads[1],
        map_grads[2],
        map_grads[3],
        first_out[0].T,
        first_out[1].T,
        first_out[2].T,
        *second_out,
        *out_out,
        *hidden_out,
        *bias_out,
    )


def solution(mesh):
    maps = P("wide", "section", None, "fc")
    wide_weight = P("fc", ("section", "wide"))
    tall_weight = P(("section", "wide", "fc"), None)
    in_specs = (
        (maps,) * 4
        + (P("wide", None), P("wide"), P("wide"), P("wide"), P("wide"), P("wide", None))
        + (wide_weight, wide_weight, tall_weight, tall_weight, P()) * 3
    )
    out_specs = (
        (P(), P())
        + (maps,) * 4
        + (wide_weight,) * 6
        + (tall_weight,) * 6
        + (P(),) * 3
    )
    return jax.shard_map(body, mesh=mesh, in_specs=in_specs, out_specs=out_specs, check_vma=False)
```

```python
import functools
import math

import jax
import jax.numpy as jnp
from jax import lax
from jax.experimental import pallas as pl
from jax.experimental.pallas import tpu as pltpu
from jax.sharding import PartitionSpec as P

CLASSES = 81
BINS = 7
CELLS = BINS * BINS
WINDOW = 24
WINDOWS = (24, 16, 8)
GROUP = 16
CHAINS = 4
SETS = 2
PADDED = 512
WIDTH = 5 * CLASSES - 4
BIAS_AT = 416
LOSS_AT = 448
MOMENTUM = 0.9
AVERAGE = 0.7
DECAY = 0.0001
SMOOTH = 0.5

F32 = jnp.float32
BF16 = jnp.bfloat16
VMEM_LIMIT = 52 * 2**20


def smem():
    return pl.BlockSpec(memory_space=pltpu.SMEM)


def vmem():
    return pl.BlockSpec(memory_space=pltpu.VMEM)


def lasting(microseconds):
    return pl.CostEstimate(
        flops=0, bytes_accessed=int(microseconds * 1e3), transcendentals=0
    )


def limits():
    return pltpu.CompilerParams(vmem_limit_bytes=VMEM_LIMIT)


def level_plan(height, width):
    shapes = [(height >> depth, width >> depth) for depth in range(4)]
    strides = [max(rows, WINDOW) for rows, cols in shapes]
    bases = [0]
    for depth in range(4):
        bases.append(bases[-1] + strides[depth] * shapes[depth][1])
    total = -(-(bases[-1] + 2 * WINDOW) // GROUP) * GROUP
    return shapes, strides, bases[:4], total


def half_starts(shapes):
    starts = [0]
    for rows, cols in shapes:
        starts.append(starts[-1] + rows // 2 * cols)
    return starts


def table_kernel(height, width, place, own, other, table):
    shapes, strides, bases, total = level_plan(height, width)
    starts = half_starts(shapes)
    table[...] = jnp.zeros_like(table)

    def fill(source, bottom):
        for depth, (rows, cols) in enumerate(shapes):
            half = rows // 2

            def column(x, carry, depth=depth, half=half, cols=cols):
                cells = source[pl.ds(starts[depth] + x, half, stride=cols), :]
                table[pl.ds(bases[depth] + x * strides[depth] + bottom * half, half), :] = cells
                return carry

            lax.fori_loop(0, cols, column, 0, unroll=4)

    bottom = place[0]
    fill(own, bottom)
    fill(other, 1 - bottom)


def build_table(place, own, other, height, width):
    total = level_plan(height, width)[3]
    return pl.pallas_call(
        functools.partial(table_kernel, height, width),
        out_shape=jax.ShapeDtypeStruct((total, own.shape[1]), F32),
        in_specs=[smem(), vmem(), vmem()],
        out_specs=vmem(),
        compiler_params=limits(),
        cost_estimate=lasting(5.0),
        name="build_table",
    )(place, own, other)


def plan_kernel(
    height,
    width,
    place,
    counts,
    boxes,
    levels,
    classes,
    sampled,
    targets,
    address,
    weight,
    row_values,
    stride,
    slots,
    features,
):
    shapes, strides, bases, total = level_plan(height, width)
    count = boxes.shape[1]
    own = address.shape[1]
    share = own // 2
    section, fc = place[0], place[1]
    lane = lax.broadcasted_iota(jnp.int32, (1, count), 1)
    live = (lane < counts[0]) & (sampled[...] > 0)
    key = (jnp.where(live, levels[...], 4) * count + lane).astype(F32)
    across = jnp.broadcast_to(key, (128, count))
    down = jnp.transpose(across)
    before = jnp.zeros((count, 128), F32)
    for start in range(0, count, 128):
        before = before + jnp.where(key[:, start : start + 128] < down, 1.0, 0.0)
    rank = jnp.sum(before, axis=1, keepdims=True).astype(jnp.int32)
    seat = rank // 2
    side = jnp.where(seat % 2 == fc, 0, share)
    seat = jnp.where(rank % 2 == section, seat // 2 + side, -1)
    deal = jnp.where(
        jnp.broadcast_to(seat, (count, own)) == lax.broadcasted_iota(jnp.int32, (count, own), 1),
        1.0,
        0.0,
    )
    features[...] = jnp.zeros_like(features)
    features[0:4, :] = boxes[...]
    features[4:8, :] = targets[...]
    features[8:9, :] = levels[...].astype(F32)
    features[9:10, :] = classes[...].astype(F32)
    features[10:11, :] = jnp.where(live, 1.0, 0.0)
    dealt = jnp.dot(
        features[...], deal, preferred_element_type=F32, precision=lax.Precision.HIGHEST
    )
    slots[...] = jnp.zeros_like(slots)
    slots[0:1, :] = dealt[10:11, 0:share]
    slots[2:3, :] = dealt[9:10, 0:share]
    slots[3:7, :] = dealt[4:8, 0:share]
    level = (dealt[8:9, :] + 0.5).astype(jnp.int32)

    def choose(values, kind):
        out = jnp.full(level.shape, values[3], kind)
        for depth in range(3):
            out = jnp.where(level == depth, jnp.asarray(values[depth], kind), out)
        return out

    reach_y = choose([h - 1 for h, w in shapes], F32)
    reach_x = choose([w - 1 for h, w in shapes], F32)
    step = choose(strides, jnp.int32)
    base = choose(bases, jnp.int32)
    top = (dealt[0:1, :] - 0.25 * dealt[2:3, :]) * reach_y
    length_y = 0.5 * dealt[2:3, :] * reach_y
    left = (dealt[1:2, :] - 0.25 * dealt[3:4, :]) * reach_x
    length_x = 0.5 * dealt[3:4, :] * reach_x
    first = jnp.clip(jnp.floor(top + length_y * (0.25 / 7.0)), 0.0, reach_y - 1.0)
    start = base + first.astype(jnp.int32)
    for at in range(2 * BINS):
        points = left + length_x * ((at // 2 + (at % 2 + 0.5) * 0.5) / 7.0)
        lower = jnp.clip(jnp.floor(points), 0.0, reach_x - 1.0)
        address[at : at + 1, :] = start + lower.astype(jnp.int32) * step
        weight[at : at + 1, :] = points - lower
    for at, value in enumerate((top, length_y, first, reach_y - 1.0)):
        row_values[at : at + 1, :] = value
    stride[0:1, :] = step
    stride[1:2, :] = jnp.where(dealt[10:11, :] > 0.5, choose([3, 2, 1, 1], jnp.int32), 0)


def plan(place, counts, boxes, levels, classes, sampled, targets, own, height, width):
    whole = jax.ShapeDtypeStruct
    count = boxes.shape[0]
    return pl.pallas_call(
        functools.partial(plan_kernel, height, width),
        out_shape=(
            whole((2 * BINS, own), jnp.int32),
            whole((2 * BINS, own), F32),
            whole((4, own), F32),
            whole((2, own), jnp.int32),
            whole((8, own // 2), F32),
        ),
        in_specs=[smem()] * 2 + [vmem()] * 5,
        out_specs=(vmem(),) * 5,
        scratch_shapes=[pltpu.VMEM((16, count), F32)],
        compiler_params=limits(),
        cost_estimate=lasting(3.0),
        name="plan",
    )(place, counts, boxes.T, levels[None], classes[None], sampled[None], targets.T)


def row_weights(values, index, offset):
    top, length, first, last = values
    total = None
    for place in (0.25, 0.75):
        points = top + length * ((index + place) / 7.0)
        lower = jnp.minimum(jnp.maximum(jnp.floor(points), 0.0), last)
        upper_weight = points - lower
        distance = offset - (lower - first)
        part = jnp.where(
            distance == 0.0, 1.0 - upper_weight, jnp.where(distance == 1.0, upper_weight, 0.0)
        )
        total = part if total is None else total + part
    return total * 0.25


def crop_kernel(rows, first, address, weight, row_values, stride, table, out, turned):
    def crops(window, step):
        depth = -(-BINS * window // 128) * 128
        lane = lax.broadcasted_iota(jnp.int32, (8, depth), 1)
        offset = (lane % window).astype(F32)
        index = lax.broadcasted_iota(jnp.int32, (8, depth), 0).astype(F32)
        inside = (
            lax.broadcasted_iota(jnp.int32, (8 * BINS, depth), 0) // 8
            == lax.broadcasted_iota(jnp.int32, (8 * BINS, depth), 1) // window
        )

        for part in range(GROUP):
            row = first + step * GROUP + part
            weights = row_weights([row_values[at, row] for at in range(4)], index, offset)
            left = jnp.where(inside, jnp.concatenate([weights] * BINS, axis=0), 0.0)
            step_x = stride[0, row]
            columns = []
            for k in range(BINS):
                total = None
                for m in range(2):
                    place = address[2 * k + m, row]
                    upper = weight[2 * k + m, row]
                    near = table[pl.ds(place, window), :]
                    far = table[pl.ds(place + step_x, window), :]
                    value = near + upper * (far - near)
                    total = value if total is None else total + value
                columns.append(total)
            columns.append(jnp.zeros((depth - BINS * window, 128), F32))
            right = jnp.concatenate(columns, axis=0).astype(BF16)
            crop = jnp.dot(left.astype(BF16), right, preferred_element_type=F32)
            for k in range(BINS):
                turned[pl.ds(part + k * BINS * GROUP, BINS, stride=GROUP), :] = crop[
                    8 * k : 8 * k + BINS
                ]

    def group(step, carry):
        start = pl.multiple_of(step * GROUP, GROUP)
        eights = stride[1, first + step * GROUP]
        for window in WINDOWS:

            @pl.when(eights == window // 8)
            def live_slots(window=window):
                crops(window, step)

        @pl.when(eights > 0)
        def store():
            for cell in range(CELLS):
                out[pl.ds(start, GROUP), cell * 128 : (cell + 1) * 128] = turned[
                    cell * GROUP : (cell + 1) * GROUP, :
                ].astype(BF16)

        @pl.when(eights == 0)
        def dead_slots():
            out[pl.ds(start, GROUP), :] = jnp.zeros((GROUP, CELLS * 128), BF16)

        return carry

    lax.fori_loop(0, rows // GROUP, group, 0)


def crop_forward(parameters, table, first, rows):
    return pl.pallas_call(
        functools.partial(crop_kernel, rows, first),
        out_shape=jax.ShapeDtypeStruct((rows, CELLS * 128), BF16),
        in_specs=[smem()] * 4 + [vmem()],
        out_specs=vmem(),
        scratch_shapes=[pltpu.VMEM((CELLS * GROUP, 128), F32)],
        compiler_params=limits(),
        cost_estimate=lasting(0.07 * rows),
        name="crop_forward",
    )(*parameters, table)


def spread_kernel(rows, first, height, width, last, place, address, weight, row_values, stride, keep, passed, *refs):
    shapes, strides, bases, total = level_plan(height, width)
    starts = half_starts(shapes)
    if last:
        before, own, other, turned, half, *tables = refs
    else:
        out, turned, *tables = refs
    for table in tables:
        table[...] = jnp.zeros_like(table)
    turned[pl.ds(CELLS * GROUP, GROUP), :] = jnp.zeros((GROUP, 128), F32)

    def spread(window, base, few):
        index = (lax.broadcasted_iota(jnp.int32, (window, 128), 1) % 8).astype(F32)
        offset = lax.broadcasted_iota(jnp.int32, (window, 128), 0).astype(F32)
        long_row = lax.broadcasted_iota(jnp.int32, (BINS * window, 128), 0)
        long_lane = lax.broadcasted_iota(jnp.int32, (BINS * window, 128), 1)
        inside = (long_row // window == long_lane // 8) & (long_lane % 8 < BINS)
        results = []
        for at in range(SETS * CHAINS):
            part = few * SETS * CHAINS + at
            row = base + at
            weights = row_weights([row_values[at, row] for at in range(4)], index, offset)
            left = jnp.where(inside, jnp.concatenate([weights] * BINS, axis=0), 0.0).astype(BF16)
            pieces = [
                turned[pl.ds(part + k * BINS * GROUP, 8, stride=GROUP), :] for k in range(BINS)
            ]
            pieces.append(jnp.zeros((128 - 8 * BINS, 128), F32))
            right = jnp.concatenate(pieces, axis=0).astype(BF16)
            results.append(jnp.dot(left, right, preferred_element_type=F32))
        for head in range(0, SETS * CHAINS, CHAINS):
            for k in range(BINS):
                for m in range(2):
                    for chain in range(CHAINS):
                        row = base + head + chain
                        table = tables[chain]
                        at = address[2 * k + m, row]
                        next_at = at + stride[0, row]
                        value = results[head + chain][k * window : (k + 1) * window]
                        upper = value * weight[2 * k + m, row]
                        near = table[pl.ds(at, window), :] + (value - upper)
                        far = table[pl.ds(next_at, window), :] + upper
                        table[pl.ds(at, window), :] = near
                        table[pl.ds(next_at, window), :] = far

    def group(step, carry):
        start = pl.multiple_of(step * GROUP, GROUP)

        @pl.when(stride[1, first + step * GROUP] > 0)
        def live_slots():
            for cell in range(CELLS):
                span = slice(cell * 128, (cell + 1) * 128)
                turned[cell * GROUP : (cell + 1) * GROUP, :] = keep[
                    pl.ds(start, GROUP), span
                ].astype(F32) + passed[pl.ds(start, GROUP), span].astype(F32)

            def some(few, carry):
                base = first + step * GROUP + few * SETS * CHAINS
                eights = stride[1, base]
                for window in WINDOWS:

                    @pl.when(eights == window // 8)
                    def one_window(window=window):
                        spread(window, base, few)

                return carry

            lax.fori_loop(0, GROUP // (SETS * CHAINS), some, 0)

        return carry

    lax.fori_loop(0, rows // GROUP, group, 0)
    result = tables[0] if last else out

    def summed(step, carry):
        span = pl.ds(pl.multiple_of(step * GROUP, GROUP), GROUP)
        value = tables[0][span, :]
        for table in tables[1:]:
            value = value + table[span, :]
        if last:
            value = value + before[span, :]
        result[span, :] = value
        return carry

    lax.fori_loop(0, total // GROUP, summed, 0)
    if not last:
        return

    def collect(target, bottom):
        for depth, (level_rows, cols) in enumerate(shapes):
            count = level_rows // 2

            def column(x, carry, depth=depth, count=count, cols=cols):
                cells = result[pl.ds(bases[depth] + x * strides[depth] + bottom * count, count), :]
                target[pl.ds(starts[depth] + x, count, stride=cols), :] = cells
                return carry

            lax.fori_loop(0, cols, column, 0, unroll=4)

    bottom = place[0]
    collect(own, bottom)
    collect(half, 1 - bottom)
    other[...] = half[...].astype(BF16)


def crop_backward(place, parameters, keep, passed, first, height, width, before=None):
    rows = keep.shape[0]
    shapes, strides, bases, total = level_plan(height, width)
    cells = half_starts(shapes)[-1]
    last = before is not None
    turned = pltpu.VMEM(((CELLS + 1) * GROUP, 128), F32)
    tables = [pltpu.VMEM((total, 128), F32)] * CHAINS
    if last:
        out_shape = (
            jax.ShapeDtypeStruct((cells, 128), F32),
            jax.ShapeDtypeStruct((cells, 128), BF16),
        )
        scratch = [turned, pltpu.VMEM((cells, 128), F32)] + tables
    else:
        out_shape = jax.ShapeDtypeStruct((total, 128), F32)
        scratch = [turned] + tables
    return pl.pallas_call(
        functools.partial(spread_kernel, rows, first, height, width, last),
        out_shape=out_shape,
        in_specs=[smem()] * 5 + [vmem()] * (3 if last else 2),
        out_specs=(vmem(),) * 2 if last else vmem(),
        scratch_shapes=scratch,
        compiler_params=limits(),
        cost_estimate=lasting(0.12 * rows),
        name="crop_backward",
    )(place, *parameters, keep, passed, *([before] if last else []))


def natural_row(cell):
    k, i = divmod(cell, BINS)
    return i * BINS + k


def turn_kernel(counts, weight, sampled, second, out_weight, hidden_bias, out, turned, tall):
    held, lanes = weight.shape
    depth = second.shape[1]
    rows = out_weight.shape[0]
    half = PADDED // 2
    for tile in range(CELLS):
        turned[tile * 128 : (tile + 1) * 128, 0:held] = jnp.transpose(
            weight[:, tile * 128 : (tile + 1) * 128]
        )
    for cell in range(CELLS):
        block = turned[pl.ds(natural_row(cell), 128, stride=CELLS), :]
        out[:, cell * 128 : (cell + 1) * 128] = jnp.transpose(block)[0:held].astype(BF16)
    lane = lax.broadcasted_iota(jnp.int32, sampled.shape, 1)
    live = jnp.sum(
        jnp.where((lane < counts[0]) & (sampled[...] > 0), 1.0, 0.0), axis=1, keepdims=True
    )
    high = jnp.floor(live / 32.0)
    tall[...] = jnp.zeros_like(tall)
    tall[:, 0:WIDTH] = out_weight[...]
    column = lax.broadcasted_iota(jnp.int32, (rows, 128), 1) + (PADDED - 128)
    value = tall[:, PADDED - 128 : PADDED]
    for at, part in enumerate(
        (hidden_bias[:, 0:1], hidden_bias[:, 1:2], high, live - 32.0 * high)
    ):
        value = jnp.where(column == WIDTH + at, part, value)
    tall[:, PADDED - 128 : PADDED] = value
    out[:, lanes : lanes + depth] = second[...].astype(BF16)
    out[:, lanes + depth : lanes + depth + half] = jnp.concatenate(
        [tall[:, 0:half], tall[:, half:PADDED]], axis=0
    ).astype(BF16)


def turn_weight(counts, weight, sampled, second, out_weight, hidden_bias):
    held, lanes = weight.shape
    return pl.pallas_call(
        turn_kernel,
        out_shape=jax.ShapeDtypeStruct((held, lanes + second.shape[1] + PADDED // 2), BF16),
        in_specs=[smem()] + [vmem()] * 5,
        out_specs=vmem(),
        scratch_shapes=[
            pltpu.VMEM((lanes, 128), F32),
            pltpu.VMEM((out_weight.shape[0], PADDED), F32),
        ],
        compiler_params=limits(),
        cost_estimate=lasting(2.7),
        name="turn_weight",
    )(counts, weight, sampled[None], second, out_weight, hidden_bias)


def renew(weight, moment, average, grad, rate):
    step_value = grad + DECAY * weight
    moment_new = MOMENTUM * moment + step_value
    weight_new = weight - rate * (step_value + MOMENTUM * moment_new)
    average_new = AVERAGE * average + (1.0 - AVERAGE) * weight_new
    return (weight_new, moment_new, average_new)


def renew_kernel(rate, count, *refs):
    terms = refs[:count]
    kept = refs[count : count + 3]
    news = refs[count + 3 : count + 6]
    turned, *places = refs[count + 6 : count + 13]
    sems = refs[count + 13]
    held, lanes = terms[0].shape
    arrive = [
        pltpu.make_async_copy(kept[at], places[at], sems.at[at, 0]) for at in range(3)
    ]
    for copy in arrive:
        copy.start()
    for cell in range(CELLS):
        span = slice(cell * 128, (cell + 1) * 128)
        grad = terms[0][:, span].astype(F32)
        for term in terms[1:]:
            grad = grad + term[:, span].astype(F32)
        turned[pl.ds(natural_row(cell), 128, stride=CELLS), 0:held] = jnp.transpose(grad)
    for copy in arrive:
        copy.wait()
    leave = []
    for part in range(BINS):
        for tile in range(part * BINS, (part + 1) * BINS):
            span = slice(tile * 128, (tile + 1) * 128)
            grad = jnp.transpose(turned[span, :])[0:held]
            values = renew(*[place[:, span] for place in places[:3]], grad, rate)
            for at in range(3):
                places[3 + at][:, span] = values[at]
        span = pl.ds(part * BINS * 128, BINS * 128)
        for at in range(3):
            copy = pltpu.make_async_copy(
                places[3 + at].at[:, span], news[at].at[:, span], sems.at[at, 1 + part]
            )
            copy.start()
            leave.append(copy)
    for copy in leave:
        copy.wait()


def renew_first(terms, weight, moment, average, rate):
    held, lanes = weight.shape
    anywhere = pl.BlockSpec(memory_space=pl.ANY)
    return pl.pallas_call(
        functools.partial(renew_kernel, rate, len(terms)),
        out_shape=(jax.ShapeDtypeStruct(weight.shape, F32),) * 3,
        in_specs=[vmem()] * len(terms) + [anywhere] * 3,
        out_specs=(anywhere,) * 3,
        scratch_shapes=[pltpu.VMEM((lanes, 128), F32)]
        + [pltpu.VMEM((held, lanes), F32)] * 6
        + [pltpu.SemaphoreType.DMA((3, 1 + BINS))],
        compiler_params=limits(),
        cost_estimate=lasting(6.5),
        name="renew_first",
    )(*terms, weight, moment, average)


def renew_small_kernel(rate, count, *refs):
    terms = refs[:count]
    second, tall, hidden, bias = (refs[count + 3 * at : count + 3 * at + 3] for at in range(4))
    second_new, tall_new, hidden_new, bias_new = (
        refs[count + 12 + 3 * at : count + 15 + 3 * at] for at in range(4)
    )
    loss = refs[count + 24]
    rows = tall[0].shape[0]
    depth = second[0].shape[1]
    half = PADDED // 2
    total = terms[0][...].astype(F32)
    for term in terms[1:]:
        total = total + term[...].astype(F32)

    def give(targets, sources, grad, rate):
        for target, value in zip(targets, renew(*[ref[...] for ref in sources], grad, rate)):
            target[...] = value

    give(second_new, second, total[:, :depth], rate)
    sums = jnp.concatenate([total[:rows, depth:], total[rows:, depth:]], axis=1)
    give(tall_new, tall, sums[:, :WIDTH], rate)
    give(hidden_new, hidden, sums[:, WIDTH : WIDTH + 2], rate)
    spare = sums[:, PADDED - 128 : PADDED]
    start = BIAS_AT - (PADDED - 128)
    source = lax.broadcasted_iota(jnp.int32, (128, PADDED), 0)
    target = lax.broadcasted_iota(jnp.int32, (128, PADDED), 1)
    spread = jnp.dot(
        spare,
        jnp.where(source == start + target % 16, 1.0, 0.0),
        preferred_element_type=F32,
        precision=lax.Precision.HIGHEST,
    )
    row = lax.broadcasted_iota(jnp.int32, (rows, PADDED), 0)
    column = lax.broadcasted_iota(jnp.int32, (rows, PADDED), 1)
    line = jnp.sum(jnp.where(column // 16 == row, spread, 0.0), axis=0, keepdims=True)
    give(bias_new, bias, line[:, :WIDTH], 4.0)
    lane = lax.broadcasted_iota(jnp.int32, (rows, 128), 1) + (PADDED - 128)
    losses = jnp.where((lane >= LOSS_AT) & (lane < LOSS_AT + 3), spare, 0.0)
    loss[...] = jnp.sum(jnp.sum(losses, axis=1, keepdims=True), axis=0, keepdims=True)


def renew_small(terms, states, rate):
    states = [value for group in states for value in group]
    return pl.pallas_call(
        functools.partial(renew_small_kernel, rate, len(terms)),
        out_shape=tuple(jax.ShapeDtypeStruct(value.shape, F32) for value in states)
        + (jax.ShapeDtypeStruct((1, 1), F32),),
        in_specs=[vmem()] * (len(terms) + len(states)),
        out_specs=(vmem(),) * (len(states) + 1),
        compiler_params=limits(),
        cost_estimate=lasting(2.0),
        name="renew_small",
    )(*terms, *states)


def map_sum_kernel(own, passed, *outs):
    start = 0
    for out in outs:
        span = slice(start, start + out.shape[0])
        out[...] = own[span, :] + passed[span, :].astype(F32)
        start += out.shape[0]


def map_sum(own, passed, maps):
    sizes = [level_map.shape[1] * level_map.shape[2] for level_map in maps]
    grads = pl.pallas_call(
        map_sum_kernel,
        out_shape=tuple(jax.ShapeDtypeStruct((size, own.shape[1]), F32) for size in sizes),
        in_specs=[vmem()] * 2,
        out_specs=(vmem(),) * len(sizes),
        compiler_params=limits(),
        cost_estimate=lasting(2.0),
        name="map_sum",
    )(own, passed)
    return [grad.reshape(level_map.shape) for grad, level_map in zip(grads, maps)]


def gelu_parts(value):
    root = math.sqrt(2.0 / math.pi)
    square = value * value
    bend = jnp.tanh(root * (value + 0.044715 * square * value))
    half = 0.5 * (1.0 + bend)
    slope = half + 0.5 * value * (1.0 - bend * bend) * (
        root * (1.0 + 3.0 * 0.044715 * square)
    )
    return value * half, slope


def dot(left, right):
    return jnp.dot(left, right, preferred_element_type=F32)


def dot_last(left, right):
    return lax.dot_general(left, right, (((1,), (1,)), ((), ())), preferred_element_type=F32)


def middle_kernel(
    blocks,
    images,
    order,
    pre_own,
    pre_other,
    second_turned,
    second,
    out_turned,
    out_weight,
    out_bias,
    slots,
    grad_own,
    grad_other,
    act_first,
    act_second,
    grad_second,
    grad_logits,
    losses,
    live_total,
    pre_first,
    slope_first,
    slope_second,
    grad_first,
):
    hidden, rows = pre_first.shape
    half = hidden // 2
    size = half // blocks
    own_start = order[3 * blocks] * half
    other_start = (1 - order[3 * blocks]) * half
    for block in range(blocks):
        span = slice(block * size, (block + 1) * size)
        at = pl.multiple_of(own_start + order[block] * size, size)
        pre_first[pl.ds(at, size), :] = pre_own[span, :]
        at = pl.multiple_of(other_start + order[block] * size, size)
        pre_first[pl.ds(at, size), :] = pre_other[span, :]
    spare = out_weight[:, PADDED - 128 : PADDED].astype(F32)
    at = WIDTH - (PADDED - 128)
    counted = 32.0 * spare[:, at + 2 : at + 3] + spare[:, at + 3 : at + 4]
    slots_total = jnp.sum(counted, axis=0, keepdims=True) * (images / hidden)
    live_total[...] = slots_total
    act, slope = gelu_parts(pre_first[...] + spare[:, at : at + 1])
    slope_first[...] = slope
    act_first[...] = act.astype(BF16)
    pre_second = (
        dot(second_turned[0], act_first[0:half, :])
        + dot(second_turned[1], act_first[half:hidden, :])
        + spare[:, at + 1 : at + 2]
    )
    act, slope = gelu_parts(pre_second)
    slope_second[...] = slope
    act_second[...] = act.astype(BF16)
    logits = dot(out_turned[...], act_second[...]) + out_bias[...]

    row = lax.broadcasted_iota(jnp.int32, logits.shape, 0)
    live = slots[0:1, :]
    scale = 1.0 / slots_total
    chosen = slots[2:3, :].astype(jnp.int32)
    foreground = jnp.where(chosen > 0, 1.0, 0.0)
    is_score = row < CLASSES
    top = jnp.max(jnp.where(is_score, logits, -jnp.inf), axis=0, keepdims=True)
    power = jnp.where(is_score, jnp.exp(logits - top), 0.0)
    total = jnp.sum(power, axis=0, keepdims=True)
    matches = row == chosen
    picked = jnp.sum(jnp.where(matches, logits, 0.0), axis=0, keepdims=True)
    value = jnp.log(total) + top - picked
    grad = power / total - jnp.where(matches, 1.0, 0.0)
    delta_row = CLASSES + 4 * (chosen - 1)
    smooth_total = jnp.zeros_like(live)
    for part in range(4):
        mine = (row == delta_row + part) & (chosen > 0)
        offset = jnp.sum(jnp.where(mine, logits, 0.0), axis=0, keepdims=True) - slots[
            3 + part : 4 + part, :
        ]
        size_of = jnp.abs(offset)
        near = size_of < SMOOTH
        smooth_total = smooth_total + jnp.where(
            near, 0.5 * offset * offset / SMOOTH, size_of - 0.5 * SMOOTH
        )
        slope = jnp.where(near, offset / SMOOTH, jnp.where(offset > 0.0, 1.0, -1.0))
        grad = jnp.where(mine, slope, grad)
    losses[...] = live * (value + foreground * smooth_total)
    grad_logits[...] = (grad * (live * scale)).astype(BF16)
    grad_second[...] = (dot(out_weight[...], grad_logits[...]) * slope_second[...]).astype(BF16)
    grad_first[...] = dot(second[...], grad_second[...]) * slope_first[...]
    for block in range(blocks):
        span = slice(block * size, (block + 1) * size)
        at = pl.multiple_of(own_start + order[block] * size, size)
        grad_own[span, :] = grad_first[pl.ds(at, size), :].astype(BF16)
        at = pl.multiple_of(other_start + order[block] * size, size)
        grad_other[span, :] = grad_first[pl.ds(at, size), :].astype(BF16)


def middle(
    blocks, images, order, pre_own, pre_other, second_turned, second, out_turned, out_weight, out_bias, slots
):
    half, rows = pre_own.shape
    hidden = 2 * half
    low = lambda *shape: jax.ShapeDtypeStruct(shape, BF16)
    return pl.pallas_call(
        functools.partial(middle_kernel, blocks, images),
        out_shape=(
            low(half, rows),
            low(half, rows),
            low(hidden, rows),
            low(hidden, rows),
            low(hidden, rows),
            low(PADDED, rows),
            jax.ShapeDtypeStruct((1, rows), F32),
            jax.ShapeDtypeStruct((1, 1), F32),
        ),
        in_specs=[smem()] + [vmem()] * 8,
        out_specs=(vmem(),) * 8,
        scratch_shapes=[pltpu.VMEM((hidden, rows), F32)] * 4,
        compiler_params=limits(),
        cost_estimate=lasting(6.5),
        name="middle",
    )(order, pre_own, pre_other, second_turned, second, out_turned, out_weight, out_bias, slots)


def small_grads_kernel(
    blocks,
    parts,
    order,
    act_first,
    act_second,
    grad_second,
    grad_own,
    grad_other,
    grad_logits,
    losses,
    own,
    other,
    bias_out,
    second_sum,
    out_sum,
):
    hidden, rows = act_first.shape
    half = hidden // 2
    size = half // blocks
    section, fc, device = order[3 * blocks], order[3 * blocks + 1], order[3 * blocks + 2]
    for side in range(2):
        second_sum[side] = dot_last(
            grad_second[...], act_first[side * half : (side + 1) * half, :]
        ).astype(BF16)
    column = lax.broadcasted_iota(jnp.int32, (rows, PADDED), 1)
    value = dot_last(act_second[...], grad_logits[...])
    value = value + dot(grad_second[...], jnp.where(column == WIDTH + 1, 1.0, 0.0).astype(BF16))
    out_sum[...] = value
    ones = jnp.where(column == WIDTH, 1.0, 0.0).astype(BF16)
    for block in range(blocks):
        span = slice(block * size, (block + 1) * size)
        for values, where in ((grad_own, section), (grad_other, 1 - section)):
            at = pl.ds(pl.multiple_of(where * half + order[block] * size, size), size)
            out_sum[at, :] = out_sum[at, :] + dot(values[span, :], ones)
    bias = jnp.sum(grad_logits[...].astype(F32), axis=1, keepdims=True)
    bias_out[...] = bias
    part = size // 2
    if parts:
        tile = slice(PADDED - 128, PADDED)
        source = lax.broadcasted_iota(jnp.int32, (PADDED, 128), 0)
        target = lax.broadcasted_iota(jnp.int32, (PADDED, 128), 1) + (PADDED - 128)
        spread = jnp.where(target == BIAS_AT + source % 16, bias, 0.0).astype(BF16)
        row = lax.broadcasted_iota(jnp.int32, (hidden, PADDED), 0) % part
        pick = jnp.where(
            row == lax.broadcasted_iota(jnp.int32, (hidden, PADDED), 1) // 16, 1.0, 0.0
        ).astype(BF16)
        value = out_sum[:, tile] + dot(pick, spread)
        row = lax.broadcasted_iota(jnp.int32, (hidden, 128), 0) % part
        column = lax.broadcasted_iota(jnp.int32, (hidden, 128), 1) + (PADDED - 128)
        rest = jnp.sum(losses[...], axis=1, keepdims=True)
        for place in range(3):
            now = rest.astype(BF16).astype(F32)
            value = jnp.where((row == device) & (column == LOSS_AT + place), now, value)
            rest = rest - now
        out_sum[:, tile] = value
    for target, where in ((own, section), (other, 1 - section)):
        for near in range(2):
            lane = fc if near == 0 else 1 - fc
            for block in range(blocks):
                start = pl.multiple_of(where * half + order[blocks + block] * size, size)
                target[near, block * size : (block + 1) * size, 0:half] = second_sum[
                    lane, pl.ds(start, size), :
                ]
                at = pl.ds(pl.multiple_of(start + lane * part, part), part)
                for side in range(2):
                    target[
                        near,
                        block * size + side * part : block * size + (side + 1) * part,
                        half : half + PADDED // 2,
                    ] = out_sum[at, side * (PADDED // 2) : (side + 1) * (PADDED // 2)].astype(BF16)


def small_grads(
    blocks, parts, order, act_first, act_second, grad_second, grad_own, grad_other, grad_logits, losses
):
    hidden = act_first.shape[0]
    half = hidden // 2
    low = jax.ShapeDtypeStruct((2, half, half + PADDED // 2), BF16)
    return pl.pallas_call(
        functools.partial(small_grads_kernel, blocks, parts),
        out_shape=(low, low, jax.ShapeDtypeStruct((PADDED, 1), F32)),
        in_specs=[smem()] + [vmem()] * 7,
        out_specs=(vmem(),) * 3,
        scratch_shapes=[
            pltpu.VMEM((2, hidden, half), BF16),
            pltpu.VMEM((hidden, PADDED), F32),
        ],
        compiler_params=limits(),
        cost_estimate=lasting(4.0),
        name="small_grads",
    )(order, act_first, act_second, grad_second, grad_own, grad_other, grad_logits, losses)


def assemble_kernel(blocks, order, *refs):
    sources, (second_turned, second, out_weight, out_turned) = refs[:-4], refs[-4:]
    hidden = second.shape[0]
    half = hidden // 2
    size = half // blocks
    part = size // 2
    section, fc = order[3 * blocks], order[3 * blocks + 1]
    first = 0
    for at in range(0, len(sources), 4):
        for index, source in enumerate(sources[at : at + 4]):
            where = section if index < 2 else 1 - section
            lane = fc if index % 2 == 0 else 1 - fc
            for block in range(source.shape[0] // size):
                rows = slice(block * size, (block + 1) * size)
                start = pl.multiple_of(
                    where * half + order[2 * blocks + first + block] * size, size
                )
                second_turned[lane, pl.ds(start, size), :] = source[rows, 0:half]
                target = pl.ds(pl.multiple_of(start + lane * part, part), part)
                for side in range(2):
                    out_weight[target, side * (PADDED // 2) : (side + 1) * (PADDED // 2)] = source[
                        block * size + side * part : block * size + (side + 1) * part,
                        half : half + PADDED // 2,
                    ]
        first += sources[at].shape[0] // size
    for side in range(2):
        second[side * half : (side + 1) * half, :] = jnp.transpose(second_turned[side])
    out_turned[...] = jnp.transpose(out_weight[...])


def assemble(blocks, order, groups):
    sources = [source for group in groups for source in group]
    half = sum(group[0].shape[0] for group in groups)
    hidden = 2 * half
    low = lambda *shape: jax.ShapeDtypeStruct(shape, BF16)
    return pl.pallas_call(
        functools.partial(assemble_kernel, blocks),
        out_shape=(low(2, hidden, half), low(hidden, hidden), low(hidden, PADDED), low(PADDED, hidden)),
        in_specs=[smem()] + [vmem()] * len(sources),
        out_specs=(vmem(),) * 4,
        compiler_params=limits(),
        cost_estimate=lasting(5.0),
        name="assemble",
    )(order, *sources)


def lane_blocks(lanes):
    for parts in (7, 1):
        if lanes % (128 * parts) == 0:
            return parts, lanes // parts


def join_kernel(straight, passed_head, crossed, passed_tail, moving, cross):
    half = straight.shape[0] // 2
    moving[0:half, :] = (
        straight[0:half, :].astype(F32) + passed_head[...].astype(F32)
    ).astype(BF16)
    moving[half : 2 * half, :] = straight[half : 2 * half, :]
    cross[0:half, :] = crossed[0:half, :]
    cross[half : 2 * half, :] = (
        crossed[half : 2 * half, :].astype(F32) + passed_tail[...].astype(F32)
    ).astype(BF16)


def join(straight, passed_head, crossed, passed_tail):
    return pl.pallas_call(
        join_kernel,
        out_shape=(jax.ShapeDtypeStruct(straight.shape, BF16),) * 2,
        in_specs=[vmem()] * 4,
        out_specs=(vmem(),) * 2,
        compiler_params=limits(),
        cost_estimate=lasting(1.5),
        name="join",
    )(straight, passed_head, crossed, passed_tail)


def input_grad_kernel(count, grad, *refs):
    weight = jnp.concatenate([ref[...] for ref in refs[:count]], axis=0)
    value = dot(grad[...], weight).astype(BF16)
    start = 0
    for out in refs[count:]:
        out[...] = value[start : start + out.shape[0]]
        start += out.shape[0]


def input_grad(grad, pieces, sizes, lanes):
    parts, size = lane_blocks(lanes)
    return pl.pallas_call(
        functools.partial(input_grad_kernel, len(pieces)),
        out_shape=tuple(jax.ShapeDtypeStruct((rows, lanes), BF16) for rows in sizes),
        grid=(parts,),
        in_specs=[pl.BlockSpec(grad.shape, lambda step: (0, 0))]
        + [pl.BlockSpec((piece.shape[0], size), lambda step: (0, step)) for piece in pieces],
        out_specs=tuple(pl.BlockSpec((rows, size), lambda step: (0, step)) for rows in sizes),
        compiler_params=limits(),
        cost_estimate=lasting(5.0),
        name="input_grad",
    )(grad, *pieces)


def line_order(line):
    return (0, 1, 3, 2) if line == 4 else tuple(range(line))


def pair_swap(value, count):
    return lax.ppermute(value, "wide", [(at, at ^ 1) for at in range(count)])


def line_step(value, count, way=1):
    places = line_order(count // 2)
    steps = []
    for at, place in enumerate(places):
        target = places[(at + way) % len(places)]
        steps += [(2 * place + side, 2 * target + side) for side in range(2)]
    return lax.ppermute(value, "wide", sorted(steps))


def line_swap(value, count, bit):
    return lax.ppermute(value, "wide", [(at, at ^ (2 * bit)) for at in range(count)])


def swap(value, axis):
    return lax.ppermute(value, axis, [(0, 1), (1, 0)])


def together(*values):
    return lax.optimization_barrier(values)


def add(*terms):
    total = terms[0].astype(F32)
    for term in terms[1:]:
        total = total + term.astype(F32)
    return total.astype(BF16)


def ring_order(wide, line):
    places = line_order(line)
    here = sum((jnp.where(wide // 2 == place, at, 0) for at, place in enumerate(places)))
    table = lambda index: sum(
        (jnp.where(index == at, place, 0) for at, place in enumerate(places))
    )
    return [
        table((here - step) % line) * 2 + ((wide % 2) ^ side)
        for side in range(2)
        for step in range(line)
    ]


def swap_order(wide, line):
    return [
        ((wide // 2) ^ step) * 2 + ((wide % 2) ^ side) for side in range(2) for step in range(line)
    ]


def split_tall(terms, n_wide):
    sections, places, half, columns = terms.shape
    held = half // n_wide
    second = terms[..., : columns - PADDED // 2].reshape(sections, places, n_wide, held, -1)
    out = terms[..., columns - PADDED // 2 :].reshape(sections, places, 2, half // 2, PADDED // 2)
    out = jnp.transpose(out, (0, 1, 3, 2, 4)).reshape(sections, half, PADDED)
    out = out.reshape(sections, n_wide, places, held // places, 2, PADDED // 2)
    out = jnp.transpose(out, (0, 2, 1, 4, 3, 5)).reshape(sections, places, n_wide, held, -1)
    return jnp.concatenate([second, out], axis=-1)


def body(
    map_p2,
    map_p3,
    map_p4,
    map_p5,
    boxes,
    levels,
    classes,
    sampled,
    counts,
    targets,
    first_weight,
    second_weight,
    out_weight,
    hidden_bias,
    out_bias,
    first_moment,
    second_moment,
    out_moment,
    hidden_moment,
    bias_moment,
    first_average,
    second_average,
    out_average,
    hidden_average,
    bias_average,
):
    n_section = lax.axis_size("section")
    n_fc = lax.axis_size("fc")
    n_wide = lax.axis_size("wide")
    section = lax.axis_index("section")
    fc = lax.axis_index("fc")
    wide = lax.axis_index("wide")
    everywhere = ("section", "wide", "fc")
    maps = [map_p2, map_p3, map_p4, map_p5]
    channels = map_p2.shape[3]
    height = map_p2.shape[1] * n_section
    width = map_p2.shape[2]
    rows_dev = boxes.shape[0]
    rows_own = rows_dev // (n_section * n_fc)
    held = first_weight.shape[1]
    classes_out = out_weight.shape[1]
    place = section.astype(jnp.int32).reshape(1)

    ring = n_wide == 8
    line = n_wide // 2
    rows_tall = out_weight.shape[0]
    rows_fc = n_section * rows_own
    half_held = held // 2
    lanes = first_weight.shape[0]

    place = jnp.stack([section, fc]).astype(jnp.int32)

    turned = turn_weight(
        counts, first_weight.T, sampled, second_weight.T, out_weight, hidden_bias
    )
    slot_parts = (counts, boxes, levels, classes, sampled, targets)
    turned, maps, slot_parts = together(turned, maps, slot_parts)
    if ring:
        places = ring_order(wide, line)
        small_at = [0, 1, 3, 4, 2, 5, 7, 6]
        order = jnp.stack(
            places
            + swap_order(wide, line)
            + [places[at] for at in small_at]
            + [section, fc, (section * n_wide + wide) * n_fc + fc]
        ).astype(jnp.int32)
        blocks = n_wide
        straight = [turned, line_step(turned, n_wide)]
        crossed = [pair_swap(turned, n_wide)]
        last_small = line_step(turned[:, lanes:], n_wide, -1)
    else:
        zero = jnp.zeros_like(section)
        order = jnp.stack([zero, zero, zero, section, fc, zero]).astype(jnp.int32)
        blocks = 1
    half_own = jnp.concatenate([level_map.reshape(-1, channels) for level_map in maps], axis=0)
    half_other = swap(half_own, "section")
    *parameters, slots = plan(place, *slot_parts, n_fc * rows_own, height, width)
    table = build_table(place, half_own, half_other, height, width)

    crops_mine = crop_forward(parameters, table, 0, rows_own)
    if ring:
        straight[1], crossed[0], last_small, table, crops_mine = together(
            straight[1], crossed[0], last_small, table, crops_mine
        )
        small_of = lambda piece: piece[:, lanes:]
        small_a = jnp.concatenate(
            [small_of(straight[0]), small_of(straight[1]), last_small, small_of(crossed[0])], axis=0
        )
        straight.append(line_step(straight[1], n_wide))
        crossed.append(pair_swap(straight[1], n_wide))
        last_crossed = pair_swap(last_small, n_wide)
        passed_a = swap(small_a, "fc")
    passed_mine = swap(crops_mine, "section")
    crops_theirs = crop_forward(parameters, table, rows_own, rows_own)

    if ring:
        straight[2], crossed, last_crossed, passed_mine, crops_theirs, small_a, passed_a = together(
            straight[2], crossed, last_crossed, passed_mine, crops_theirs, small_a, passed_a
        )
        straight.append(line_step(straight[2], n_wide))
        crossed.append(pair_swap(straight[2], n_wide))
        small_b = jnp.concatenate(
            [small_of(straight[2]), small_of(crossed[1]), last_crossed], axis=0
        )
        passed_b = swap(small_b, "fc")
        passed_theirs = swap(crops_theirs, "section")
        weight_of = lambda piece: piece[:, :lanes]
        early_weight = jnp.concatenate(
            [weight_of(piece) for piece in straight[:3] + crossed[:2]], axis=0
        )
        inputs_all = jnp.concatenate([crops_mine, passed_mine, crops_theirs, passed_theirs], axis=0)
        early = dot_last(early_weight, inputs_all)
        early, early_passed = early[:, :rows_fc], swap(early[:, rows_fc:].astype(BF16), "fc")
        straight[3], crossed[2], inputs_all, early, early_passed, small_b, passed_b = together(
            straight[3], crossed[2], inputs_all, early, early_passed, small_b, passed_b
        )
        tail = [
            pair_swap(straight[3][:half_held, :lanes], n_wide),
            line_step(crossed[2][half_held:, :lanes], n_wide),
        ]
        small_c = small_of(crossed[2])
        late = dot_last(
            jnp.concatenate([weight_of(straight[3]), weight_of(crossed[2])], axis=0), inputs_all
        )
        late, late_passed = late[:, :rows_fc], late[:, rows_fc:].astype(BF16)
        both = swap(
            jnp.concatenate([late_passed, small_c.reshape(-1, late_passed.shape[1])], axis=0), "fc"
        )
        groups = [[small, passed, swap(small, "section"), swap(passed, "section")]
            for small, passed in ((small_a, passed_a), (small_b, passed_b))
        ]
        tail, early, late, both, groups = together(tail, early, late, both, groups)
        late_passed = both[: 2 * held]
        passed_c = both[2 * held :].reshape(small_c.shape)
        last = jnp.concatenate(tail, axis=0)
        end_passed = swap(dot_last(last, inputs_all[rows_fc:]).astype(BF16), "fc")
        groups.append([small_c, passed_c, swap(small_c, "section"), swap(passed_c, "section")])
        small_weights = assemble(blocks, order, groups)
        end_passed, small_weights = together(end_passed, small_weights)
        w_second_turned, w_second, w_out, w_out_turned = small_weights
        end = dot_last(last, inputs_all[:rows_fc]) + end_passed.astype(F32)
        early = early + early_passed.astype(F32)
        late = late + late_passed.astype(F32)
        cut = (line - 1) * held
        pre = jnp.concatenate([early[:cut], late[:held], early[cut:], late[held:], end], axis=0)
        pieces = straight + crossed + [last]
    else:
        passed_theirs = swap(crops_theirs, "section")
        inputs_all = jnp.concatenate([crops_mine, passed_mine, crops_theirs, passed_theirs], axis=0)
        pieces = [lax.all_gather(turned[:, :lanes], "wide", axis=0, tiled=True)]
        pre = dot_last(pieces[0], inputs_all)
        pre = pre[:, :rows_fc] + swap(pre[:, rows_fc:], "fc")
        small = lax.all_gather(turned[:, lanes:], everywhere, axis=0, tiled=True)
        small = small.reshape(-1, n_fc, held, turned.shape[1] - lanes)
        w_second_turned = jnp.transpose(
            small[..., : second_weight.shape[0]], (1, 0, 2, 3)
        ).reshape(n_fc, -1, second_weight.shape[0])
        w_second = jnp.transpose(w_second_turned, (0, 2, 1)).reshape(
            -1, w_second_turned.shape[1]
        )
        w_out = small[..., second_weight.shape[0] :].reshape(-1, 2, rows_tall, PADDED // 2)
        w_out = jnp.transpose(w_out, (0, 2, 1, 3)).reshape(-1, PADDED)
        w_out_turned = w_out.T
    pre_own = pre[:, :rows_own]
    pre_other = swap(pre[:, rows_own:], "section")

    grad_own, grad_other, act_first, act_second, grad_second, grad_logits, losses, total = middle(
        blocks,
        n_wide,
        order,
        pre_own,
        pre_other,
        w_second_turned,
        w_second,
        w_out_turned,
        w_out,
        jnp.pad(out_bias, (0, PADDED - classes_out))[:, None],
        slots,
    )
    grad_passed = swap(grad_other, "section")
    grad_passed, grad_own, act_first = together(grad_passed, grad_own, act_first)
    grad_mine = jnp.concatenate([grad_own, grad_passed], axis=1)
    rate = 0.15 * math.sqrt(rows_dev * n_wide)
    back = lambda sent: swap(sent, "section")

    if ring:
        def all_slots(parts):
            mine = jnp.concatenate([grad_mine[at * held : (at + 1) * held] for at in parts], axis=0)
            return jnp.concatenate([mine, swap(mine, "fc")], axis=1)

        def block(values, at):
            return values[at * held : (at + 1) * held]

        rest_at = [0, 2, 3, line, line + 2, line + 3]
        first_grads = all_slots([1, line + 1])
        terms_own, terms_other, bias_terms = small_grads(
            blocks, True, order, act_first, act_second, grad_second, grad_own, grad_other, grad_logits, losses
        )
        first_grads, terms_own, terms_other = together(first_grads, terms_own, terms_other)
        first_terms = dot(first_grads, inputs_all).astype(BF16)
        rest_grads = all_slots(rest_at)
        first_terms, rest_grads, terms_other = together(first_terms, rest_grads, terms_other)
        moving, cross = block(first_terms, 0), block(first_terms, 1)
        tail = line_step(cross[half_held:], n_wide)
        head = pair_swap(cross[:half_held], n_wide)
        small = swap(terms_other, "section")
        rest = dot(rest_grads, inputs_all).astype(BF16)
        small = add(terms_own, small)
        rest, small, first_grads, rest_grads = together(rest, small, first_grads, rest_grads)
        small_passed = swap(small[1], "fc")
        grad_all = jnp.concatenate(
            [
                block(rest_grads, 0),
                first_grads[:held],
                rest_grads[held : 3 * held],
                block(rest_grads, 3),
                first_grads[held:],
                rest_grads[4 * held :],
            ],
            axis=0,
        )
        parts = [rows_own // 4] * 4
        keep_mine, *sent = input_grad(
            grad_all.T, pieces, [rows_own] + parts + [rows_own] + parts, lanes
        )
        keep_theirs = sent.pop(4)
        tail, head, rest, keep_mine, keep_theirs, sent = together(
            tail, head, rest, keep_mine, keep_theirs, sent
        )

        moving, cross = join(moving, head, block(rest, 4), tail)
        moving, cross, sent = together(moving, cross, sent)
        cross = pair_swap(cross, n_wide)
        moving = line_step(moving, n_wide)
        back_mine = jnp.concatenate([back(part) for part in sent[:4]], axis=0)
        before = crop_backward(place, parameters, keep_mine, back_mine, 0, height, width)
        back_theirs = [back(part) for part in sent[4:]]
        moving, cross, rest, before, keep_theirs, back_theirs, small_passed = together(
            moving, cross, rest, before, keep_theirs, back_theirs, small_passed
        )

        moving = add(block(rest, 1), cross, moving)
        moving, before = together(moving, before)
        moving = line_step(moving, n_wide)
        cross = pair_swap(block(rest, 5), n_wide)
        back_theirs = jnp.concatenate(back_theirs, axis=0)
        map_own, map_other = crop_backward(
            place, parameters, keep_theirs, back_theirs, rows_own, height, width, before
        )
        small = add(small[0], small_passed)
        moving, cross, rest, small, map_own, map_other = together(
            moving, cross, rest, small, map_own, map_other
        )

        moving = add(block(rest, 2), cross, moving)
        moving, map_other = together(moving, map_other)
        moving = line_step(moving, n_wide)
        cut = small.shape[0] // 2
        cross = pair_swap(block(rest, 3), n_wide)
        small_passed = pair_swap(small[cut:], n_wide)
        map_grads = map_sum(map_own, swap(map_other, "section"), maps)
        small_passed, map_grads = together(small_passed, map_grads)
        small = add(small[:cut], small_passed)
        small_terms = [small[:held]] + [
            line_swap(small[bits * held : (bits + 1) * held], n_wide, bits)
            for bits in range(1, line)
        ]
        moving, cross, map_grads = together(moving, cross, map_grads)
        small_out = renew_small(
            small_terms,
            (
                (second_weight.T, second_moment.T, second_average.T),
                (out_weight, out_moment, out_average),
                (hidden_bias, hidden_moment, hidden_average),
                (out_bias[None], bias_moment[None], bias_average[None]),
            ),
            rate,
        )
        first_sums = [block(rest, 0), cross, moving]
    else:
        grad_all = jnp.concatenate([grad_mine, swap(grad_mine, "fc")], axis=1)
        first_sums = [
            lax.psum_scatter(
                dot(grad_all, inputs_all).astype(BF16), "wide", scatter_dimension=0, tiled=True
            )
        ]
        keep_mine, send_mine, keep_theirs, send_theirs = input_grad(
            grad_all.T, pieces, [rows_own] * 4, lanes
        )
        before = crop_backward(place, parameters, keep_mine, back(send_mine), 0, height, width)
        map_own, map_other = crop_backward(
            place, parameters, keep_theirs, back(send_theirs), rows_own, height, width, before
        )
        map_grads = map_sum(map_own, swap(map_other, "section"), maps)
        terms_own, terms_other, bias_terms = small_grads(
            blocks, False, order, act_first, act_second, grad_second, grad_own, grad_other, grad_logits, losses
        )
        terms = jnp.stack(
            [jnp.where(section == at, terms_own, terms_other) for at in range(n_section)]
        )
        terms = jnp.where(fc == 0, terms, terms[:, ::-1])
        terms = jnp.transpose(split_tall(terms, n_wide), (0, 2, 1, 3, 4))
        small_sum = lax.psum_scatter(
            terms.reshape(-1, terms.shape[-1]), everywhere, scatter_dimension=0, tiled=True
        ).astype(F32)
    first_out = renew_first(first_sums, first_weight.T, first_moment.T, first_average.T, rate)
    if ring:
        *small_out, loss_sum = small_out
        loss_sum = loss_sum[0, 0]
        second_out = [value.T for value in small_out[:3]]
        out_out, hidden_out = small_out[3:6], small_out[6:9]
        bias_out = [value[0] for value in small_out[9:]]
    else:
        second_sum = small_sum[:, : second_weight.shape[0]]
        tall_sum = small_sum[:, second_weight.shape[0] :]
        tall_sum = jnp.concatenate([tall_sum[:rows_tall], tall_sum[rows_tall:]], axis=1)
        vector = jnp.concatenate([bias_terms[:classes_out, 0], jnp.sum(losses).reshape(1)])
        vector = lax.psum(vector, everywhere)
        loss_sum = vector[classes_out]
        second_out = renew(second_weight, second_moment, second_average, second_sum.T, rate)
        out_out = renew(out_weight, out_moment, out_average, tall_sum[:, :classes_out], rate)
        hidden_out = renew(
            hidden_bias,
            hidden_moment,
            hidden_average,
            tall_sum[:, classes_out : classes_out + 2],
            rate,
        )
        bias_out = renew(out_bias, bias_moment, bias_average, vector[:classes_out], 4.0)
    return (
        loss_sum,
        total[0, 0],
        map_grads[0],
        map_grads[1],
        map_grads[2],
        map_grads[3],
        first_out[0].T,
        first_out[1].T,
        first_out[2].T,
        *second_out,
        *out_out,
        *hidden_out,
        *bias_out,
    )


def solution(mesh):
    maps = P("wide", "section", None, "fc")
    wide_weight = P("fc", ("section", "wide"))
    tall_weight = P(("section", "wide", "fc"), None)
    in_specs = (
        (maps,) * 4
        + (P("wide", None), P("wide"), P("wide"), P("wide"), P("wide"), P("wide", None))
        + (wide_weight, wide_weight, tall_weight, tall_weight, P()) * 3
    )
    out_specs = (
        (P(), P())
        + (maps,) * 4
        + (wide_weight,) * 6
        + (tall_weight,) * 6
        + (P(),) * 3
    )
    return jax.shard_map(body, mesh=mesh, in_specs=in_specs, out_specs=out_specs, check_vma=False)
```

```python
import functools
import math

import jax
import jax.numpy as jnp
from jax import lax
from jax.experimental import pallas as pl
from jax.experimental.pallas import tpu as pltpu
from jax.sharding import PartitionSpec as P

CLASSES = 81
BINS = 7
CELLS = BINS * BINS
WINDOW = 24
WINDOWS = (24, 16, 8)
GROUP = 16
CHAINS = 4
SETS = 2
PADDED = 512
WIDTH = 5 * CLASSES - 4
BIAS_AT = 416
LOSS_AT = 448
MOMENTUM = 0.9
AVERAGE = 0.7
DECAY = 0.0001
SMOOTH = 0.5

F32 = jnp.float32
BF16 = jnp.bfloat16


def smem():
    return pl.BlockSpec(memory_space=pltpu.SMEM)


def vmem():
    return pl.BlockSpec(memory_space=pltpu.VMEM)


def lasting(microseconds):
    return pl.CostEstimate(
        flops=0, bytes_accessed=int(microseconds * 1e3), transcendentals=0
    )


def limits(mebibytes):
    return pltpu.CompilerParams(vmem_limit_bytes=mebibytes * 2**20)


def level_plan(height, width):
    shapes = [(height >> depth, width >> depth) for depth in range(4)]
    strides = [max(rows, WINDOW) for rows, cols in shapes]
    bases = [0]
    for depth in range(4):
        bases.append(bases[-1] + strides[depth] * shapes[depth][1])
    total = -(-(bases[-1] + 2 * WINDOW) // GROUP) * GROUP
    return shapes, strides, bases[:4], total


def half_starts(shapes):
    starts = [0]
    for rows, cols in shapes:
        starts.append(starts[-1] + rows // 2 * cols)
    return starts


def table_kernel(height, width, place, own, other, table):
    shapes, strides, bases, total = level_plan(height, width)
    starts = half_starts(shapes)
    table[...] = jnp.zeros_like(table)

    def fill(source, bottom):
        for depth, (rows, cols) in enumerate(shapes):
            half = rows // 2

            def column(x, carry, depth=depth, half=half, cols=cols):
                cells = source[pl.ds(starts[depth] + x, half, stride=cols), :]
                table[pl.ds(bases[depth] + x * strides[depth] + bottom * half, half), :] = cells
                return carry

            lax.fori_loop(0, cols, column, 0, unroll=4)

    bottom = place[0]
    fill(own, bottom)
    fill(other, 1 - bottom)


def build_table(place, own, other, height, width):
    total = level_plan(height, width)[3]
    return pl.pallas_call(
        functools.partial(table_kernel, height, width),
        out_shape=jax.ShapeDtypeStruct((total, own.shape[1]), F32),
        in_specs=[smem(), vmem(), vmem()],
        out_specs=vmem(),
        compiler_params=limits(52),
        cost_estimate=lasting(5.0),
        name="build_table",
    )(place, own, other)


def plan_kernel(
    height,
    width,
    place,
    counts,
    boxes,
    levels,
    classes,
    sampled,
    targets,
    address,
    weight,
    row_values,
    stride,
    slots,
    features,
):
    shapes, strides, bases, total = level_plan(height, width)
    count = boxes.shape[1]
    own = address.shape[1]
    share = own // 2
    section, fc = place[0], place[1]
    lane = lax.broadcasted_iota(jnp.int32, (1, count), 1)
    live = (lane < counts[0]) & (sampled[...] > 0)
    key = (jnp.where(live, levels[...], 4) * count + lane).astype(F32)
    across = jnp.broadcast_to(key, (128, count))
    down = jnp.transpose(across)
    before = jnp.zeros((count, 128), F32)
    for start in range(0, count, 128):
        before = before + jnp.where(key[:, start : start + 128] < down, 1.0, 0.0)
    rank = jnp.sum(before, axis=1, keepdims=True).astype(jnp.int32)
    seat = rank // 2
    side = jnp.where(seat % 2 == fc, 0, share)
    seat = jnp.where(rank % 2 == section, seat // 2 + side, -1)
    deal = jnp.where(
        jnp.broadcast_to(seat, (count, own)) == lax.broadcasted_iota(jnp.int32, (count, own), 1),
        1.0,
        0.0,
    )
    features[...] = jnp.zeros_like(features)
    features[0:4, :] = boxes[...]
    features[4:8, :] = targets[...]
    features[8:9, :] = levels[...].astype(F32)
    features[9:10, :] = classes[...].astype(F32)
    features[10:11, :] = jnp.where(live, 1.0, 0.0)
    dealt = jnp.dot(
        features[...], deal, preferred_element_type=F32, precision=lax.Precision.HIGHEST
    )
    slots[...] = jnp.zeros_like(slots)
    slots[0:1, :] = dealt[10:11, 0:share]
    slots[2:3, :] = dealt[9:10, 0:share]
    slots[3:7, :] = dealt[4:8, 0:share]
    level = (dealt[8:9, :] + 0.5).astype(jnp.int32)

    def choose(values, kind):
        out = jnp.full(level.shape, values[3], kind)
        for depth in range(3):
            out = jnp.where(level == depth, jnp.asarray(values[depth], kind), out)
        return out

    reach_y = choose([h - 1 for h, w in shapes], F32)
    reach_x = choose([w - 1 for h, w in shapes], F32)
    step = choose(strides, jnp.int32)
    base = choose(bases, jnp.int32)
    top = (dealt[0:1, :] - 0.25 * dealt[2:3, :]) * reach_y
    length_y = 0.5 * dealt[2:3, :] * reach_y
    left = (dealt[1:2, :] - 0.25 * dealt[3:4, :]) * reach_x
    length_x = 0.5 * dealt[3:4, :] * reach_x
    first = jnp.clip(jnp.floor(top + length_y * (0.25 / 7.0)), 0.0, reach_y - 1.0)
    start = base + first.astype(jnp.int32)
    for at in range(2 * BINS):
        points = left + length_x * ((at // 2 + (at % 2 + 0.5) * 0.5) / 7.0)
        lower = jnp.clip(jnp.floor(points), 0.0, reach_x - 1.0)
        address[at : at + 1, :] = start + lower.astype(jnp.int32) * step
        weight[at : at + 1, :] = points - lower
    for at, value in enumerate((top, length_y, first, reach_y - 1.0)):
        row_values[at : at + 1, :] = value
    stride[0:1, :] = step
    stride[1:2, :] = jnp.where(dealt[10:11, :] > 0.5, choose([3, 2, 1, 1], jnp.int32), 0)


def plan(place, counts, boxes, levels, classes, sampled, targets, own, height, width):
    whole = jax.ShapeDtypeStruct
    count = boxes.shape[0]
    return pl.pallas_call(
        functools.partial(plan_kernel, height, width),
        out_shape=(
            whole((2 * BINS, own), jnp.int32),
            whole((2 * BINS, own), F32),
            whole((4, own), F32),
            whole((2, own), jnp.int32),
            whole((8, own // 2), F32),
        ),
        in_specs=[smem()] * 2 + [vmem()] * 5,
        out_specs=(vmem(),) * 5,
        scratch_shapes=[pltpu.VMEM((16, count), F32)],
        compiler_params=limits(52),
        cost_estimate=lasting(3.0),
        name="plan",
    )(place, counts, boxes.T, levels[None], classes[None], sampled[None], targets.T)


def row_weights(values, index, offset):
    top, length, first, last = values
    total = None
    for place in (0.25, 0.75):
        points = top + length * ((index + place) / 7.0)
        lower = jnp.minimum(jnp.maximum(jnp.floor(points), 0.0), last)
        upper_weight = points - lower
        distance = offset - (lower - first)
        part = jnp.where(
            distance == 0.0, 1.0 - upper_weight, jnp.where(distance == 1.0, upper_weight, 0.0)
        )
        total = part if total is None else total + part
    return total * 0.25


def crop_kernel(rows, first, address, weight, row_values, stride, table, out, turned):
    def crops(window, step):
        depth = -(-BINS * window // 128) * 128
        lane = lax.broadcasted_iota(jnp.int32, (8, depth), 1)
        offset = (lane % window).astype(F32)
        index = lax.broadcasted_iota(jnp.int32, (8, depth), 0).astype(F32)
        inside = (
            lax.broadcasted_iota(jnp.int32, (8 * BINS, depth), 0) // 8
            == lax.broadcasted_iota(jnp.int32, (8 * BINS, depth), 1) // window
        )

        for part in range(GROUP):
            row = first + step * GROUP + part
            weights = row_weights([row_values[at, row] for at in range(4)], index, offset)
            left = jnp.where(inside, jnp.concatenate([weights] * BINS, axis=0), 0.0)
            step_x = stride[0, row]
            columns = []
            for k in range(BINS):
                total = None
                for m in range(2):
                    place = address[2 * k + m, row]
                    upper = weight[2 * k + m, row]
                    near = table[pl.ds(place, window), :]
                    far = table[pl.ds(place + step_x, window), :]
                    value = near + upper * (far - near)
                    total = value if total is None else total + value
                columns.append(total)
            columns.append(jnp.zeros((depth - BINS * window, 128), F32))
            right = jnp.concatenate(columns, axis=0).astype(BF16)
            crop = jnp.dot(left.astype(BF16), right, preferred_element_type=F32)
            for k in range(BINS):
                turned[pl.ds(part + k * BINS * GROUP, BINS, stride=GROUP), :] = crop[
                    8 * k : 8 * k + BINS
                ]

    def group(step, carry):
        start = pl.multiple_of(step * GROUP, GROUP)
        eights = stride[1, first + step * GROUP]
        for window in WINDOWS:

            @pl.when(eights == window // 8)
            def live_slots(window=window):
                crops(window, step)

        @pl.when(eights > 0)
        def store():
            for cell in range(CELLS):
                out[pl.ds(start, GROUP), cell * 128 : (cell + 1) * 128] = turned[
                    cell * GROUP : (cell + 1) * GROUP, :
                ].astype(BF16)

        @pl.when(eights == 0)
        def dead_slots():
            out[pl.ds(start, GROUP), :] = jnp.zeros((GROUP, CELLS * 128), BF16)

        return carry

    lax.fori_loop(0, rows // GROUP, group, 0)


def crop_forward(parameters, table, first, rows):
    return pl.pallas_call(
        functools.partial(crop_kernel, rows, first),
        out_shape=jax.ShapeDtypeStruct((rows, CELLS * 128), BF16),
        in_specs=[smem()] * 4 + [vmem()],
        out_specs=vmem(),
        scratch_shapes=[pltpu.VMEM((CELLS * GROUP, 128), F32)],
        compiler_params=limits(52),
        cost_estimate=lasting(0.07 * rows),
        name="crop_forward",
    )(*parameters, table)


def spread_kernel(
    rows, first, height, width, last, parts, place, address, weight, row_values, stride, keep, *refs
):
    shapes, strides, bases, total = level_plan(height, width)
    starts = half_starts(shapes)
    passed_parts, refs = refs[:parts], refs[parts:]
    if last:
        before, own, other, passed, turned, half, *tables = refs
    else:
        out, passed, turned, *tables = refs
    size = rows // parts
    for at, part in enumerate(passed_parts):
        passed[at * size : (at + 1) * size, :] = part[...]
    for table in tables:
        table[...] = jnp.zeros_like(table)
    turned[pl.ds(CELLS * GROUP, GROUP), :] = jnp.zeros((GROUP, 128), F32)

    def spread(window, base, few):
        index = (lax.broadcasted_iota(jnp.int32, (window, 128), 1) % 8).astype(F32)
        offset = lax.broadcasted_iota(jnp.int32, (window, 128), 0).astype(F32)
        long_row = lax.broadcasted_iota(jnp.int32, (BINS * window, 128), 0)
        long_lane = lax.broadcasted_iota(jnp.int32, (BINS * window, 128), 1)
        inside = (long_row // window == long_lane // 8) & (long_lane % 8 < BINS)
        results = []
        for at in range(SETS * CHAINS):
            part = few * SETS * CHAINS + at
            row = base + at
            weights = row_weights([row_values[at, row] for at in range(4)], index, offset)
            left = jnp.where(inside, jnp.concatenate([weights] * BINS, axis=0), 0.0).astype(BF16)
            pieces = [
                turned[pl.ds(part + k * BINS * GROUP, 8, stride=GROUP), :] for k in range(BINS)
            ]
            pieces.append(jnp.zeros((128 - 8 * BINS, 128), F32))
            right = jnp.concatenate(pieces, axis=0).astype(BF16)
            results.append(jnp.dot(left, right, preferred_element_type=F32))
        for head in range(0, SETS * CHAINS, CHAINS):
            for k in range(BINS):
                for m in range(2):
                    for chain in range(CHAINS):
                        row = base + head + chain
                        table = tables[chain]
                        at = address[2 * k + m, row]
                        next_at = at + stride[0, row]
                        value = results[head + chain][k * window : (k + 1) * window]
                        upper = value * weight[2 * k + m, row]
                        near = table[pl.ds(at, window), :] + (value - upper)
                        far = table[pl.ds(next_at, window), :] + upper
                        table[pl.ds(at, window), :] = near
                        table[pl.ds(next_at, window), :] = far

    def group(step, carry):
        start = pl.multiple_of(step * GROUP, GROUP)

        @pl.when(stride[1, first + step * GROUP] > 0)
        def live_slots():
            for cell in range(CELLS):
                span = slice(cell * 128, (cell + 1) * 128)
                turned[cell * GROUP : (cell + 1) * GROUP, :] = keep[
                    pl.ds(start, GROUP), span
                ].astype(F32) + passed[pl.ds(start, GROUP), span].astype(F32)

            def some(few, carry):
                base = first + step * GROUP + few * SETS * CHAINS
                eights = stride[1, base]
                for window in WINDOWS:

                    @pl.when(eights == window // 8)
                    def one_window(window=window):
                        spread(window, base, few)

                return carry

            lax.fori_loop(0, GROUP // (SETS * CHAINS), some, 0)

        return carry

    lax.fori_loop(0, rows // GROUP, group, 0)
    result = tables[0] if last else out

    def summed(step, carry):
        span = pl.ds(pl.multiple_of(step * GROUP, GROUP), GROUP)
        value = tables[0][span, :]
        for table in tables[1:]:
            value = value + table[span, :]
        if last:
            value = value + before[span, :]
        result[span, :] = value
        return carry

    lax.fori_loop(0, total // GROUP, summed, 0)
    if not last:
        return

    def collect(target, bottom):
        for depth, (level_rows, cols) in enumerate(shapes):
            count = level_rows // 2

            def column(x, carry, depth=depth, count=count, cols=cols):
                cells = result[pl.ds(bases[depth] + x * strides[depth] + bottom * count, count), :]
                target[pl.ds(starts[depth] + x, count, stride=cols), :] = cells
                return carry

            lax.fori_loop(0, cols, column, 0, unroll=4)

    bottom = place[0]
    collect(own, bottom)
    collect(half, 1 - bottom)
    other[...] = half[...].astype(BF16)


def crop_backward(place, parameters, keep, passed, first, height, width, before=None):
    rows = keep.shape[0]
    shapes, strides, bases, total = level_plan(height, width)
    cells = half_starts(shapes)[-1]
    last = before is not None
    turned = pltpu.VMEM(((CELLS + 1) * GROUP, 128), F32)
    joined = pltpu.VMEM(keep.shape, BF16)
    tables = [pltpu.VMEM((total, 128), F32)] * CHAINS
    if last:
        out_shape = (
            jax.ShapeDtypeStruct((cells, 128), F32),
            jax.ShapeDtypeStruct((cells, 128), BF16),
        )
        scratch = [joined, turned, pltpu.VMEM((cells, 128), F32)] + tables
    else:
        out_shape = jax.ShapeDtypeStruct((total, 128), F32)
        scratch = [joined, turned] + tables
    return pl.pallas_call(
        functools.partial(spread_kernel, rows, first, height, width, last, len(passed)),
        out_shape=out_shape,
        in_specs=[smem()] * 5 + [vmem()] * ((2 if last else 1) + len(passed)),
        out_specs=(vmem(),) * 2 if last else vmem(),
        scratch_shapes=scratch,
        compiler_params=limits(52),
        cost_estimate=lasting(0.12 * rows),
        name="crop_backward",
    )(place, *parameters, keep, *passed, *([before] if last else []))


def natural_row(cell):
    k, i = divmod(cell, BINS)
    return i * BINS + k


def turn_kernel(
    counts, weight, sampled, second_far, out_far, bias_far, out, turned, tall, second, out_weight, hidden_bias, sems
):
    held, lanes = weight.shape
    depth = second.shape[1]
    rows = out_weight.shape[0]
    half = PADDED // 2
    copies = [
        pltpu.make_async_copy(source, target, sems.at[at])
        for at, (source, target) in enumerate(
            ((second_far, second), (out_far, out_weight), (bias_far, hidden_bias))
        )
    ]
    for copy in copies:
        copy.start()
    for tile in range(CELLS):
        turned[tile * 128 : (tile + 1) * 128, 0:held] = jnp.transpose(
            weight[:, tile * 128 : (tile + 1) * 128]
        )
    for cell in range(CELLS):
        block = turned[pl.ds(natural_row(cell), 128, stride=CELLS), :]
        out[:, cell * 128 : (cell + 1) * 128] = jnp.transpose(block)[0:held].astype(BF16)
    lane = lax.broadcasted_iota(jnp.int32, sampled.shape, 1)
    live = jnp.sum(
        jnp.where((lane < counts[0]) & (sampled[...] > 0), 1.0, 0.0), axis=1, keepdims=True
    )
    high = jnp.floor(live / 32.0)
    for copy in copies:
        copy.wait()
    same = lax.broadcasted_iota(jnp.int32, (rows, rows), 0) == lax.broadcasted_iota(
        jnp.int32, (rows, rows), 1
    )
    biases = [
        jnp.sum(jnp.where(same, hidden_bias[at : at + 1, :], 0.0), axis=1, keepdims=True)
        for at in range(2)
    ]
    tall[...] = jnp.zeros_like(tall)
    tall[:, 0:WIDTH] = out_weight[...]
    column = lax.broadcasted_iota(jnp.int32, (rows, 128), 1) + (PADDED - 128)
    value = tall[:, PADDED - 128 : PADDED]
    for at, part in enumerate(
        (*biases, high, live - 32.0 * high)
    ):
        value = jnp.where(column == WIDTH + at, part, value)
    tall[:, PADDED - 128 : PADDED] = value
    out[:, lanes : lanes + depth] = second[...].astype(BF16)
    out[:, lanes + depth : lanes + depth + half] = jnp.concatenate(
        [tall[:, 0:half], tall[:, half:PADDED]], axis=0
    ).astype(BF16)


def turn_weight(counts, weight, sampled, second, out_weight, hidden_bias):
    held, lanes = weight.shape
    return pl.pallas_call(
        turn_kernel,
        out_shape=jax.ShapeDtypeStruct((held, lanes + second.shape[1] + PADDED // 2), BF16),
        in_specs=[smem()] + [vmem()] * 2 + [pl.BlockSpec(memory_space=pl.ANY)] * 3,
        out_specs=vmem(),
        scratch_shapes=[
            pltpu.VMEM((lanes, 128), F32),
            pltpu.VMEM((out_weight.shape[0], PADDED), F32),
            pltpu.VMEM(second.shape, F32),
            pltpu.VMEM(out_weight.shape, F32),
            pltpu.VMEM(hidden_bias.T.shape, F32),
            pltpu.SemaphoreType.DMA((3,)),
        ],
        compiler_params=limits(52),
        cost_estimate=lasting(2.7),
        name="turn_weight",
    )(counts, weight, sampled[None], second, out_weight, hidden_bias.T)


def renew(weight, moment, average, grad, rate):
    step_value = grad + DECAY * weight
    moment_new = MOMENTUM * moment + step_value
    weight_new = weight - rate * (step_value + MOMENTUM * moment_new)
    average_new = AVERAGE * average + (1.0 - AVERAGE) * weight_new
    return (weight_new, moment_new, average_new)


def renew_kernel(rate, count, *refs):
    terms = refs[:count]
    kept = refs[count : count + 3]
    news = refs[count + 3 : count + 6]
    turned, *places = refs[count + 6 : count + 13]
    sems = refs[count + 13]
    held, lanes = terms[0].shape
    arrive = [
        pltpu.make_async_copy(kept[at], places[at], sems.at[at, 0]) for at in range(3)
    ]
    for copy in arrive:
        copy.start()
    for cell in range(CELLS):
        span = slice(cell * 128, (cell + 1) * 128)
        grad = terms[0][:, span].astype(F32)
        for term in terms[1:]:
            grad = grad + term[:, span].astype(F32)
        turned[pl.ds(natural_row(cell), 128, stride=CELLS), 0:held] = jnp.transpose(grad)
    for copy in arrive:
        copy.wait()
    leave = []
    for part in range(BINS):
        for tile in range(part * BINS, (part + 1) * BINS):
            span = slice(tile * 128, (tile + 1) * 128)
            grad = jnp.transpose(turned[span, :])[0:held]
            values = renew(*[place[:, span] for place in places[:3]], grad, rate)
            for at in range(3):
                places[3 + at][:, span] = values[at]
        span = pl.ds(part * BINS * 128, BINS * 128)
        for at in range(3):
            copy = pltpu.make_async_copy(
                places[3 + at].at[:, span], news[at].at[:, span], sems.at[at, 1 + part]
            )
            copy.start()
            leave.append(copy)
    for copy in leave:
        copy.wait()


def renew_first(terms, weight, moment, average, rate):
    held, lanes = weight.shape
    anywhere = pl.BlockSpec(memory_space=pl.ANY)
    return pl.pallas_call(
        functools.partial(renew_kernel, rate, len(terms)),
        out_shape=(jax.ShapeDtypeStruct(weight.shape, F32),) * 3,
        in_specs=[vmem()] * len(terms) + [anywhere] * 3,
        out_specs=(anywhere,) * 3,
        scratch_shapes=[pltpu.VMEM((lanes, 128), F32)]
        + [pltpu.VMEM((held, lanes), F32)] * 6
        + [pltpu.SemaphoreType.DMA((3, 1 + BINS))],
        compiler_params=limits(52),
        cost_estimate=lasting(6.5),
        name="renew_first",
    )(*terms, weight, moment, average)


def renew_small_kernel(rate, count, *refs):
    terms = refs[:count]
    second, tall, hidden, bias = (refs[count + 3 * at : count + 3 * at + 3] for at in range(4))
    second_new, tall_new, hidden_new, bias_new = (
        refs[count + 12 + 3 * at : count + 15 + 3 * at] for at in range(4)
    )
    loss = refs[count + 24]
    rows = tall[0].shape[0]
    depth = second[0].shape[1]
    half = PADDED // 2
    total = terms[0][...].astype(F32)
    for term in terms[1:]:
        total = total + term[...].astype(F32)

    def give(targets, sources, grad, rate):
        for target, value in zip(targets, renew(*[ref[...] for ref in sources], grad, rate)):
            target[...] = value

    give(second_new, second, total[:, :depth], rate)
    sums = jnp.concatenate([total[:rows, depth:], total[rows:, depth:]], axis=1)
    give(tall_new, tall, sums[:, :WIDTH], rate)
    give(hidden_new, hidden, sums[:, WIDTH : WIDTH + 2], rate)
    spare = sums[:, PADDED - 128 : PADDED]
    start = BIAS_AT - (PADDED - 128)
    source = lax.broadcasted_iota(jnp.int32, (128, PADDED), 0)
    target = lax.broadcasted_iota(jnp.int32, (128, PADDED), 1)
    spread = jnp.dot(
        spare,
        jnp.where(source == start + target % 16, 1.0, 0.0),
        preferred_element_type=F32,
        precision=lax.Precision.HIGHEST,
    )
    row = lax.broadcasted_iota(jnp.int32, (rows, PADDED), 0)
    column = lax.broadcasted_iota(jnp.int32, (rows, PADDED), 1)
    line = jnp.sum(jnp.where(column // 16 == row, spread, 0.0), axis=0, keepdims=True)
    give(bias_new, bias, line[:, :WIDTH], 4.0)
    lane = lax.broadcasted_iota(jnp.int32, (rows, 128), 1) + (PADDED - 128)
    losses = jnp.where((lane >= LOSS_AT) & (lane < LOSS_AT + 3), spare, 0.0)
    loss[...] = jnp.sum(jnp.sum(losses, axis=1, keepdims=True), axis=0, keepdims=True)


def renew_small(terms, states, rate):
    states = [value for group in states for value in group]
    return pl.pallas_call(
        functools.partial(renew_small_kernel, rate, len(terms)),
        out_shape=tuple(jax.ShapeDtypeStruct(value.shape, F32) for value in states)
        + (jax.ShapeDtypeStruct((1, 1), F32),),
        in_specs=[vmem()] * (len(terms) + len(states)),
        out_specs=(vmem(),) * (len(states) + 1),
        compiler_params=limits(52),
        cost_estimate=lasting(2.0),
        name="renew_small",
    )(*terms, *states)


def map_sum_kernel(parts, own, *refs):
    passed, outs = refs[:parts], refs[parts:]
    ends = []
    for part in passed:
        ends.append((ends[-1] if ends else 0) + part.shape[0])
    start = 0
    for out in outs:
        end = start + out.shape[0]
        first = 0
        for part, last in zip(passed, ends):
            low, high = max(start, first), min(end, last)
            if low < high:
                out[low - start : high - start, :] = own[low:high, :] + part[
                    low - first : high - first, :
                ].astype(F32)
            first = last
        start = end


def map_sum(own, passed, maps):
    sizes = [level_map.shape[1] * level_map.shape[2] for level_map in maps]
    grads = pl.pallas_call(
        functools.partial(map_sum_kernel, len(passed)),
        out_shape=tuple(jax.ShapeDtypeStruct((size, own.shape[1]), F32) for size in sizes),
        in_specs=[vmem()] * (1 + len(passed)),
        out_specs=(vmem(),) * len(sizes),
        compiler_params=limits(52),
        cost_estimate=lasting(2.0),
        name="map_sum",
    )(own, *passed)
    return [grad.reshape(level_map.shape) for grad, level_map in zip(grads, maps)]


def gelu_parts(value):
    root = math.sqrt(2.0 / math.pi)
    square = value * value
    bend = jnp.tanh(root * (value + 0.044715 * square * value))
    half = 0.5 * (1.0 + bend)
    slope = half + 0.5 * value * (1.0 - bend * bend) * (
        root * (1.0 + 3.0 * 0.044715 * square)
    )
    return value * half, slope


def dot(left, right):
    return jnp.dot(left, right, preferred_element_type=F32)


def dot_last(left, right):
    return lax.dot_general(left, right, (((1,), (1,)), ((), ())), preferred_element_type=F32)


def middle_kernel(
    blocks,
    images,
    parts,
    order,
    *refs,
):
    pre_parts, refs = refs[: 2 * parts], refs[2 * parts :]
    middle_of(blocks, images, order, pre_parts, *refs)


def middle_of(
    blocks,
    images,
    order,
    pre_parts,
    second_turned_far,
    second_far,
    out_turned_far,
    out_weight,
    out_bias,
    slots,
    grad_own,
    grad_other,
    act_first,
    act_second,
    grad_second,
    grad_logits,
    losses,
    live_total,
    pre_first,
    slope_first,
    slope_second,
    grad_first,
    second_turned,
    second,
    out_turned,
    sems,
):
    copies = [
        pltpu.make_async_copy(source, target, sems.at[at])
        for at, (source, target) in enumerate(
            (
                (second_turned_far, second_turned),
                (out_turned_far, out_turned),
                (second_far, second),
            )
        )
    ]
    for copy in copies:
        copy.start()
    hidden, rows = pre_first.shape
    half = hidden // 2
    size = half // blocks
    own_start = order[3 * blocks] * half
    other_start = (1 - order[3 * blocks]) * half
    parts = len(pre_parts) // 2
    block = 0
    for own, other in zip(pre_parts[:parts], pre_parts[parts:]):
        for row in range(0, own.shape[0], size):
            at = pl.multiple_of(own_start + order[3 * blocks + 3 + block] * size, size)
            pre_first[pl.ds(at, size), :] = own[row : row + size, :]
            at = pl.multiple_of(other_start + order[3 * blocks + 3 + block] * size, size)
            pre_first[pl.ds(at, size), :] = other[row : row + size, :]
            block += 1
    spare = out_weight[:, PADDED - 128 : PADDED].astype(F32)
    at = WIDTH - (PADDED - 128)
    counted = 32.0 * spare[:, at + 2 : at + 3] + spare[:, at + 3 : at + 4]
    slots_total = jnp.sum(counted, axis=0, keepdims=True) * (images / hidden)
    live_total[...] = slots_total
    act, slope = gelu_parts(pre_first[...] + spare[:, at : at + 1])
    slope_first[...] = slope
    act_first[...] = act.astype(BF16)
    copies[0].wait()
    pre_second = (
        dot(second_turned[0], act_first[0:half, :])
        + dot(second_turned[1], act_first[half:hidden, :])
        + spare[:, at + 1 : at + 2]
    )
    act, slope = gelu_parts(pre_second)
    slope_second[...] = slope
    act_second[...] = act.astype(BF16)
    copies[1].wait()
    logits = dot(out_turned[...], act_second[...]) + out_bias[...]

    row = lax.broadcasted_iota(jnp.int32, logits.shape, 0)
    live = slots[0:1, :]
    scale = 1.0 / slots_total
    chosen = slots[2:3, :].astype(jnp.int32)
    foreground = jnp.where(chosen > 0, 1.0, 0.0)
    is_score = row < CLASSES
    top = jnp.max(jnp.where(is_score, logits, -jnp.inf), axis=0, keepdims=True)
    power = jnp.where(is_score, jnp.exp(logits - top), 0.0)
    total = jnp.sum(power, axis=0, keepdims=True)
    matches = row == chosen
    picked = jnp.sum(jnp.where(matches, logits, 0.0), axis=0, keepdims=True)
    value = jnp.log(total) + top - picked
    grad = power / total - jnp.where(matches, 1.0, 0.0)
    delta_row = CLASSES + 4 * (chosen - 1)
    smooth_total = jnp.zeros_like(live)
    for part in range(4):
        mine = (row == delta_row + part) & (chosen > 0)
        offset = jnp.sum(jnp.where(mine, logits, 0.0), axis=0, keepdims=True) - slots[
            3 + part : 4 + part, :
        ]
        size_of = jnp.abs(offset)
        near = size_of < SMOOTH
        smooth_total = smooth_total + jnp.where(
            near, 0.5 * offset * offset / SMOOTH, size_of - 0.5 * SMOOTH
        )
        slope = jnp.where(near, offset / SMOOTH, jnp.where(offset > 0.0, 1.0, -1.0))
        grad = jnp.where(mine, slope, grad)
    losses[...] = live * (value + foreground * smooth_total)
    grad_logits[...] = (grad * (live * scale)).astype(BF16)
    grad_second[...] = (dot(out_weight[...], grad_logits[...]) * slope_second[...]).astype(BF16)
    copies[2].wait()
    grad_first[...] = dot(second[...], grad_second[...]) * slope_first[...]
    for block in range(blocks):
        span = slice(block * size, (block + 1) * size)
        at = pl.multiple_of(own_start + order[block] * size, size)
        grad_own[span, :] = grad_first[pl.ds(at, size), :].astype(BF16)
        at = pl.multiple_of(other_start + order[block] * size, size)
        grad_other[span, :] = grad_first[pl.ds(at, size), :].astype(BF16)


def middle(blocks, images, order, pre_own, pre_other, *values):
    half, rows = (sum(part.shape[0] for part in pre_own), pre_own[0].shape[1])
    hidden = 2 * half
    low = lambda *shape: jax.ShapeDtypeStruct(shape, BF16)
    return pl.pallas_call(
        functools.partial(middle_kernel, blocks, images, len(pre_own)),
        out_shape=(
            low(half, rows),
            low(half, rows),
            low(hidden, rows),
            low(hidden, rows),
            low(hidden, rows),
            low(PADDED, rows),
            jax.ShapeDtypeStruct((1, rows), F32),
            jax.ShapeDtypeStruct((1, 1), F32),
        ),
        in_specs=[smem()]
        + [vmem()] * (2 * len(pre_own))
        + [pl.BlockSpec(memory_space=pl.ANY)] * 3
        + [vmem()] * (len(values) - 3),
        out_specs=(vmem(),) * 8,
        scratch_shapes=[pltpu.VMEM((hidden, rows), F32)] * 4
        + [pltpu.VMEM(value.shape, BF16) for value in values[:3]]
        + [pltpu.SemaphoreType.DMA((3,))],
        compiler_params=limits(52),
        cost_estimate=lasting(6.5),
        name="middle",
    )(order, *pre_own, *pre_other, *values)


def small_grads_kernel(
    blocks,
    parts,
    order,
    act_first,
    act_second,
    grad_second,
    grad_own,
    grad_other,
    grad_logits,
    losses,
    own,
    other,
    bias_out,
    second_sum,
    out_sum,
):
    hidden, rows = act_first.shape
    half = hidden // 2
    size = half // blocks
    section, fc, device = order[3 * blocks], order[3 * blocks + 1], order[3 * blocks + 2]
    for side in range(2):
        second_sum[side] = dot_last(
            grad_second[...], act_first[side * half : (side + 1) * half, :]
        ).astype(BF16)
    column = lax.broadcasted_iota(jnp.int32, (rows, PADDED), 1)
    value = dot_last(act_second[...], grad_logits[...])
    value = value + dot(grad_second[...], jnp.where(column == WIDTH + 1, 1.0, 0.0).astype(BF16))
    out_sum[...] = value
    ones = jnp.where(column == WIDTH, 1.0, 0.0).astype(BF16)
    for block in range(blocks):
        span = slice(block * size, (block + 1) * size)
        for values, where in ((grad_own, section), (grad_other, 1 - section)):
            at = pl.ds(pl.multiple_of(where * half + order[block] * size, size), size)
            out_sum[at, :] = out_sum[at, :] + dot(values[span, :], ones)
    bias = jnp.sum(grad_logits[...].astype(F32), axis=1, keepdims=True)
    bias_out[...] = bias
    part = size // 2
    if parts:
        tile = slice(PADDED - 128, PADDED)
        source = lax.broadcasted_iota(jnp.int32, (PADDED, 128), 0)
        target = lax.broadcasted_iota(jnp.int32, (PADDED, 128), 1) + (PADDED - 128)
        spread = jnp.where(target == BIAS_AT + source % 16, bias, 0.0).astype(BF16)
        row = lax.broadcasted_iota(jnp.int32, (hidden, PADDED), 0) % part
        pick = jnp.where(
            row == lax.broadcasted_iota(jnp.int32, (hidden, PADDED), 1) // 16, 1.0, 0.0
        ).astype(BF16)
        value = out_sum[:, tile] + dot(pick, spread)
        row = lax.broadcasted_iota(jnp.int32, (hidden, 128), 0) % part
        column = lax.broadcasted_iota(jnp.int32, (hidden, 128), 1) + (PADDED - 128)
        rest = jnp.sum(losses[...], axis=1, keepdims=True)
        for place in range(3):
            now = rest.astype(BF16).astype(F32)
            value = jnp.where((row == device) & (column == LOSS_AT + place), now, value)
            rest = rest - now
        out_sum[:, tile] = value
    for target, where in ((own, section), (other, 1 - section)):
        for near in range(2):
            lane = fc if near == 0 else 1 - fc
            for block in range(blocks):
                start = pl.multiple_of(where * half + order[blocks + block] * size, size)
                target[near, block * size : (block + 1) * size, 0:half] = second_sum[
                    lane, pl.ds(start, size), :
                ]
                at = pl.ds(pl.multiple_of(start + lane * part, part), part)
                for side in range(2):
                    target[
                        near,
                        block * size + side * part : block * size + (side + 1) * part,
                        half : half + PADDED // 2,
                    ] = out_sum[at, side * (PADDED // 2) : (side + 1) * (PADDED // 2)].astype(BF16)


def small_grads(
    blocks, parts, order, act_first, act_second, grad_second, grad_own, grad_other, grad_logits, losses
):
    hidden = act_first.shape[0]
    half = hidden // 2
    low = jax.ShapeDtypeStruct((2, half, half + PADDED // 2), BF16)
    return pl.pallas_call(
        functools.partial(small_grads_kernel, blocks, parts),
        out_shape=(low, low, jax.ShapeDtypeStruct((PADDED, 1), F32)),
        in_specs=[smem()] + [vmem()] * 7,
        out_specs=(vmem(),) * 3,
        scratch_shapes=[
            pltpu.VMEM((2, hidden, half), BF16),
            pltpu.VMEM((hidden, PADDED), F32),
        ],
        compiler_params=limits(52),
        cost_estimate=lasting(4.0),
        name="small_grads",
    )(order, act_first, act_second, grad_second, grad_own, grad_other, grad_logits, losses)


def assemble_kernel(blocks, order, *refs):
    sources, (second_turned, second, out_weight, out_turned) = refs[:-4], refs[-4:]
    hidden = second.shape[0]
    half = hidden // 2
    size = half // blocks
    part = size // 2
    section, fc = order[3 * blocks], order[3 * blocks + 1]
    first = 0
    for at in range(0, len(sources), 4):
        for index, source in enumerate(sources[at : at + 4]):
            where = section if index < 2 else 1 - section
            lane = fc if index % 2 == 0 else 1 - fc
            for block in range(source.shape[0] // size):
                rows = slice(block * size, (block + 1) * size)
                start = pl.multiple_of(
                    where * half + order[2 * blocks + first + block] * size, size
                )
                second_turned[lane, pl.ds(start, size), :] = source[rows, 0:half]
                target = pl.ds(pl.multiple_of(start + lane * part, part), part)
                for side in range(2):
                    out_weight[target, side * (PADDED // 2) : (side + 1) * (PADDED // 2)] = source[
                        block * size + side * part : block * size + (side + 1) * part,
                        half : half + PADDED // 2,
                    ]
        first += sources[at].shape[0] // size
    for side in range(2):
        second[side * half : (side + 1) * half, :] = jnp.transpose(second_turned[side])
    out_turned[...] = jnp.transpose(out_weight[...])


def assemble(blocks, order, groups):
    sources = [source for group in groups for source in group]
    half = sum(group[0].shape[0] for group in groups)
    hidden = 2 * half
    low = lambda *shape: jax.ShapeDtypeStruct(shape, BF16)
    return pl.pallas_call(
        functools.partial(assemble_kernel, blocks),
        out_shape=(low(2, hidden, half), low(hidden, hidden), low(hidden, PADDED), low(PADDED, hidden)),
        in_specs=[smem()] + [vmem()] * len(sources),
        out_specs=(vmem(),) * 4,
        compiler_params=limits(52),
        cost_estimate=lasting(5.0),
        name="assemble",
    )(order, *sources)


def lane_blocks(lanes):
    for parts in (7, 1):
        if lanes % (128 * parts) == 0:
            return parts, lanes // parts


def join_kernel(straight, passed_head, crossed, passed_tail, moving, cross):
    half = straight.shape[0] // 2
    moving[0:half, :] = (
        straight[0:half, :].astype(F32) + passed_head[...].astype(F32)
    ).astype(BF16)
    moving[half : 2 * half, :] = straight[half : 2 * half, :]
    cross[0:half, :] = crossed[0:half, :]
    cross[half : 2 * half, :] = (
        crossed[half : 2 * half, :].astype(F32) + passed_tail[...].astype(F32)
    ).astype(BF16)


def join(straight, passed_head, blocks, at, passed_tail):
    held, lanes = straight.shape
    return pl.pallas_call(
        join_kernel,
        out_shape=(jax.ShapeDtypeStruct(straight.shape, BF16),) * 2,
        grid=(1,),
        in_specs=[
            pl.BlockSpec((held, lanes), lambda step: (0, 0)),
            pl.BlockSpec((held // 2, lanes), lambda step: (0, 0)),
            pl.BlockSpec((held, lanes), lambda step: (at, 0)),
            pl.BlockSpec((held // 2, lanes), lambda step: (0, 0)),
        ],
        out_specs=(pl.BlockSpec((held, lanes), lambda step: (0, 0)),) * 2,
        compiler_params=limits(52),
        cost_estimate=lasting(1.5),
        name="join",
    )(straight, passed_head, blocks, passed_tail)


def input_grad_kernel(count, grad, *refs):
    weight = jnp.concatenate([ref[...] for ref in refs[:count]], axis=0)
    value = dot(grad[...], weight).astype(BF16)
    start = 0
    for out in refs[count:]:
        out[...] = value[start : start + out.shape[0]]
        start += out.shape[0]


def input_grad(grad, pieces, sizes, lanes):
    parts, size = lane_blocks(lanes)
    return pl.pallas_call(
        functools.partial(input_grad_kernel, len(pieces)),
        out_shape=tuple(jax.ShapeDtypeStruct((rows, lanes), BF16) for rows in sizes),
        grid=(parts,),
        in_specs=[pl.BlockSpec(grad.shape, lambda step: (0, 0))]
        + [pl.BlockSpec((piece.shape[0], size), lambda step: (0, step)) for piece in pieces],
        out_specs=tuple(pl.BlockSpec((rows, size), lambda step: (0, step)) for rows in sizes),
        compiler_params=limits(52),
        cost_estimate=lasting(5.0),
        name="input_grad",
    )(grad, *pieces)


def line_order(line):
    return (0, 1, 3, 2) if line == 4 else tuple(range(line))


def pair_swap(value, count):
    return lax.ppermute(value, "wide", [(at, at ^ 1) for at in range(count)])


def line_step(value, count, way=1):
    places = line_order(count // 2)
    steps = []
    for at, place in enumerate(places):
        target = places[(at + way) % len(places)]
        steps += [(2 * place + side, 2 * target + side) for side in range(2)]
    return lax.ppermute(value, "wide", sorted(steps))


def line_swap(value, count, bit):
    return lax.ppermute(value, "wide", [(at, at ^ (2 * bit)) for at in range(count)])


def swap(value, axis):
    return lax.ppermute(value, axis, [(0, 1), (1, 0)])


def together(*values):
    return lax.optimization_barrier(values)


def add(*terms):
    total = terms[0].astype(F32)
    for term in terms[1:]:
        total = total + term.astype(F32)
    return total.astype(BF16)


def ring_order(wide, line):
    places = line_order(line)
    here = sum((jnp.where(wide // 2 == place, at, 0) for at, place in enumerate(places)))
    table = lambda index: sum(
        (jnp.where(index == at, place, 0) for at, place in enumerate(places))
    )
    return [
        table((here - step) % line) * 2 + ((wide % 2) ^ side)
        for side in range(2)
        for step in range(line)
    ]


def swap_order(wide, line):
    return [
        ((wide // 2) ^ step) * 2 + ((wide % 2) ^ side) for side in range(2) for step in range(line)
    ]


def split_tall(terms, n_wide):
    sections, places, half, columns = terms.shape
    held = half // n_wide
    second = terms[..., : columns - PADDED // 2].reshape(sections, places, n_wide, held, -1)
    out = terms[..., columns - PADDED // 2 :].reshape(sections, places, 2, half // 2, PADDED // 2)
    out = jnp.transpose(out, (0, 1, 3, 2, 4)).reshape(sections, half, PADDED)
    out = out.reshape(sections, n_wide, places, held // places, 2, PADDED // 2)
    out = jnp.transpose(out, (0, 2, 1, 4, 3, 5)).reshape(sections, places, n_wide, held, -1)
    return jnp.concatenate([second, out], axis=-1)


def body(
    map_p2,
    map_p3,
    map_p4,
    map_p5,
    boxes,
    levels,
    classes,
    sampled,
    counts,
    targets,
    first_weight,
    second_weight,
    out_weight,
    hidden_bias,
    out_bias,
    first_moment,
    second_moment,
    out_moment,
    hidden_moment,
    bias_moment,
    first_average,
    second_average,
    out_average,
    hidden_average,
    bias_average,
):
    n_section = lax.axis_size("section")
    n_fc = lax.axis_size("fc")
    n_wide = lax.axis_size("wide")
    section = lax.axis_index("section")
    fc = lax.axis_index("fc")
    wide = lax.axis_index("wide")
    everywhere = ("section", "wide", "fc")
    maps = [map_p2, map_p3, map_p4, map_p5]
    channels = map_p2.shape[3]
    height = map_p2.shape[1] * n_section
    width = map_p2.shape[2]
    rows_dev = boxes.shape[0]
    rows_own = rows_dev // (n_section * n_fc)
    held = first_weight.shape[1]
    classes_out = out_weight.shape[1]
    place = section.astype(jnp.int32).reshape(1)

    ring = n_wide == 8
    line = n_wide // 2
    rows_tall = out_weight.shape[0]
    rows_fc = n_section * rows_own
    half_held = held // 2
    lanes = first_weight.shape[0]

    place = jnp.stack([section, fc]).astype(jnp.int32)

    turned = turn_weight(
        counts, first_weight.T, sampled, second_weight.T, out_weight, hidden_bias
    )
    slot_parts = (counts, boxes, levels, classes, sampled, targets)
    turned, maps, slot_parts = together(turned, maps, slot_parts)
    if ring:
        places = ring_order(wide, line)
        small_at = [0, 1, 3, 4, 2, 5, 7, 6]
        order = jnp.stack(
            places
            + swap_order(wide, line)
            + [places[at] for at in small_at]
            + [section, fc, (section * n_wide + wide) * n_fc + fc]
            + [places[at] for at in (0, 1, 2, 4, 5, 3, 6, 7)]
        ).astype(jnp.int32)
        blocks = n_wide
        straight = [turned, line_step(turned, n_wide)]
        crossed = [pair_swap(turned, n_wide)]
        last_small = line_step(turned[:, lanes:], n_wide, -1)
    else:
        zero = jnp.zeros_like(section)
        order = jnp.stack([zero, zero, zero, section, fc, zero, zero]).astype(jnp.int32)
        blocks = 1
    half_own = jnp.concatenate([level_map.reshape(-1, channels) for level_map in maps], axis=0)
    half_other = swap(half_own, "section")
    *parameters, slots = plan(place, *slot_parts, n_fc * rows_own, height, width)
    table = build_table(place, half_own, half_other, height, width)

    crops_mine = crop_forward(parameters, table, 0, rows_own)
    if ring:
        straight[1], crossed[0], last_small, table, crops_mine = together(
            straight[1], crossed[0], last_small, table, crops_mine
        )
        small_of = lambda piece: piece[:, lanes:]
        small_a = jnp.concatenate(
            [small_of(straight[0]), small_of(straight[1]), last_small, small_of(crossed[0])], axis=0
        )
        straight.append(line_step(straight[1], n_wide))
        crossed.append(pair_swap(straight[1], n_wide))
        last_crossed = pair_swap(last_small, n_wide)
        passed_a = swap(small_a, "fc")
    passed_mine = swap(crops_mine, "section")
    crops_theirs = crop_forward(parameters, table, rows_own, rows_own)

    if ring:
        straight[2], crossed, last_crossed, passed_mine, crops_theirs, small_a, passed_a = together(
            straight[2], crossed, last_crossed, passed_mine, crops_theirs, small_a, passed_a
        )
        straight.append(line_step(straight[2], n_wide))
        crossed.append(pair_swap(straight[2], n_wide))
        small_b = jnp.concatenate(
            [small_of(straight[2]), small_of(crossed[1]), last_crossed], axis=0
        )
        passed_b = swap(small_b, "fc")
        passed_theirs = swap(crops_theirs, "section")
        weight_of = lambda piece: piece[:, :lanes]
        early_weight = jnp.concatenate(
            [weight_of(piece) for piece in straight[:3] + crossed[:2]], axis=0
        )
        inputs_all = jnp.concatenate([crops_mine, passed_mine, crops_theirs, passed_theirs], axis=0)
        early = dot_last(early_weight, inputs_all)
        early, early_passed = early[:, :rows_fc], swap(early[:, rows_fc:].astype(BF16), "fc")
        straight[3], crossed[2], inputs_all, early, small_b, passed_b = together(
            straight[3], crossed[2], inputs_all, early, small_b, passed_b
        )
        tail = [
            pair_swap(straight[3][:half_held, :lanes], n_wide),
            line_step(crossed[2][half_held:, :lanes], n_wide),
        ]
        small_c = small_of(crossed[2])
        late = dot_last(
            jnp.concatenate([weight_of(straight[3]), weight_of(crossed[2])], axis=0), inputs_all
        )
        passed_c = swap(small_c, "fc")
        groups = [
            [small, passed, swap(small, "section"), swap(passed, "section")]
            for small, passed in ((small_a, passed_a), (small_b, passed_b))
        ]
        early = early + early_passed.astype(F32)
        tail, late, early, passed_c, inputs_all = together(tail, late, early, passed_c, inputs_all)
        last = jnp.concatenate(tail, axis=0)
        end = dot_last(last, inputs_all)
        late, late_passed = late[:, :rows_fc], swap(late[:, rows_fc:].astype(BF16), "fc")
        early_other = swap(early[:, rows_own:], "section")
        end_passed = end[:, rows_fc:].astype(BF16)
        end_passed, end, early, early_other, late, late_passed, groups = together(
            end_passed, end, early, early_other, late, late_passed, groups
        )
        end_passed = swap(end_passed, "fc")
        late = late + late_passed.astype(F32)
        late_other = swap(late[:, rows_own:], "section")
        groups.append([small_c, passed_c, swap(small_c, "section"), swap(passed_c, "section")])
        small_weights = assemble(blocks, order, groups)
        end_passed, small_weights, late, late_other = together(
            end_passed, small_weights, late, late_other
        )
        w_second_turned, w_second, w_out, w_out_turned = small_weights
        end = end[:, :rows_fc] + end_passed.astype(F32)
        end_other = swap(end[:, rows_own:], "section")
        pre_own = [part[:, :rows_own] for part in (early, late, end)]
        pre_other = [early_other, late_other, end_other]
        pieces = straight + crossed + [last]
    else:
        passed_theirs = swap(crops_theirs, "section")
        inputs_all = jnp.concatenate([crops_mine, passed_mine, crops_theirs, passed_theirs], axis=0)
        pieces = [lax.all_gather(turned[:, :lanes], "wide", axis=0, tiled=True)]
        pre = dot_last(pieces[0], inputs_all)
        pre = pre[:, :rows_fc] + swap(pre[:, rows_fc:], "fc")
        pre_own, pre_other = [pre[:, :rows_own]], [swap(pre[:, rows_own:], "section")]
        small = lax.all_gather(turned[:, lanes:], everywhere, axis=0, tiled=True)
        small = small.reshape(-1, n_fc, held, turned.shape[1] - lanes)
        w_second_turned = jnp.transpose(
            small[..., : second_weight.shape[0]], (1, 0, 2, 3)
        ).reshape(n_fc, -1, second_weight.shape[0])
        w_second = jnp.transpose(w_second_turned, (0, 2, 1)).reshape(
            -1, w_second_turned.shape[1]
        )
        w_out = small[..., second_weight.shape[0] :].reshape(-1, 2, rows_tall, PADDED // 2)
        w_out = jnp.transpose(w_out, (0, 2, 1, 3)).reshape(-1, PADDED)
        w_out_turned = w_out.T
    grad_own, grad_other, act_first, act_second, grad_second, grad_logits, losses, total = middle(
        blocks,
        n_wide,
        order,
        pre_own,
        pre_other,
        w_second_turned,
        w_second,
        w_out_turned,
        w_out,
        jnp.pad(out_bias, (0, PADDED - classes_out))[:, None],
        slots,
    )
    grad_passed = swap(grad_other, "section")
    grad_passed, grad_own, act_first = together(grad_passed, grad_own, act_first)
    grad_mine = jnp.concatenate([grad_own, grad_passed], axis=1)
    rate = 0.15 * math.sqrt(rows_dev * n_wide)
    back = lambda sent: swap(sent, "section")

    if ring:
        def all_slots(parts):
            mine = jnp.concatenate([grad_mine[at * held : (at + 1) * held] for at in parts], axis=0)
            return jnp.concatenate([mine, swap(mine, "fc")], axis=1)

        def block(values, at):
            return values[at * held : (at + 1) * held]

        rest_at = [0, 2, 3, line, line + 2, line + 3]
        first_grads = all_slots([1, line + 1])
        terms_own, terms_other, bias_terms = small_grads(
            blocks, True, order, act_first, act_second, grad_second, grad_own, grad_other, grad_logits, losses
        )
        first_grads, terms_own, terms_other = together(first_grads, terms_own, terms_other)
        first_terms = dot(first_grads, inputs_all).astype(BF16)
        rest_grads = all_slots(rest_at)
        first_terms, rest_grads, terms_other = together(first_terms, rest_grads, terms_other)
        moving, cross = block(first_terms, 0), block(first_terms, 1)
        tail = line_step(cross[half_held:], n_wide)
        head = pair_swap(cross[:half_held], n_wide)
        small = swap(terms_other, "section")
        rest = dot(rest_grads, inputs_all).astype(BF16)
        small = [add(terms_own[at], small[at]) for at in range(n_fc)]
        tail, head, rest, small, first_grads, rest_grads = together(
            tail, head, rest, small, first_grads, rest_grads
        )

        moving, cross = join(moving, head, rest, 4, tail)
        moving, cross, rest_grads = together(moving, cross, rest_grads)
        cross = pair_swap(cross, n_wide)
        moving = line_step(moving, n_wide)
        small_passed = swap(small[1], "fc")
        grad_all = jnp.concatenate(
            [
                block(rest_grads, 0),
                first_grads[:held],
                rest_grads[held : 3 * held],
                block(rest_grads, 3),
                first_grads[held:],
                rest_grads[4 * held :],
            ],
            axis=0,
        )
        keep_mine, send_mine, keep_theirs, send_theirs = input_grad(
            grad_all.T, pieces, [rows_own] * 4, lanes
        )
        moving, cross, rest, keep_mine, keep_theirs, send_mine, send_theirs = together(
            moving, cross, rest, keep_mine, keep_theirs, send_mine, send_theirs
        )

        back_mine = [back(send_mine)]
        moving = add(block(rest, 1), cross, moving)
        moving, keep_mine = together(moving, keep_mine)
        moving = line_step(moving, n_wide)
        cross = pair_swap(block(rest, 5), n_wide)
        before = crop_backward(place, parameters, keep_mine, back_mine, 0, height, width)
        moving, cross, rest, before, keep_theirs, send_theirs, small_passed = together(
            moving, cross, rest, before, keep_theirs, send_theirs, small_passed
        )

        back_theirs = [back(send_theirs)]
        moving = add(block(rest, 2), cross, moving)
        small = add(small[0], small_passed)
        moving, small, before = together(moving, small, before)
        moving = line_step(moving, n_wide)
        cut = small.shape[0] // 2
        small_passed = pair_swap(small[cut:], n_wide)
        cross = pair_swap(block(rest, 3), n_wide)
        map_own, map_other = crop_backward(
            place, parameters, keep_theirs, back_theirs, rows_own, height, width, before
        )
        small_passed, map_own, map_other = together(small_passed, map_own, map_other)
        small = add(small[:cut], small_passed)
        small_terms = [small[:held]] + [
            line_swap(small[bits * held : (bits + 1) * held], n_wide, bits)
            for bits in range(1, line)
        ]
        cut = map_other.shape[0] // (2 * GROUP) * GROUP
        map_passed = [swap(map_other[:cut], "section"), swap(map_other[cut:], "section")]
        map_grads = map_sum(map_own, map_passed, maps)
        moving, cross, map_grads = together(moving, cross, map_grads)
        first_sums = [block(rest, 0), cross, moving]
    else:
        grad_all = jnp.concatenate([grad_mine, swap(grad_mine, "fc")], axis=1)
        first_sums = [
            lax.psum_scatter(
                dot(grad_all, inputs_all).astype(BF16), "wide", scatter_dimension=0, tiled=True
            )
        ]
        keep_mine, send_mine, keep_theirs, send_theirs = input_grad(
            grad_all.T, pieces, [rows_own] * 4, lanes
        )
        before = crop_backward(place, parameters, keep_mine, [back(send_mine)], 0, height, width)
        map_own, map_other = crop_backward(
            place, parameters, keep_theirs, [back(send_theirs)], rows_own, height, width, before
        )
        map_grads = map_sum(map_own, [swap(map_other, "section")], maps)
        terms_own, terms_other, bias_terms = small_grads(
            blocks, False, order, act_first, act_second, grad_second, grad_own, grad_other, grad_logits, losses
        )
        terms = jnp.stack(
            [jnp.where(section == at, terms_own, terms_other) for at in range(n_section)]
        )
        terms = jnp.where(fc == 0, terms, terms[:, ::-1])
        terms = jnp.transpose(split_tall(terms, n_wide), (0, 2, 1, 3, 4))
        small_sum = lax.psum_scatter(
            terms.reshape(-1, terms.shape[-1]), everywhere, scatter_dimension=0, tiled=True
        ).astype(F32)
    first_out = renew_first(first_sums, first_weight.T, first_moment.T, first_average.T, rate)
    if ring:
        first_out, small_terms = together(first_out, small_terms)
        small_out = renew_small(
            small_terms,
            (
                (second_weight.T, second_moment.T, second_average.T),
                (out_weight, out_moment, out_average),
                (hidden_bias, hidden_moment, hidden_average),
                (out_bias[None], bias_moment[None], bias_average[None]),
            ),
            rate,
        )
        *small_out, loss_sum = small_out
        loss_sum = loss_sum[0, 0]
        second_out = [value.T for value in small_out[:3]]
        out_out, hidden_out = small_out[3:6], small_out[6:9]
        bias_out = [value[0] for value in small_out[9:]]
    else:
        second_sum = small_sum[:, : second_weight.shape[0]]
        tall_sum = small_sum[:, second_weight.shape[0] :]
        tall_sum = jnp.concatenate([tall_sum[:rows_tall], tall_sum[rows_tall:]], axis=1)
        vector = jnp.concatenate([bias_terms[:classes_out, 0], jnp.sum(losses).reshape(1)])
        vector = lax.psum(vector, everywhere)
        loss_sum = vector[classes_out]
        second_out = renew(second_weight, second_moment, second_average, second_sum.T, rate)
        out_out = renew(out_weight, out_moment, out_average, tall_sum[:, :classes_out], rate)
        hidden_out = renew(
            hidden_bias,
            hidden_moment,
            hidden_average,
            tall_sum[:, classes_out : classes_out + 2],
            rate,
        )
        bias_out = renew(out_bias, bias_moment, bias_average, vector[:classes_out], 4.0)
    return (
        loss_sum,
        total[0, 0],
        map_grads[0],
        map_grads[1],
        map_grads[2],
        map_grads[3],
        first_out[0].T,
        first_out[1].T,
        first_out[2].T,
        *second_out,
        *out_out,
        *hidden_out,
        *bias_out,
    )


def solution(mesh):
    maps = P("wide", "section", None, "fc")
    wide_weight = P("fc", ("section", "wide"))
    tall_weight = P(("section", "wide", "fc"), None)
    in_specs = (
        (maps,) * 4
        + (P("wide", None), P("wide"), P("wide"), P("wide"), P("wide"), P("wide", None))
        + (wide_weight, wide_weight, tall_weight, tall_weight, P()) * 3
    )
    out_specs = (
        (P(), P())
        + (maps,) * 4
        + (wide_weight,) * 6
        + (tall_weight,) * 6
        + (P(),) * 3
    )
    return jax.shard_map(body, mesh=mesh, in_specs=in_specs, out_specs=out_specs, check_vma=False)
```

```python
import functools
import math

import jax
import jax.numpy as jnp
from jax import lax
from jax.experimental import pallas as pl
from jax.experimental.pallas import tpu as pltpu
from jax.sharding import PartitionSpec as P

CLASSES = 81
BINS = 7
CELLS = BINS * BINS
WINDOW = 24
WINDOWS = (24, 16, 8)
GROUP = 16
CHAINS = 4
SETS = 2
PADDED = 512
WIDTH = 5 * CLASSES - 4
BIAS_AT = 416
LOSS_AT = 448
MOMENTUM = 0.9
AVERAGE = 0.7
DECAY = 0.0001
SMOOTH = 0.5

F32 = jnp.float32
BF16 = jnp.bfloat16


def smem():
    return pl.BlockSpec(memory_space=pltpu.SMEM)


def vmem():
    return pl.BlockSpec(memory_space=pltpu.VMEM)


def lasting(microseconds):
    return pl.CostEstimate(
        flops=0, bytes_accessed=int(microseconds * 1e3), transcendentals=0
    )


def limits(mebibytes):
    return pltpu.CompilerParams(vmem_limit_bytes=mebibytes * 2**20)


def level_plan(height, width):
    shapes = [(height >> depth, width >> depth) for depth in range(4)]
    strides = [max(rows, WINDOW) for rows, cols in shapes]
    bases = [0]
    for depth in range(4):
        bases.append(bases[-1] + strides[depth] * shapes[depth][1])
    total = -(-(bases[-1] + 2 * WINDOW) // GROUP) * GROUP
    return shapes, strides, bases[:4], total


def half_starts(shapes):
    starts = [0]
    for rows, cols in shapes:
        starts.append(starts[-1] + rows // 2 * cols)
    return starts


def table_kernel(height, width, place, own, other, table):
    shapes, strides, bases, total = level_plan(height, width)
    starts = half_starts(shapes)
    table[...] = jnp.zeros_like(table)

    def fill(source, bottom):
        for depth, (rows, cols) in enumerate(shapes):
            half = rows // 2

            def column(x, carry, depth=depth, half=half, cols=cols):
                cells = source[pl.ds(starts[depth] + x, half, stride=cols), :]
                table[pl.ds(bases[depth] + x * strides[depth] + bottom * half, half), :] = cells
                return carry

            lax.fori_loop(0, cols, column, 0, unroll=4)

    bottom = place[0]
    fill(own, bottom)
    fill(other, 1 - bottom)


def build_table(place, own, other, height, width):
    total = level_plan(height, width)[3]
    return pl.pallas_call(
        functools.partial(table_kernel, height, width),
        out_shape=jax.ShapeDtypeStruct((total, own.shape[1]), F32),
        in_specs=[smem(), vmem(), vmem()],
        out_specs=vmem(),
        compiler_params=limits(52),
        cost_estimate=lasting(5.0),
        name="build_table",
    )(place, own, other)


def plan_kernel(
    height,
    width,
    place,
    counts,
    boxes,
    levels,
    classes,
    sampled,
    targets,
    address,
    weight,
    row_values,
    stride,
    slots,
    features,
):
    shapes, strides, bases, total = level_plan(height, width)
    count = boxes.shape[1]
    own = address.shape[1]
    share = own // 2
    section, fc = place[0], place[1]
    lane = lax.broadcasted_iota(jnp.int32, (1, count), 1)
    live = (lane < counts[0]) & (sampled[...] > 0)
    key = (jnp.where(live, levels[...], 4) * count + lane).astype(F32)
    across = jnp.broadcast_to(key, (128, count))
    down = jnp.transpose(across)
    before = jnp.zeros((count, 128), F32)
    for start in range(0, count, 128):
        before = before + jnp.where(key[:, start : start + 128] < down, 1.0, 0.0)
    rank = jnp.sum(before, axis=1, keepdims=True).astype(jnp.int32)
    seat = rank // 2
    side = jnp.where(seat % 2 == fc, 0, share)
    seat = jnp.where(rank % 2 == section, seat // 2 + side, -1)
    deal = jnp.where(
        jnp.broadcast_to(seat, (count, own)) == lax.broadcasted_iota(jnp.int32, (count, own), 1),
        1.0,
        0.0,
    )
    features[...] = jnp.zeros_like(features)
    features[0:4, :] = boxes[...]
    features[4:8, :] = targets[...]
    features[8:9, :] = levels[...].astype(F32)
    features[9:10, :] = classes[...].astype(F32)
    features[10:11, :] = jnp.where(live, 1.0, 0.0)
    dealt = jnp.dot(
        features[...], deal, preferred_element_type=F32, precision=lax.Precision.HIGHEST
    )
    slots[...] = jnp.zeros_like(slots)
    slots[0:1, :] = dealt[10:11, 0:share]
    slots[2:3, :] = dealt[9:10, 0:share]
    slots[3:7, :] = dealt[4:8, 0:share]
    level = (dealt[8:9, :] + 0.5).astype(jnp.int32)

    def choose(values, kind):
        out = jnp.full(level.shape, values[3], kind)
        for depth in range(3):
            out = jnp.where(level == depth, jnp.asarray(values[depth], kind), out)
        return out

    reach_y = choose([h - 1 for h, w in shapes], F32)
    reach_x = choose([w - 1 for h, w in shapes], F32)
    step = choose(strides, jnp.int32)
    base = choose(bases, jnp.int32)
    top = (dealt[0:1, :] - 0.25 * dealt[2:3, :]) * reach_y
    length_y = 0.5 * dealt[2:3, :] * reach_y
    left = (dealt[1:2, :] - 0.25 * dealt[3:4, :]) * reach_x
    length_x = 0.5 * dealt[3:4, :] * reach_x
    first = jnp.clip(jnp.floor(top + length_y * (0.25 / 7.0)), 0.0, reach_y - 1.0)
    start = base + first.astype(jnp.int32)
    for at in range(2 * BINS):
        points = left + length_x * ((at // 2 + (at % 2 + 0.5) * 0.5) / 7.0)
        lower = jnp.clip(jnp.floor(points), 0.0, reach_x - 1.0)
        address[at : at + 1, :] = start + lower.astype(jnp.int32) * step
        weight[at : at + 1, :] = points - lower
    for at, value in enumerate((top, length_y, first, reach_y - 1.0)):
        row_values[at : at + 1, :] = value
    stride[0:1, :] = step
    stride[1:2, :] = jnp.where(dealt[10:11, :] > 0.5, choose([3, 2, 1, 1], jnp.int32), 0)


def plan(place, counts, boxes, levels, classes, sampled, targets, own, height, width):
    whole = jax.ShapeDtypeStruct
    count = boxes.shape[0]
    return pl.pallas_call(
        functools.partial(plan_kernel, height, width),
        out_shape=(
            whole((2 * BINS, own), jnp.int32),
            whole((2 * BINS, own), F32),
            whole((4, own), F32),
            whole((2, own), jnp.int32),
            whole((8, own // 2), F32),
        ),
        in_specs=[smem()] * 2 + [vmem()] * 5,
        out_specs=(vmem(),) * 5,
        scratch_shapes=[pltpu.VMEM((16, count), F32)],
        compiler_params=limits(52),
        cost_estimate=lasting(3.0),
        name="plan",
    )(place, counts, boxes.T, levels[None], classes[None], sampled[None], targets.T)


def row_weights(values, index, offset):
    top, length, first, last = values
    total = None
    for place in (0.25, 0.75):
        points = top + length * ((index + place) / 7.0)
        lower = jnp.minimum(jnp.maximum(jnp.floor(points), 0.0), last)
        upper_weight = points - lower
        distance = offset - (lower - first)
        part = jnp.where(
            distance == 0.0, 1.0 - upper_weight, jnp.where(distance == 1.0, upper_weight, 0.0)
        )
        total = part if total is None else total + part
    return total * 0.25


def crop_kernel(rows, first, address, weight, row_values, stride, table, out, turned):
    def crops(window, step):
        depth = -(-BINS * window // 128) * 128
        lane = lax.broadcasted_iota(jnp.int32, (8, depth), 1)
        offset = (lane % window).astype(F32)
        index = lax.broadcasted_iota(jnp.int32, (8, depth), 0).astype(F32)
        inside = (
            lax.broadcasted_iota(jnp.int32, (8 * BINS, depth), 0) // 8
            == lax.broadcasted_iota(jnp.int32, (8 * BINS, depth), 1) // window
        )

        for part in range(GROUP):
            row = first + step * GROUP + part
            weights = row_weights([row_values[at, row] for at in range(4)], index, offset)
            left = jnp.where(inside, jnp.concatenate([weights] * BINS, axis=0), 0.0)
            step_x = stride[0, row]
            columns = []
            for k in range(BINS):
                total = None
                for m in range(2):
                    place = address[2 * k + m, row]
                    upper = weight[2 * k + m, row]
                    near = table[pl.ds(place, window), :]
                    far = table[pl.ds(place + step_x, window), :]
                    value = near + upper * (far - near)
                    total = value if total is None else total + value
                columns.append(total)
            columns.append(jnp.zeros((depth - BINS * window, 128), F32))
            right = jnp.concatenate(columns, axis=0).astype(BF16)
            crop = jnp.dot(left.astype(BF16), right, preferred_element_type=F32)
            for k in range(BINS):
                turned[pl.ds(part + k * BINS * GROUP, BINS, stride=GROUP), :] = crop[
                    8 * k : 8 * k + BINS
                ]

    def group(step, carry):
        start = pl.multiple_of(step * GROUP, GROUP)
        eights = stride[1, first + step * GROUP]
        for window in WINDOWS:

            @pl.when(eights == window // 8)
            def live_slots(window=window):
                crops(window, step)

        @pl.when(eights > 0)
        def store():
            for cell in range(CELLS):
                out[pl.ds(start, GROUP), cell * 128 : (cell + 1) * 128] = turned[
                    cell * GROUP : (cell + 1) * GROUP, :
                ].astype(BF16)

        @pl.when(eights == 0)
        def dead_slots():
            out[pl.ds(start, GROUP), :] = jnp.zeros((GROUP, CELLS * 128), BF16)

        return carry

    lax.fori_loop(0, rows // GROUP, group, 0)


def crop_forward(parameters, table, first, rows):
    return pl.pallas_call(
        functools.partial(crop_kernel, rows, first),
        out_shape=jax.ShapeDtypeStruct((rows, CELLS * 128), BF16),
        in_specs=[smem()] * 4 + [vmem()],
        out_specs=vmem(),
        scratch_shapes=[pltpu.VMEM((CELLS * GROUP, 128), F32)],
        compiler_params=limits(52),
        cost_estimate=lasting(0.07 * rows),
        name="crop_forward",
    )(*parameters, table)


def spread_kernel(
    rows, first, height, width, last, parts, place, address, weight, row_values, stride, keep, *refs
):
    shapes, strides, bases, total = level_plan(height, width)
    starts = half_starts(shapes)
    passed_parts, refs = refs[:parts], refs[parts:]
    if last:
        before, own, other, passed, turned, half, *tables = refs
    else:
        out, passed, turned, *tables = refs
    size = rows // parts
    for at, part in enumerate(passed_parts):
        passed[at * size : (at + 1) * size, :] = part[...]
    for table in tables:
        table[...] = jnp.zeros_like(table)
    turned[pl.ds(CELLS * GROUP, GROUP), :] = jnp.zeros((GROUP, 128), F32)

    def spread(window, base, few):
        index = (lax.broadcasted_iota(jnp.int32, (window, 128), 1) % 8).astype(F32)
        offset = lax.broadcasted_iota(jnp.int32, (window, 128), 0).astype(F32)
        long_row = lax.broadcasted_iota(jnp.int32, (BINS * window, 128), 0)
        long_lane = lax.broadcasted_iota(jnp.int32, (BINS * window, 128), 1)
        inside = (long_row // window == long_lane // 8) & (long_lane % 8 < BINS)
        results = []
        for at in range(SETS * CHAINS):
            part = few * SETS * CHAINS + at
            row = base + at
            weights = row_weights([row_values[at, row] for at in range(4)], index, offset)
            left = jnp.where(inside, jnp.concatenate([weights] * BINS, axis=0), 0.0).astype(BF16)
            pieces = [
                turned[pl.ds(part + k * BINS * GROUP, 8, stride=GROUP), :] for k in range(BINS)
            ]
            pieces.append(jnp.zeros((128 - 8 * BINS, 128), F32))
            right = jnp.concatenate(pieces, axis=0).astype(BF16)
            results.append(jnp.dot(left, right, preferred_element_type=F32))
        for head in range(0, SETS * CHAINS, CHAINS):
            for k in range(BINS):
                for m in range(2):
                    for chain in range(CHAINS):
                        row = base + head + chain
                        table = tables[chain]
                        at = address[2 * k + m, row]
                        next_at = at + stride[0, row]
                        value = results[head + chain][k * window : (k + 1) * window]
                        upper = value * weight[2 * k + m, row]
                        near = table[pl.ds(at, window), :] + (value - upper)
                        far = table[pl.ds(next_at, window), :] + upper
                        table[pl.ds(at, window), :] = near
                        table[pl.ds(next_at, window), :] = far

    def group(step, carry):
        start = pl.multiple_of(step * GROUP, GROUP)

        @pl.when(stride[1, first + step * GROUP] > 0)
        def live_slots():
            for cell in range(CELLS):
                span = slice(cell * 128, (cell + 1) * 128)
                turned[cell * GROUP : (cell + 1) * GROUP, :] = keep[
                    pl.ds(start, GROUP), span
                ].astype(F32) + passed[pl.ds(start, GROUP), span].astype(F32)

            def some(few, carry):
                base = first + step * GROUP + few * SETS * CHAINS
                eights = stride[1, base]
                for window in WINDOWS:

                    @pl.when(eights == window // 8)
                    def one_window(window=window):
                        spread(window, base, few)

                return carry

            lax.fori_loop(0, GROUP // (SETS * CHAINS), some, 0)

        return carry

    lax.fori_loop(0, rows // GROUP, group, 0)
    result = tables[0] if last else out

    def summed(step, carry):
        span = pl.ds(pl.multiple_of(step * GROUP, GROUP), GROUP)
        value = tables[0][span, :]
        for table in tables[1:]:
            value = value + table[span, :]
        if last:
            value = value + before[span, :]
        result[span, :] = value
        return carry

    lax.fori_loop(0, total // GROUP, summed, 0)
    if not last:
        return

    def collect(target, bottom):
        for depth, (level_rows, cols) in enumerate(shapes):
            count = level_rows // 2

            def column(x, carry, depth=depth, count=count, cols=cols):
                cells = result[pl.ds(bases[depth] + x * strides[depth] + bottom * count, count), :]
                target[pl.ds(starts[depth] + x, count, stride=cols), :] = cells
                return carry

            lax.fori_loop(0, cols, column, 0, unroll=4)

    bottom = place[0]
    collect(own, bottom)
    collect(half, 1 - bottom)
    other[...] = half[...].astype(BF16)


def crop_backward(place, parameters, keep, passed, first, height, width, before=None):
    rows = keep.shape[0]
    shapes, strides, bases, total = level_plan(height, width)
    cells = half_starts(shapes)[-1]
    last = before is not None
    turned = pltpu.VMEM(((CELLS + 1) * GROUP, 128), F32)
    joined = pltpu.VMEM(keep.shape, BF16)
    tables = [pltpu.VMEM((total, 128), F32)] * CHAINS
    if last:
        out_shape = (
            jax.ShapeDtypeStruct((cells, 128), F32),
            jax.ShapeDtypeStruct((cells, 128), BF16),
        )
        scratch = [joined, turned, pltpu.VMEM((cells, 128), F32)] + tables
    else:
        out_shape = jax.ShapeDtypeStruct((total, 128), F32)
        scratch = [joined, turned] + tables
    return pl.pallas_call(
        functools.partial(spread_kernel, rows, first, height, width, last, len(passed)),
        out_shape=out_shape,
        in_specs=[smem()] * 5 + [vmem()] * ((2 if last else 1) + len(passed)),
        out_specs=(vmem(),) * 2 if last else vmem(),
        scratch_shapes=scratch,
        compiler_params=limits(52),
        cost_estimate=lasting(0.12 * rows),
        name="crop_backward",
    )(place, *parameters, keep, *passed, *([before] if last else []))


def natural_row(cell):
    k, i = divmod(cell, BINS)
    return i * BINS + k


def turn_kernel(
    counts,
    weight,
    sampled_far,
    second_far,
    out_far,
    bias_far,
    out,
    turned,
    tall,
    second,
    out_weight,
    hidden_bias,
    sampled,
    sems,
):
    held, lanes = weight.shape
    depth = second.shape[1]
    rows = out_weight.shape[0]
    half = PADDED // 2
    copies = [
        pltpu.make_async_copy(source, target, sems.at[at])
        for at, (source, target) in enumerate(
            (
                (second_far, second),
                (out_far, out_weight),
                (bias_far, hidden_bias),
                (sampled_far, sampled),
            )
        )
    ]
    for copy in copies:
        copy.start()
    for tile in range(CELLS):
        turned[tile * 128 : (tile + 1) * 128, 0:held] = jnp.transpose(
            weight[:, tile * 128 : (tile + 1) * 128]
        )
    for cell in range(CELLS):
        block = turned[pl.ds(natural_row(cell), 128, stride=CELLS), :]
        out[:, cell * 128 : (cell + 1) * 128] = jnp.transpose(block)[0:held].astype(BF16)
    for copy in copies:
        copy.wait()
    lane = lax.broadcasted_iota(jnp.int32, sampled.shape, 1)
    live = jnp.sum(
        jnp.where((lane < counts[0]) & (sampled[...] > 0), 1.0, 0.0), axis=1, keepdims=True
    )
    high = jnp.floor(live / 32.0)
    same = lax.broadcasted_iota(jnp.int32, (rows, rows), 0) == lax.broadcasted_iota(
        jnp.int32, (rows, rows), 1
    )
    biases = [
        jnp.sum(jnp.where(same, hidden_bias[at : at + 1, :], 0.0), axis=1, keepdims=True)
        for at in range(2)
    ]
    tall[...] = jnp.zeros_like(tall)
    tall[:, 0:WIDTH] = out_weight[...]
    column = lax.broadcasted_iota(jnp.int32, (rows, 128), 1) + (PADDED - 128)
    value = tall[:, PADDED - 128 : PADDED]
    for at, part in enumerate(
        (*biases, high, live - 32.0 * high)
    ):
        value = jnp.where(column == WIDTH + at, part, value)
    tall[:, PADDED - 128 : PADDED] = value
    out[:, lanes : lanes + depth] = second[...].astype(BF16)
    out[:, lanes + depth : lanes + depth + half] = jnp.concatenate(
        [tall[:, 0:half], tall[:, half:PADDED]], axis=0
    ).astype(BF16)


def turn_weight(counts, weight, sampled, second, out_weight, hidden_bias):
    held, lanes = weight.shape
    return pl.pallas_call(
        turn_kernel,
        out_shape=jax.ShapeDtypeStruct((held, lanes + second.shape[1] + PADDED // 2), BF16),
        in_specs=[smem(), vmem()] + [pl.BlockSpec(memory_space=pltpu.HBM)] * 4,
        out_specs=vmem(),
        scratch_shapes=[
            pltpu.VMEM((lanes, 128), F32),
            pltpu.VMEM((out_weight.shape[0], PADDED), F32),
            pltpu.VMEM(second.shape, F32),
            pltpu.VMEM(out_weight.shape, F32),
            pltpu.VMEM(hidden_bias.T.shape, F32),
            pltpu.VMEM((1, sampled.shape[0]), jnp.int32),
            pltpu.SemaphoreType.DMA((4,)),
        ],
        compiler_params=limits(62),
        cost_estimate=lasting(2.7),
        name="turn_weight",
    )(counts, weight, sampled[None], second, out_weight, hidden_bias.T)


def renew(weight, moment, average, grad, rate):
    step_value = grad + DECAY * weight
    moment_new = MOMENTUM * moment + step_value
    weight_new = weight - rate * (step_value + MOMENTUM * moment_new)
    average_new = AVERAGE * average + (1.0 - AVERAGE) * weight_new
    return (weight_new, moment_new, average_new)


def renew_kernel(rate, count, *refs):
    terms = refs[:count]
    kept = refs[count : count + 3]
    news = refs[count + 3 : count + 6]
    turned, *places = refs[count + 6 : count + 13]
    sems = refs[count + 13]
    held, lanes = terms[0].shape
    arrive = [
        pltpu.make_async_copy(kept[at], places[at], sems.at[at, 0]) for at in range(3)
    ]
    for copy in arrive:
        copy.start()
    for cell in range(CELLS):
        span = slice(cell * 128, (cell + 1) * 128)
        grad = terms[0][:, span].astype(F32)
        for term in terms[1:]:
            grad = grad + term[:, span].astype(F32)
        turned[pl.ds(natural_row(cell), 128, stride=CELLS), 0:held] = jnp.transpose(grad)
    for copy in arrive:
        copy.wait()
    leave = []
    for part in range(BINS):
        for tile in range(part * BINS, (part + 1) * BINS):
            span = slice(tile * 128, (tile + 1) * 128)
            grad = jnp.transpose(turned[span, :])[0:held]
            values = renew(*[place[:, span] for place in places[:3]], grad, rate)
            for at in range(3):
                places[3 + at][:, span] = values[at]
        span = pl.ds(part * BINS * 128, BINS * 128)
        for at in range(3):
            copy = pltpu.make_async_copy(
                places[3 + at].at[:, span], news[at].at[:, span], sems.at[at, 1 + part]
            )
            copy.start()
            leave.append(copy)
    for copy in leave:
        copy.wait()


def renew_first(terms, weight, moment, average, rate):
    held, lanes = weight.shape
    anywhere = pl.BlockSpec(memory_space=pl.ANY)
    return pl.pallas_call(
        functools.partial(renew_kernel, rate, len(terms)),
        out_shape=(jax.ShapeDtypeStruct(weight.shape, F32),) * 3,
        in_specs=[vmem()] * len(terms) + [anywhere] * 3,
        out_specs=(anywhere,) * 3,
        scratch_shapes=[pltpu.VMEM((lanes, 128), F32)]
        + [pltpu.VMEM((held, lanes), F32)] * 6
        + [pltpu.SemaphoreType.DMA((3, 1 + BINS))],
        compiler_params=limits(52),
        cost_estimate=lasting(6.5),
        name="renew_first",
    )(*terms, weight, moment, average)


def renew_small_kernel(rate, count, *refs):
    terms = refs[:count]
    second, tall, hidden, bias = (refs[count + 3 * at : count + 3 * at + 3] for at in range(4))
    second_new, tall_new, hidden_new, bias_new = (
        refs[count + 12 + 3 * at : count + 15 + 3 * at] for at in range(4)
    )
    loss = refs[count + 24]
    rows = tall[0].shape[0]
    depth = second[0].shape[1]
    half = PADDED // 2
    total = terms[0][...].astype(F32)
    for term in terms[1:]:
        total = total + term[...].astype(F32)

    def give(targets, sources, grad, rate):
        for target, value in zip(targets, renew(*[ref[...] for ref in sources], grad, rate)):
            target[...] = value

    give(second_new, second, total[:, :depth], rate)
    sums = jnp.concatenate([total[:rows, depth:], total[rows:, depth:]], axis=1)
    give(tall_new, tall, sums[:, :WIDTH], rate)
    same = lax.broadcasted_iota(jnp.int32, (rows, rows), 0) == lax.broadcasted_iota(
        jnp.int32, (rows, rows), 1
    )
    turned = [
        jnp.sum(jnp.where(same, sums[:, WIDTH + at : WIDTH + at + 1], 0.0), axis=0, keepdims=True)
        for at in range(2)
    ]
    give(hidden_new, hidden, jnp.concatenate(turned, axis=0), rate)
    spare = sums[:, PADDED - 128 : PADDED]
    start = BIAS_AT - (PADDED - 128)
    source = lax.broadcasted_iota(jnp.int32, (128, PADDED), 0)
    target = lax.broadcasted_iota(jnp.int32, (128, PADDED), 1)
    spread = jnp.dot(
        spare,
        jnp.where(source == start + target % 16, 1.0, 0.0),
        preferred_element_type=F32,
        precision=lax.Precision.HIGHEST,
    )
    row = lax.broadcasted_iota(jnp.int32, (rows, PADDED), 0)
    column = lax.broadcasted_iota(jnp.int32, (rows, PADDED), 1)
    line = jnp.sum(jnp.where(column // 16 == row, spread, 0.0), axis=0, keepdims=True)
    give(bias_new, bias, line[:, :WIDTH], 4.0)
    lane = lax.broadcasted_iota(jnp.int32, (rows, 128), 1) + (PADDED - 128)
    losses = jnp.where((lane >= LOSS_AT) & (lane < LOSS_AT + 3), spare, 0.0)
    loss[...] = jnp.sum(jnp.sum(losses, axis=1, keepdims=True), axis=0, keepdims=True)


def renew_small(terms, states, rate):
    states = [value for group in states for value in group]
    return pl.pallas_call(
        functools.partial(renew_small_kernel, rate, len(terms)),
        out_shape=tuple(jax.ShapeDtypeStruct(value.shape, F32) for value in states)
        + (jax.ShapeDtypeStruct((1, 1), F32),),
        in_specs=[vmem()] * (len(terms) + len(states)),
        out_specs=(vmem(),) * (len(states) + 1),
        compiler_params=limits(52),
        cost_estimate=lasting(2.0),
        name="renew_small",
    )(*terms, *states)


def map_sum_kernel(parts, own, *refs):
    passed, outs = refs[:parts], refs[parts:]
    ends = []
    for part in passed:
        ends.append((ends[-1] if ends else 0) + part.shape[0])
    start = 0
    for out in outs:
        end = start + out.shape[0]
        first = 0
        for part, last in zip(passed, ends):
            low, high = max(start, first), min(end, last)
            if low < high:
                out[low - start : high - start, :] = own[low:high, :] + part[
                    low - first : high - first, :
                ].astype(F32)
            first = last
        start = end


def map_sum(own, passed, maps):
    sizes = [level_map.shape[1] * level_map.shape[2] for level_map in maps]
    grads = pl.pallas_call(
        functools.partial(map_sum_kernel, len(passed)),
        out_shape=tuple(jax.ShapeDtypeStruct((size, own.shape[1]), F32) for size in sizes),
        in_specs=[vmem()] * (1 + len(passed)),
        out_specs=(vmem(),) * len(sizes),
        compiler_params=limits(52),
        cost_estimate=lasting(2.0),
        name="map_sum",
    )(own, *passed)
    return [grad.reshape(level_map.shape) for grad, level_map in zip(grads, maps)]


def gelu_parts(value):
    root = math.sqrt(2.0 / math.pi)
    square = value * value
    bend = jnp.tanh(root * (value + 0.044715 * square * value))
    half = 0.5 * (1.0 + bend)
    slope = half + 0.5 * value * (1.0 - bend * bend) * (
        root * (1.0 + 3.0 * 0.044715 * square)
    )
    return value * half, slope


def dot(left, right):
    return jnp.dot(left, right, preferred_element_type=F32)


def dot_last(left, right):
    return lax.dot_general(left, right, (((1,), (1,)), ((), ())), preferred_element_type=F32)


def middle_kernel(
    blocks,
    images,
    parts,
    order,
    *refs,
):
    pre_parts, refs = refs[: 2 * parts], refs[2 * parts :]
    middle_of(blocks, images, order, pre_parts, *refs)


def middle_of(
    blocks,
    images,
    order,
    pre_parts,
    second_turned_far,
    second_far,
    out_turned_far,
    out_weight,
    out_bias,
    slots,
    grad_own,
    grad_other,
    act_first,
    act_second,
    grad_second,
    grad_logits,
    losses,
    live_total,
    pre_first,
    slope_first,
    slope_second,
    grad_first,
    second_turned,
    second,
    out_turned,
    sems,
):
    copies = [
        pltpu.make_async_copy(source, target, sems.at[at])
        for at, (source, target) in enumerate(
            (
                (second_turned_far, second_turned),
                (out_turned_far, out_turned),
                (second_far, second),
            )
        )
    ]
    for copy in copies:
        copy.start()
    hidden, rows = pre_first.shape
    half = hidden // 2
    size = half // blocks
    own_start = order[3 * blocks] * half
    other_start = (1 - order[3 * blocks]) * half
    parts = len(pre_parts) // 2
    block = 0
    for own, other in zip(pre_parts[:parts], pre_parts[parts:]):
        for row in range(0, own.shape[0], size):
            at = pl.multiple_of(own_start + order[3 * blocks + 3 + block] * size, size)
            pre_first[pl.ds(at, size), :] = own[row : row + size, :]
            at = pl.multiple_of(other_start + order[3 * blocks + 3 + block] * size, size)
            pre_first[pl.ds(at, size), :] = other[row : row + size, :]
            block += 1
    spare = out_weight[:, PADDED - 128 : PADDED].astype(F32)
    at = WIDTH - (PADDED - 128)
    counted = 32.0 * spare[:, at + 2 : at + 3] + spare[:, at + 3 : at + 4]
    slots_total = jnp.sum(counted, axis=0, keepdims=True) * (images / hidden)
    live_total[...] = slots_total
    act, slope = gelu_parts(pre_first[...] + spare[:, at : at + 1])
    slope_first[...] = slope
    act_first[...] = act.astype(BF16)
    copies[0].wait()
    pre_second = (
        dot(second_turned[0], act_first[0:half, :])
        + dot(second_turned[1], act_first[half:hidden, :])
        + spare[:, at + 1 : at + 2]
    )
    act, slope = gelu_parts(pre_second)
    slope_second[...] = slope
    act_second[...] = act.astype(BF16)
    copies[1].wait()
    logits = dot(out_turned[...], act_second[...]) + out_bias[...]

    row = lax.broadcasted_iota(jnp.int32, logits.shape, 0)
    live = slots[0:1, :]
    scale = 1.0 / slots_total
    chosen = slots[2:3, :].astype(jnp.int32)
    foreground = jnp.where(chosen > 0, 1.0, 0.0)
    is_score = row < CLASSES
    top = jnp.max(jnp.where(is_score, logits, -jnp.inf), axis=0, keepdims=True)
    power = jnp.where(is_score, jnp.exp(logits - top), 0.0)
    total = jnp.sum(power, axis=0, keepdims=True)
    matches = row == chosen
    picked = jnp.sum(jnp.where(matches, logits, 0.0), axis=0, keepdims=True)
    value = jnp.log(total) + top - picked
    grad = power / total - jnp.where(matches, 1.0, 0.0)
    delta_row = CLASSES + 4 * (chosen - 1)
    smooth_total = jnp.zeros_like(live)
    for part in range(4):
        mine = (row == delta_row + part) & (chosen > 0)
        offset = jnp.sum(jnp.where(mine, logits, 0.0), axis=0, keepdims=True) - slots[
            3 + part : 4 + part, :
        ]
        size_of = jnp.abs(offset)
        near = size_of < SMOOTH
        smooth_total = smooth_total + jnp.where(
            near, 0.5 * offset * offset / SMOOTH, size_of - 0.5 * SMOOTH
        )
        slope = jnp.where(near, offset / SMOOTH, jnp.where(offset > 0.0, 1.0, -1.0))
        grad = jnp.where(mine, slope, grad)
    losses[...] = live * (value + foreground * smooth_total)
    grad_logits[...] = (grad * (live * scale)).astype(BF16)
    grad_second[...] = (dot(out_weight[...], grad_logits[...]) * slope_second[...]).astype(BF16)
    copies[2].wait()
    grad_first[...] = dot(second[...], grad_second[...]) * slope_first[...]
    for block in range(blocks):
        span = slice(block * size, (block + 1) * size)
        at = pl.multiple_of(own_start + order[block] * size, size)
        grad_own[span, :] = grad_first[pl.ds(at, size), :].astype(BF16)
        at = pl.multiple_of(other_start + order[block] * size, size)
        grad_other[span, :] = grad_first[pl.ds(at, size), :].astype(BF16)


def middle(blocks, images, order, pre_own, pre_other, *values):
    half, rows = (sum(part.shape[0] for part in pre_own), pre_own[0].shape[1])
    hidden = 2 * half
    low = lambda *shape: jax.ShapeDtypeStruct(shape, BF16)
    return pl.pallas_call(
        functools.partial(middle_kernel, blocks, images, len(pre_own)),
        out_shape=(
            low(half, rows),
            low(half, rows),
            low(hidden, rows),
            low(hidden, rows),
            low(hidden, rows),
            low(PADDED, rows),
            jax.ShapeDtypeStruct((1, rows), F32),
            jax.ShapeDtypeStruct((1, 1), F32),
        ),
        in_specs=[smem()]
        + [vmem()] * (2 * len(pre_own))
        + [pl.BlockSpec(memory_space=pl.ANY)] * 3
        + [vmem()] * (len(values) - 3),
        out_specs=(vmem(),) * 8,
        scratch_shapes=[pltpu.VMEM((hidden, rows), F32)] * 4
        + [pltpu.VMEM(value.shape, BF16) for value in values[:3]]
        + [pltpu.SemaphoreType.DMA((3,))],
        compiler_params=limits(52),
        cost_estimate=lasting(6.5),
        name="middle",
    )(order, *pre_own, *pre_other, *values)


def small_grads_kernel(
    blocks,
    parts,
    order,
    act_first,
    act_second,
    grad_second,
    grad_own,
    grad_other,
    grad_logits,
    losses,
    own,
    other,
    bias_out,
    second_sum,
    out_sum,
):
    hidden, rows = act_first.shape
    half = hidden // 2
    size = half // blocks
    section, fc, device = order[3 * blocks], order[3 * blocks + 1], order[3 * blocks + 2]
    for side in range(2):
        second_sum[side] = dot_last(
            grad_second[...], act_first[side * half : (side + 1) * half, :]
        ).astype(BF16)
    column = lax.broadcasted_iota(jnp.int32, (rows, PADDED), 1)
    value = dot_last(act_second[...], grad_logits[...])
    value = value + dot(grad_second[...], jnp.where(column == WIDTH + 1, 1.0, 0.0).astype(BF16))
    out_sum[...] = value
    ones = jnp.where(column == WIDTH, 1.0, 0.0).astype(BF16)
    for block in range(blocks):
        span = slice(block * size, (block + 1) * size)
        for values, where in ((grad_own, section), (grad_other, 1 - section)):
            at = pl.ds(pl.multiple_of(where * half + order[block] * size, size), size)
            out_sum[at, :] = out_sum[at, :] + dot(values[span, :], ones)
    bias = jnp.sum(grad_logits[...].astype(F32), axis=1, keepdims=True)
    bias_out[...] = bias
    part = size // 2
    if parts:
        tile = slice(PADDED - 128, PADDED)
        source = lax.broadcasted_iota(jnp.int32, (PADDED, 128), 0)
        target = lax.broadcasted_iota(jnp.int32, (PADDED, 128), 1) + (PADDED - 128)
        spread = jnp.where(target == BIAS_AT + source % 16, bias, 0.0).astype(BF16)
        row = lax.broadcasted_iota(jnp.int32, (hidden, PADDED), 0) % part
        pick = jnp.where(
            row == lax.broadcasted_iota(jnp.int32, (hidden, PADDED), 1) // 16, 1.0, 0.0
        ).astype(BF16)
        value = out_sum[:, tile] + dot(pick, spread)
        row = lax.broadcasted_iota(jnp.int32, (hidden, 128), 0) % part
        column = lax.broadcasted_iota(jnp.int32, (hidden, 128), 1) + (PADDED - 128)
        rest = jnp.sum(losses[...], axis=1, keepdims=True)
        for place in range(3):
            now = rest.astype(BF16).astype(F32)
            value = jnp.where((row == device) & (column == LOSS_AT + place), now, value)
            rest = rest - now
        out_sum[:, tile] = value
    for target, where in ((own, section), (other, 1 - section)):
        for near in range(2):
            lane = fc if near == 0 else 1 - fc
            for block in range(blocks):
                start = pl.multiple_of(where * half + order[blocks + block] * size, size)
                target[near, block * size : (block + 1) * size, 0:half] = second_sum[
                    lane, pl.ds(start, size), :
                ]
                at = pl.ds(pl.multiple_of(start + lane * part, part), part)
                for side in range(2):
                    target[
                        near,
                        block * size + side * part : block * size + (side + 1) * part,
                        half : half + PADDED // 2,
                    ] = out_sum[at, side * (PADDED // 2) : (side + 1) * (PADDED // 2)].astype(BF16)


def small_grads(
    blocks, parts, order, act_first, act_second, grad_second, grad_own, grad_other, grad_logits, losses
):
    hidden = act_first.shape[0]
    half = hidden // 2
    low = jax.ShapeDtypeStruct((2, half, half + PADDED // 2), BF16)
    return pl.pallas_call(
        functools.partial(small_grads_kernel, blocks, parts),
        out_shape=(low, low, jax.ShapeDtypeStruct((PADDED, 1), F32)),
        in_specs=[smem()] + [vmem()] * 7,
        out_specs=(vmem(),) * 3,
        scratch_shapes=[
            pltpu.VMEM((2, hidden, half), BF16),
            pltpu.VMEM((hidden, PADDED), F32),
        ],
        compiler_params=limits(52),
        cost_estimate=lasting(4.0),
        name="small_grads",
    )(order, act_first, act_second, grad_second, grad_own, grad_other, grad_logits, losses)


def assemble_kernel(blocks, order, *refs):
    sources, (second_turned, second, out_weight, out_turned) = refs[:-4], refs[-4:]
    hidden = second.shape[0]
    half = hidden // 2
    size = half // blocks
    part = size // 2
    section, fc = order[3 * blocks], order[3 * blocks + 1]
    first = 0
    for at in range(0, len(sources), 4):
        for index, source in enumerate(sources[at : at + 4]):
            where = section if index < 2 else 1 - section
            lane = fc if index % 2 == 0 else 1 - fc
            for block in range(source.shape[0] // size):
                rows = slice(block * size, (block + 1) * size)
                start = pl.multiple_of(
                    where * half + order[2 * blocks + first + block] * size, size
                )
                second_turned[lane, pl.ds(start, size), :] = source[rows, 0:half]
                target = pl.ds(pl.multiple_of(start + lane * part, part), part)
                for side in range(2):
                    out_weight[target, side * (PADDED // 2) : (side + 1) * (PADDED // 2)] = source[
                        block * size + side * part : block * size + (side + 1) * part,
                        half : half + PADDED // 2,
                    ]
        first += sources[at].shape[0] // size
    for side in range(2):
        second[side * half : (side + 1) * half, :] = jnp.transpose(second_turned[side])
    out_turned[...] = jnp.transpose(out_weight[...])


def assemble(blocks, order, groups):
    sources = [source for group in groups for source in group]
    half = sum(group[0].shape[0] for group in groups)
    hidden = 2 * half
    low = lambda *shape: jax.ShapeDtypeStruct(shape, BF16)
    return pl.pallas_call(
        functools.partial(assemble_kernel, blocks),
        out_shape=(low(2, hidden, half), low(hidden, hidden), low(hidden, PADDED), low(PADDED, hidden)),
        in_specs=[smem()] + [vmem()] * len(sources),
        out_specs=(vmem(),) * 4,
        compiler_params=limits(52),
        cost_estimate=lasting(5.0),
        name="assemble",
    )(order, *sources)


def lane_blocks(lanes):
    for parts in (7, 1):
        if lanes % (128 * parts) == 0:
            return parts, lanes // parts


def join_kernel(straight, passed_head, crossed, passed_tail, moving, cross):
    half = straight.shape[0] // 2
    moving[0:half, :] = (
        straight[0:half, :].astype(F32) + passed_head[...].astype(F32)
    ).astype(BF16)
    moving[half : 2 * half, :] = straight[half : 2 * half, :]
    cross[0:half, :] = crossed[0:half, :]
    cross[half : 2 * half, :] = (
        crossed[half : 2 * half, :].astype(F32) + passed_tail[...].astype(F32)
    ).astype(BF16)


def join(straight, passed_head, blocks, at, passed_tail):
    held, lanes = straight.shape
    return pl.pallas_call(
        join_kernel,
        out_shape=(jax.ShapeDtypeStruct(straight.shape, BF16),) * 2,
        grid=(1,),
        in_specs=[
            pl.BlockSpec((held, lanes), lambda step: (0, 0)),
            pl.BlockSpec((held // 2, lanes), lambda step: (0, 0)),
            pl.BlockSpec((held, lanes), lambda step: (at, 0)),
            pl.BlockSpec((held // 2, lanes), lambda step: (0, 0)),
        ],
        out_specs=(pl.BlockSpec((held, lanes), lambda step: (0, 0)),) * 2,
        compiler_params=limits(52),
        cost_estimate=lasting(1.5),
        name="join",
    )(straight, passed_head, blocks, passed_tail)


def input_grad_kernel(count, grad, *refs):
    weight = jnp.concatenate([ref[...] for ref in refs[:count]], axis=0)
    value = dot(grad[...], weight).astype(BF16)
    start = 0
    for out in refs[count:]:
        out[...] = value[start : start + out.shape[0]]
        start += out.shape[0]


def input_grad(grad, pieces, sizes, lanes):
    parts, size = lane_blocks(lanes)
    return pl.pallas_call(
        functools.partial(input_grad_kernel, len(pieces)),
        out_shape=tuple(jax.ShapeDtypeStruct((rows, lanes), BF16) for rows in sizes),
        grid=(parts,),
        in_specs=[pl.BlockSpec(grad.shape, lambda step: (0, 0))]
        + [pl.BlockSpec((piece.shape[0], size), lambda step: (0, step)) for piece in pieces],
        out_specs=tuple(pl.BlockSpec((rows, size), lambda step: (0, step)) for rows in sizes),
        compiler_params=limits(52),
        cost_estimate=lasting(5.0),
        name="input_grad",
    )(grad, *pieces)


def line_order(line):
    return (0, 1, 3, 2) if line == 4 else tuple(range(line))


def pair_swap(value, count):
    return lax.ppermute(value, "wide", [(at, at ^ 1) for at in range(count)])


def line_step(value, count, way=1):
    places = line_order(count // 2)
    steps = []
    for at, place in enumerate(places):
        target = places[(at + way) % len(places)]
        steps += [(2 * place + side, 2 * target + side) for side in range(2)]
    return lax.ppermute(value, "wide", sorted(steps))


def line_swap(value, count, bit):
    return lax.ppermute(value, "wide", [(at, at ^ (2 * bit)) for at in range(count)])


def swap(value, axis):
    return lax.ppermute(value, axis, [(0, 1), (1, 0)])


def together(*values):
    return lax.optimization_barrier(values)


def add(*terms):
    total = terms[0].astype(F32)
    for term in terms[1:]:
        total = total + term.astype(F32)
    return total.astype(BF16)


def ring_order(wide, line):
    places = line_order(line)
    here = sum((jnp.where(wide // 2 == place, at, 0) for at, place in enumerate(places)))
    table = lambda index: sum(
        (jnp.where(index == at, place, 0) for at, place in enumerate(places))
    )
    return [
        table((here - step) % line) * 2 + ((wide % 2) ^ side)
        for side in range(2)
        for step in range(line)
    ]


def swap_order(wide, line):
    return [
        ((wide // 2) ^ step) * 2 + ((wide % 2) ^ side) for side in range(2) for step in range(line)
    ]


def split_tall(terms, n_wide):
    sections, places, half, columns = terms.shape
    held = half // n_wide
    second = terms[..., : columns - PADDED // 2].reshape(sections, places, n_wide, held, -1)
    out = terms[..., columns - PADDED // 2 :].reshape(sections, places, 2, half // 2, PADDED // 2)
    out = jnp.transpose(out, (0, 1, 3, 2, 4)).reshape(sections, half, PADDED)
    out = out.reshape(sections, n_wide, places, held // places, 2, PADDED // 2)
    out = jnp.transpose(out, (0, 2, 1, 4, 3, 5)).reshape(sections, places, n_wide, held, -1)
    return jnp.concatenate([second, out], axis=-1)


def body(
    map_p2,
    map_p3,
    map_p4,
    map_p5,
    boxes,
    levels,
    classes,
    sampled,
    counts,
    targets,
    first_weight,
    second_weight,
    out_weight,
    hidden_bias,
    out_bias,
    first_moment,
    second_moment,
    out_moment,
    hidden_moment,
    bias_moment,
    first_average,
    second_average,
    out_average,
    hidden_average,
    bias_average,
):
    n_section = lax.axis_size("section")
    n_fc = lax.axis_size("fc")
    n_wide = lax.axis_size("wide")
    section = lax.axis_index("section")
    fc = lax.axis_index("fc")
    wide = lax.axis_index("wide")
    everywhere = ("section", "wide", "fc")
    maps = [map_p2, map_p3, map_p4, map_p5]
    channels = map_p2.shape[3]
    height = map_p2.shape[1] * n_section
    width = map_p2.shape[2]
    rows_dev = boxes.shape[0]
    rows_own = rows_dev // (n_section * n_fc)
    held = first_weight.shape[1]
    classes_out = out_weight.shape[1]
    place = section.astype(jnp.int32).reshape(1)

    ring = n_wide == 8
    line = n_wide // 2
    rows_tall = out_weight.shape[0]
    rows_fc = n_section * rows_own
    half_held = held // 2
    lanes = first_weight.shape[0]

    place = jnp.stack([section, fc]).astype(jnp.int32)

    turned = turn_weight(
        counts, first_weight.T, sampled, second_weight.T, out_weight, hidden_bias
    )
    slot_parts = (counts, boxes, levels, classes, sampled, targets)
    turned, maps, slot_parts = together(turned, maps, slot_parts)
    if ring:
        places = ring_order(wide, line)
        small_at = [0, 1, 3, 4, 2, 5, 7, 6]
        order = jnp.stack(
            places
            + swap_order(wide, line)
            + [places[at] for at in small_at]
            + [section, fc, (section * n_wide + wide) * n_fc + fc]
            + [places[at] for at in (0, 1, 2, 4, 5, 3, 6, 7)]
        ).astype(jnp.int32)
        blocks = n_wide
        straight = [turned, line_step(turned, n_wide)]
        crossed = [pair_swap(turned, n_wide)]
        last_small = line_step(turned[:, lanes:], n_wide, -1)
    else:
        zero = jnp.zeros_like(section)
        order = jnp.stack([zero, zero, zero, section, fc, zero, zero]).astype(jnp.int32)
        blocks = 1
    half_own = jnp.concatenate([level_map.reshape(-1, channels) for level_map in maps], axis=0)
    half_other = swap(half_own, "section")
    *parameters, slots = plan(place, *slot_parts, n_fc * rows_own, height, width)
    table = build_table(place, half_own, half_other, height, width)

    crops_mine = crop_forward(parameters, table, 0, rows_own)
    if ring:
        straight[1], crossed[0], last_small, table, crops_mine = together(
            straight[1], crossed[0], last_small, table, crops_mine
        )
        small_of = lambda piece: piece[:, lanes:]
        small_a = jnp.concatenate(
            [small_of(straight[0]), small_of(straight[1]), last_small, small_of(crossed[0])], axis=0
        )
        straight.append(line_step(straight[1], n_wide))
        crossed.append(pair_swap(straight[1], n_wide))
        last_crossed = pair_swap(last_small, n_wide)
        passed_a = swap(small_a, "fc")
    passed_mine = swap(crops_mine, "section")
    crops_theirs = crop_forward(parameters, table, rows_own, rows_own)

    if ring:
        straight[2], crossed, last_crossed, passed_mine, crops_theirs, small_a, passed_a = together(
            straight[2], crossed, last_crossed, passed_mine, crops_theirs, small_a, passed_a
        )
        straight.append(line_step(straight[2], n_wide))
        crossed.append(pair_swap(straight[2], n_wide))
        small_b = jnp.concatenate(
            [small_of(straight[2]), small_of(crossed[1]), last_crossed], axis=0
        )
        passed_b = swap(small_b, "fc")
        passed_theirs = swap(crops_theirs, "section")
        weight_of = lambda piece: piece[:, :lanes]
        early_weight = jnp.concatenate(
            [weight_of(piece) for piece in straight[:3] + crossed[:2]], axis=0
        )
        inputs_all = jnp.concatenate([crops_mine, passed_mine, crops_theirs, passed_theirs], axis=0)
        early = dot_last(early_weight, inputs_all)
        early, early_passed = early[:, :rows_fc], swap(early[:, rows_fc:].astype(BF16), "fc")
        straight[3], crossed[2], inputs_all, early, small_b, passed_b = together(
            straight[3], crossed[2], inputs_all, early, small_b, passed_b
        )
        tail = [
            pair_swap(straight[3][:half_held, :lanes], n_wide),
            line_step(crossed[2][half_held:, :lanes], n_wide),
        ]
        small_c = small_of(crossed[2])
        late = dot_last(
            jnp.concatenate([weight_of(straight[3]), weight_of(crossed[2])], axis=0), inputs_all
        )
        passed_c = swap(small_c, "fc")
        groups = [
            [small, passed, swap(small, "section"), swap(passed, "section")]
            for small, passed in ((small_a, passed_a), (small_b, passed_b))
        ]
        early = early + early_passed.astype(F32)
        tail, late, early, passed_c, inputs_all = together(tail, late, early, passed_c, inputs_all)
        last = jnp.concatenate(tail, axis=0)
        end = dot_last(last, inputs_all)
        late, late_passed = late[:, :rows_fc], swap(late[:, rows_fc:].astype(BF16), "fc")
        early_other = swap(early[:, rows_own:], "section")
        end_passed = end[:, rows_fc:].astype(BF16)
        end_passed, end, early, early_other, late, late_passed, groups = together(
            end_passed, end, early, early_other, late, late_passed, groups
        )
        end_passed = swap(end_passed, "fc")
        late = late + late_passed.astype(F32)
        late_other = swap(late[:, rows_own:], "section")
        groups.append([small_c, passed_c, swap(small_c, "section"), swap(passed_c, "section")])
        small_weights = assemble(blocks, order, groups)
        end_passed, small_weights, late, late_other = together(
            end_passed, small_weights, late, late_other
        )
        w_second_turned, w_second, w_out, w_out_turned = small_weights
        end = end[:, :rows_fc] + end_passed.astype(F32)
        end_other = swap(end[:, rows_own:], "section")
        pre_own = [part[:, :rows_own] for part in (early, late, end)]
        pre_other = [early_other, late_other, end_other]
        pieces = straight + crossed + [last]
    else:
        passed_theirs = swap(crops_theirs, "section")
        inputs_all = jnp.concatenate([crops_mine, passed_mine, crops_theirs, passed_theirs], axis=0)
        pieces = [lax.all_gather(turned[:, :lanes], "wide", axis=0, tiled=True)]
        pre = dot_last(pieces[0], inputs_all)
        pre = pre[:, :rows_fc] + swap(pre[:, rows_fc:], "fc")
        pre_own, pre_other = [pre[:, :rows_own]], [swap(pre[:, rows_own:], "section")]
        small = lax.all_gather(turned[:, lanes:], everywhere, axis=0, tiled=True)
        small = small.reshape(-1, n_fc, held, turned.shape[1] - lanes)
        w_second_turned = jnp.transpose(
            small[..., : second_weight.shape[0]], (1, 0, 2, 3)
        ).reshape(n_fc, -1, second_weight.shape[0])
        w_second = jnp.transpose(w_second_turned, (0, 2, 1)).reshape(
            -1, w_second_turned.shape[1]
        )
        w_out = small[..., second_weight.shape[0] :].reshape(-1, 2, rows_tall, PADDED // 2)
        w_out = jnp.transpose(w_out, (0, 2, 1, 3)).reshape(-1, PADDED)
        w_out_turned = w_out.T
    grad_own, grad_other, act_first, act_second, grad_second, grad_logits, losses, total = middle(
        blocks,
        n_wide,
        order,
        pre_own,
        pre_other,
        w_second_turned,
        w_second,
        w_out_turned,
        w_out,
        jnp.pad(out_bias, (0, PADDED - classes_out))[:, None],
        slots,
    )
    grad_passed = swap(grad_other, "section")
    grad_passed, grad_own, act_first = together(grad_passed, grad_own, act_first)
    grad_mine = jnp.concatenate([grad_own, grad_passed], axis=1)
    rate = 0.15 * math.sqrt(rows_dev * n_wide)
    back = lambda sent: swap(sent, "section")

    if ring:
        def all_slots(parts):
            mine = jnp.concatenate([grad_mine[at * held : (at + 1) * held] for at in parts], axis=0)
            return jnp.concatenate([mine, swap(mine, "fc")], axis=1)

        def block(values, at):
            return values[at * held : (at + 1) * held]

        rest_at = [0, 2, 3, line, line + 2, line + 3]
        first_grads = all_slots([1, line + 1])
        terms_own, terms_other, bias_terms = small_grads(
            blocks, True, order, act_first, act_second, grad_second, grad_own, grad_other, grad_logits, losses
        )
        first_grads, terms_own, terms_other = together(first_grads, terms_own, terms_other)
        first_terms = dot(first_grads, inputs_all).astype(BF16)
        rest_grads = all_slots(rest_at)
        first_terms, rest_grads, terms_other = together(first_terms, rest_grads, terms_other)
        moving, cross = block(first_terms, 0), block(first_terms, 1)
        tail = line_step(cross[half_held:], n_wide)
        head = pair_swap(cross[:half_held], n_wide)
        small = swap(terms_other, "section")
        rest = dot(rest_grads, inputs_all).astype(BF16)
        small = [add(terms_own[at], small[at]) for at in range(n_fc)]
        tail, head, rest, small, first_grads, rest_grads = together(
            tail, head, rest, small, first_grads, rest_grads
        )

        moving, cross = join(moving, head, rest, 4, tail)
        moving, cross, rest_grads = together(moving, cross, rest_grads)
        cross = pair_swap(cross, n_wide)
        moving = line_step(moving, n_wide)
        small_passed = swap(small[1], "fc")
        grad_all = jnp.concatenate(
            [
                block(rest_grads, 0),
                first_grads[:held],
                rest_grads[held : 3 * held],
                block(rest_grads, 3),
                first_grads[held:],
                rest_grads[4 * held :],
            ],
            axis=0,
        )
        keep_mine, send_mine, keep_theirs, send_theirs = input_grad(
            grad_all.T, pieces, [rows_own] * 4, lanes
        )
        sent_later = [block(rest, 5), block(rest, 3)]
        moving, cross, rest, sent_later, keep_mine, keep_theirs, send_mine, send_theirs, small_passed = together(
            moving, cross, rest, sent_later, keep_mine, keep_theirs, send_mine, send_theirs, small_passed
        )

        back_mine = [back(send_mine)]
        moving = add(block(rest, 1), cross, moving)
        moving, keep_mine = together(moving, keep_mine)
        moving = line_step(moving, n_wide)
        cross = pair_swap(sent_later[0], n_wide)
        before = crop_backward(place, parameters, keep_mine, back_mine, 0, height, width)
        small = add(small[0], small_passed)
        moving, cross, rest, sent_later, before, keep_theirs, send_theirs, small = together(
            moving, cross, rest, sent_later, before, keep_theirs, send_theirs, small
        )

        back_theirs = [back(send_theirs)]
        moving = add(block(rest, 2), cross, moving)
        moving, before = together(moving, before)
        moving = line_step(moving, n_wide)
        cut = small.shape[0] // 2
        cross = pair_swap(sent_later[1], n_wide)
        small_passed = pair_swap(small[cut:], n_wide)
        map_own, map_other = crop_backward(
            place, parameters, keep_theirs, back_theirs, rows_own, height, width, before
        )
        small_passed, map_own, map_other = together(small_passed, map_own, map_other)
        small = add(small[:cut], small_passed)
        small_terms = [small[:held]] + [
            line_swap(small[bits * held : (bits + 1) * held], n_wide, bits)
            for bits in range(1, line)
        ]
        cut = map_other.shape[0] // (2 * GROUP) * GROUP
        map_passed = [swap(map_other[:cut], "section"), swap(map_other[cut:], "section")]
        map_grads = map_sum(map_own, map_passed, maps)
        moving, cross, map_grads = together(moving, cross, map_grads)
        first_sums = [block(rest, 0), cross, moving]
    else:
        grad_all = jnp.concatenate([grad_mine, swap(grad_mine, "fc")], axis=1)
        first_sums = [
            lax.psum_scatter(
                dot(grad_all, inputs_all).astype(BF16), "wide", scatter_dimension=0, tiled=True
            )
        ]
        keep_mine, send_mine, keep_theirs, send_theirs = input_grad(
            grad_all.T, pieces, [rows_own] * 4, lanes
        )
        before = crop_backward(place, parameters, keep_mine, [back(send_mine)], 0, height, width)
        map_own, map_other = crop_backward(
            place, parameters, keep_theirs, [back(send_theirs)], rows_own, height, width, before
        )
        map_grads = map_sum(map_own, [swap(map_other, "section")], maps)
        terms_own, terms_other, bias_terms = small_grads(
            blocks, False, order, act_first, act_second, grad_second, grad_own, grad_other, grad_logits, losses
        )
        terms = jnp.stack(
            [jnp.where(section == at, terms_own, terms_other) for at in range(n_section)]
        )
        terms = jnp.where(fc == 0, terms, terms[:, ::-1])
        terms = jnp.transpose(split_tall(terms, n_wide), (0, 2, 1, 3, 4))
        small_sum = lax.psum_scatter(
            terms.reshape(-1, terms.shape[-1]), everywhere, scatter_dimension=0, tiled=True
        ).astype(F32)
    first_out = renew_first(first_sums, first_weight.T, first_moment.T, first_average.T, rate)
    if ring:
        first_out, small_terms = together(first_out, small_terms)
        small_out = renew_small(
            small_terms,
            (
                (second_weight.T, second_moment.T, second_average.T),
                (out_weight, out_moment, out_average),
                (hidden_bias.T, hidden_moment.T, hidden_average.T),
                (out_bias[None], bias_moment[None], bias_average[None]),
            ),
            rate,
        )
        *small_out, loss_sum = small_out
        loss_sum = loss_sum[0, 0]
        second_out = [value.T for value in small_out[:3]]
        out_out, hidden_out = small_out[3:6], [value.T for value in small_out[6:9]]
        bias_out = [value[0] for value in small_out[9:]]
    else:
        second_sum = small_sum[:, : second_weight.shape[0]]
        tall_sum = small_sum[:, second_weight.shape[0] :]
        tall_sum = jnp.concatenate([tall_sum[:rows_tall], tall_sum[rows_tall:]], axis=1)
        vector = jnp.concatenate([bias_terms[:classes_out, 0], jnp.sum(losses).reshape(1)])
        vector = lax.psum(vector, everywhere)
        loss_sum = vector[classes_out]
        second_out = renew(second_weight, second_moment, second_average, second_sum.T, rate)
        out_out = renew(out_weight, out_moment, out_average, tall_sum[:, :classes_out], rate)
        hidden_out = renew(
            hidden_bias,
            hidden_moment,
            hidden_average,
            tall_sum[:, classes_out : classes_out + 2],
            rate,
        )
        bias_out = renew(out_bias, bias_moment, bias_average, vector[:classes_out], 4.0)
    return (
        loss_sum,
        total[0, 0],
        map_grads[0],
        map_grads[1],
        map_grads[2],
        map_grads[3],
        first_out[0].T,
        first_out[1].T,
        first_out[2].T,
        *second_out,
        *out_out,
        *hidden_out,
        *bias_out,
    )


def solution(mesh):
    maps = P("wide", "section", None, "fc")
    wide_weight = P("fc", ("section", "wide"))
    tall_weight = P(("section", "wide", "fc"), None)
    in_specs = (
        (maps,) * 4
        + (P("wide", None), P("wide"), P("wide"), P("wide"), P("wide"), P("wide", None))
        + (wide_weight, wide_weight, tall_weight, tall_weight, P()) * 3
    )
    out_specs = (
        (P(), P())
        + (maps,) * 4
        + (wide_weight,) * 6
        + (tall_weight,) * 6
        + (P(),) * 3
    )
    return jax.shard_map(body, mesh=mesh, in_specs=in_specs, out_specs=out_specs, check_vma=False)
```

```python
import functools
import math

import jax
import jax.numpy as jnp
from jax import lax
from jax.experimental import pallas as pl
from jax.experimental.pallas import tpu as pltpu
from jax.sharding import PartitionSpec as P

CLASSES = 81
BINS = 7
CELLS = BINS * BINS
WINDOW = 24
WINDOWS = (24, 16, 8)
GROUP = 16
CHAINS = 2
SETS = 8
PADDED = 512
WIDTH = 5 * CLASSES - 4
BIAS_AT = 416
LOSS_AT = 448
MOMENTUM = 0.9
AVERAGE = 0.7
DECAY = 0.0001
SMOOTH = 0.5

F32 = jnp.float32
BF16 = jnp.bfloat16


def smem():
    return pl.BlockSpec(memory_space=pltpu.SMEM)


def vmem():
    return pl.BlockSpec(memory_space=pltpu.VMEM)


def lasting(microseconds):
    return pl.CostEstimate(
        flops=0, bytes_accessed=int(microseconds * 1e3), transcendentals=0
    )


def limits(mebibytes):
    return pltpu.CompilerParams(vmem_limit_bytes=mebibytes * 2**20)


def level_plan(height, width):
    shapes = [(height >> depth, width >> depth) for depth in range(4)]
    strides = [max(rows, WINDOW) for rows, cols in shapes]
    bases = [0]
    for depth in range(4):
        bases.append(bases[-1] + strides[depth] * shapes[depth][1])
    total = -(-(bases[-1] + 2 * WINDOW) // GROUP) * GROUP
    return shapes, strides, bases[:4], total


def half_starts(shapes):
    starts = [0]
    for rows, cols in shapes:
        starts.append(starts[-1] + rows // 2 * cols)
    return starts


def table_kernel(height, width, place, own, other, table):
    shapes, strides, bases, total = level_plan(height, width)
    starts = half_starts(shapes)
    table[...] = jnp.zeros_like(table)

    def fill(source, bottom):
        for depth, (rows, cols) in enumerate(shapes):
            half = rows // 2

            def column(x, carry, depth=depth, half=half, cols=cols):
                cells = source[pl.ds(starts[depth] + x, half, stride=cols), :]
                table[pl.ds(bases[depth] + x * strides[depth] + bottom * half, half), :] = cells
                return carry

            lax.fori_loop(0, cols, column, 0, unroll=4)

    bottom = place[0]
    fill(own, bottom)
    fill(other, 1 - bottom)


def build_table(place, own, other, height, width):
    total = level_plan(height, width)[3]
    return pl.pallas_call(
        functools.partial(table_kernel, height, width),
        out_shape=jax.ShapeDtypeStruct((total, own.shape[1]), F32),
        in_specs=[smem(), vmem(), vmem()],
        out_specs=vmem(),
        compiler_params=limits(52),
        cost_estimate=lasting(5.0),
        name="build_table",
    )(place, own, other)


def plan_kernel(
    height,
    width,
    place,
    counts,
    boxes,
    levels,
    classes,
    sampled,
    targets,
    address,
    weight,
    row_values,
    stride,
    slots,
    features,
):
    shapes, strides, bases, total = level_plan(height, width)
    count = boxes.shape[1]
    own = address.shape[1]
    share = own // 2
    section, fc = place[0], place[1]
    lane = lax.broadcasted_iota(jnp.int32, (1, count), 1)
    live = (lane < counts[0]) & (sampled[...] > 0)
    key = (jnp.where(live, levels[...], 4) * count + lane).astype(F32)
    across = jnp.broadcast_to(key, (128, count))
    down = jnp.transpose(across)
    before = jnp.zeros((count, 128), F32)
    for start in range(0, count, 128):
        before = before + jnp.where(key[:, start : start + 128] < down, 1.0, 0.0)
    rank = jnp.sum(before, axis=1, keepdims=True).astype(jnp.int32)
    seat = rank // 2
    side = jnp.where(seat % 2 == fc, 0, share)
    seat = jnp.where(rank % 2 == section, seat // 2 + side, -1)
    deal = jnp.where(
        jnp.broadcast_to(seat, (count, own)) == lax.broadcasted_iota(jnp.int32, (count, own), 1),
        1.0,
        0.0,
    )
    features[...] = jnp.zeros_like(features)
    features[0:4, :] = boxes[...]
    features[4:8, :] = targets[...]
    features[8:9, :] = levels[...].astype(F32)
    features[9:10, :] = classes[...].astype(F32)
    features[10:11, :] = jnp.where(live, 1.0, 0.0)
    dealt = jnp.dot(
        features[...], deal, preferred_element_type=F32, precision=lax.Precision.HIGHEST
    )
    slots[...] = jnp.zeros_like(slots)
    slots[0:1, :] = dealt[10:11, 0:share]
    slots[2:3, :] = dealt[9:10, 0:share]
    slots[3:7, :] = dealt[4:8, 0:share]
    level = (dealt[8:9, :] + 0.5).astype(jnp.int32)

    def choose(values, kind):
        out = jnp.full(level.shape, values[3], kind)
        for depth in range(3):
            out = jnp.where(level == depth, jnp.asarray(values[depth], kind), out)
        return out

    reach_y = choose([h - 1 for h, w in shapes], F32)
    reach_x = choose([w - 1 for h, w in shapes], F32)
    step = choose(strides, jnp.int32)
    base = choose(bases, jnp.int32)
    top = (dealt[0:1, :] - 0.25 * dealt[2:3, :]) * reach_y
    length_y = 0.5 * dealt[2:3, :] * reach_y
    left = (dealt[1:2, :] - 0.25 * dealt[3:4, :]) * reach_x
    length_x = 0.5 * dealt[3:4, :] * reach_x
    first = jnp.clip(jnp.floor(top + length_y * (0.25 / 7.0)), 0.0, reach_y - 1.0)
    start = base + first.astype(jnp.int32)
    for at in range(2 * BINS):
        points = left + length_x * ((at // 2 + (at % 2 + 0.5) * 0.5) / 7.0)
        lower = jnp.clip(jnp.floor(points), 0.0, reach_x - 1.0)
        address[at : at + 1, :] = start + lower.astype(jnp.int32) * step
        weight[at : at + 1, :] = points - lower
    for at, value in enumerate((top, length_y, first, reach_y - 1.0)):
        row_values[at : at + 1, :] = value
    stride[0:1, :] = step
    stride[1:2, :] = jnp.where(dealt[10:11, :] > 0.5, choose([3, 2, 1, 1], jnp.int32), 0)


def plan(place, counts, boxes, levels, classes, sampled, targets, own, height, width):
    whole = jax.ShapeDtypeStruct
    count = boxes.shape[0]
    return pl.pallas_call(
        functools.partial(plan_kernel, height, width),
        out_shape=(
            whole((2 * BINS, own), jnp.int32),
            whole((2 * BINS, own), F32),
            whole((4, own), F32),
            whole((2, own), jnp.int32),
            whole((8, own // 2), F32),
        ),
        in_specs=[smem()] * 2 + [vmem()] * 5,
        out_specs=(vmem(),) * 5,
        scratch_shapes=[pltpu.VMEM((16, count), F32)],
        compiler_params=limits(52),
        cost_estimate=lasting(3.0),
        name="plan",
    )(place, counts, boxes.T, levels[None], classes[None], sampled[None], targets.T)


def row_weights(values, index, offset):
    top, length, first, last = values
    total = None
    for place in (0.25, 0.75):
        points = top + length * ((index + place) / 7.0)
        lower = jnp.minimum(jnp.maximum(jnp.floor(points), 0.0), last)
        upper_weight = points - lower
        distance = offset - (lower - first)
        part = jnp.where(
            distance == 0.0, 1.0 - upper_weight, jnp.where(distance == 1.0, upper_weight, 0.0)
        )
        total = part if total is None else total + part
    return total * 0.25


def crop_kernel(rows, first, address, weight, row_values, stride, table, out, turned):
    def crops(window, step):
        depth = -(-BINS * window // 128) * 128
        lane = lax.broadcasted_iota(jnp.int32, (8, depth), 1)
        offset = (lane % window).astype(F32)
        index = lax.broadcasted_iota(jnp.int32, (8, depth), 0).astype(F32)
        inside = (
            lax.broadcasted_iota(jnp.int32, (8 * BINS, depth), 0) // 8
            == lax.broadcasted_iota(jnp.int32, (8 * BINS, depth), 1) // window
        )

        for part in range(GROUP):
            row = first + step * GROUP + part
            weights = row_weights([row_values[at, row] for at in range(4)], index, offset)
            left = jnp.where(inside, jnp.concatenate([weights] * BINS, axis=0), 0.0)
            step_x = stride[0, row]
            columns = []
            for k in range(BINS):
                total = None
                for m in range(2):
                    place = address[2 * k + m, row]
                    upper = weight[2 * k + m, row]
                    near = table[pl.ds(place, window), :]
                    far = table[pl.ds(place + step_x, window), :]
                    value = near + upper * (far - near)
                    total = value if total is None else total + value
                columns.append(total)
            columns.append(jnp.zeros((depth - BINS * window, 128), F32))
            right = jnp.concatenate(columns, axis=0).astype(BF16)
            crop = jnp.dot(left.astype(BF16), right, preferred_element_type=F32)
            for k in range(BINS):
                turned[pl.ds(part + k * BINS * GROUP, BINS, stride=GROUP), :] = crop[
                    8 * k : 8 * k + BINS
                ]

    def group(step, carry):
        start = pl.multiple_of(step * GROUP, GROUP)
        eights = stride[1, first + step * GROUP]
        for window in WINDOWS:

            @pl.when(eights == window // 8)
            def live_slots(window=window):
                crops(window, step)

        @pl.when(eights > 0)
        def store():
            for cell in range(CELLS):
                out[pl.ds(start, GROUP), cell * 128 : (cell + 1) * 128] = turned[
                    cell * GROUP : (cell + 1) * GROUP, :
                ].astype(BF16)

        @pl.when(eights == 0)
        def dead_slots():
            out[pl.ds(start, GROUP), :] = jnp.zeros((GROUP, CELLS * 128), BF16)

        return carry

    lax.fori_loop(0, rows // GROUP, group, 0)


def crop_forward(parameters, table, first, rows):
    return pl.pallas_call(
        functools.partial(crop_kernel, rows, first),
        out_shape=jax.ShapeDtypeStruct((rows, CELLS * 128), BF16),
        in_specs=[smem()] * 4 + [vmem()],
        out_specs=vmem(),
        scratch_shapes=[pltpu.VMEM((CELLS * GROUP, 128), F32)],
        compiler_params=limits(52),
        cost_estimate=lasting(0.07 * rows),
        name="crop_forward",
    )(*parameters, table)


def spread_kernel(
    rows, first, height, width, last, parts, place, address, weight, row_values, stride, keep, *refs
):
    shapes, strides, bases, total = level_plan(height, width)
    starts = half_starts(shapes)
    passed_parts, refs = refs[:parts], refs[parts:]
    if last:
        before, own, other, passed, turned, half, *tables = refs
    else:
        out, passed, turned, *tables = refs
    size = rows // parts
    for at, part in enumerate(passed_parts):
        passed[at * size : (at + 1) * size, :] = part[...]
    for table in tables[1 if last else 0 :]:
        table[...] = jnp.zeros_like(table)
    if last:
        tables[0][...] = before[...]
    turned[pl.ds(CELLS * GROUP, GROUP), :] = jnp.zeros((GROUP, 128), F32)

    def spread(window, base, few):
        index = (lax.broadcasted_iota(jnp.int32, (window, 128), 1) % 8).astype(F32)
        offset = lax.broadcasted_iota(jnp.int32, (window, 128), 0).astype(F32)
        long_row = lax.broadcasted_iota(jnp.int32, (BINS * window, 128), 0)
        long_lane = lax.broadcasted_iota(jnp.int32, (BINS * window, 128), 1)
        inside = (long_row // window == long_lane // 8) & (long_lane % 8 < BINS)
        results = []
        for at in range(SETS * CHAINS):
            part = few * SETS * CHAINS + at
            row = base + at
            weights = row_weights([row_values[at, row] for at in range(4)], index, offset)
            left = jnp.where(inside, jnp.concatenate([weights] * BINS, axis=0), 0.0).astype(BF16)
            pieces = [
                turned[pl.ds(part + k * BINS * GROUP, 8, stride=GROUP), :] for k in range(BINS)
            ]
            pieces.append(jnp.zeros((128 - 8 * BINS, 128), F32))
            right = jnp.concatenate(pieces, axis=0).astype(BF16)
            results.append(jnp.dot(left, right, preferred_element_type=F32))
        for head in range(0, SETS * CHAINS, CHAINS):
            for k in range(BINS):
                for m in range(2):
                    for chain in range(CHAINS):
                        row = base + head + chain
                        table = tables[chain]
                        at = address[2 * k + m, row]
                        next_at = at + stride[0, row]
                        value = results[head + chain][k * window : (k + 1) * window]
                        upper = value * weight[2 * k + m, row]
                        near = table[pl.ds(at, window), :] + (value - upper)
                        far = table[pl.ds(next_at, window), :] + upper
                        table[pl.ds(at, window), :] = near
                        table[pl.ds(next_at, window), :] = far

    def group(step, carry):
        start = pl.multiple_of(step * GROUP, GROUP)

        @pl.when(stride[1, first + step * GROUP] > 0)
        def live_slots():
            for cell in range(CELLS):
                span = slice(cell * 128, (cell + 1) * 128)
                turned[cell * GROUP : (cell + 1) * GROUP, :] = keep[
                    pl.ds(start, GROUP), span
                ].astype(F32) + passed[pl.ds(start, GROUP), span].astype(F32)

            def some(few, carry):
                base = first + step * GROUP + few * SETS * CHAINS
                eights = stride[1, base]
                for window in WINDOWS:

                    @pl.when(eights == window // 8)
                    def one_window(window=window):
                        spread(window, base, few)

                return carry

            lax.fori_loop(0, GROUP // (SETS * CHAINS), some, 0)

        return carry

    lax.fori_loop(0, rows // GROUP, group, 0)
    result = tables[0] if last else out

    def summed(step, carry):
        span = pl.ds(pl.multiple_of(step * GROUP, GROUP), GROUP)
        value = tables[0][span, :]
        for table in tables[1:]:
            value = value + table[span, :]
        result[span, :] = value
        return carry

    lax.fori_loop(0, total // GROUP, summed, 0)
    if not last:
        return

    def collect(target, bottom):
        for depth, (level_rows, cols) in enumerate(shapes):
            count = level_rows // 2

            def column(x, carry, depth=depth, count=count, cols=cols):
                cells = result[pl.ds(bases[depth] + x * strides[depth] + bottom * count, count), :]
                target[pl.ds(starts[depth] + x, count, stride=cols), :] = cells
                return carry

            lax.fori_loop(0, cols, column, 0, unroll=4)

    bottom = place[0]
    collect(own, bottom)
    collect(half, 1 - bottom)
    other[...] = half[...].astype(BF16)


def crop_backward(place, parameters, keep, passed, first, height, width, before=None):
    rows = keep.shape[0]
    shapes, strides, bases, total = level_plan(height, width)
    cells = half_starts(shapes)[-1]
    last = before is not None
    turned = pltpu.VMEM(((CELLS + 1) * GROUP, 128), F32)
    joined = pltpu.VMEM(keep.shape, BF16)
    tables = [pltpu.VMEM((total, 128), F32)] * CHAINS
    if last:
        out_shape = (
            jax.ShapeDtypeStruct((cells, 128), F32),
            jax.ShapeDtypeStruct((cells, 128), BF16),
        )
        scratch = [joined, turned, pltpu.VMEM((cells, 128), F32)] + tables
    else:
        out_shape = jax.ShapeDtypeStruct((total, 128), F32)
        scratch = [joined, turned] + tables
    return pl.pallas_call(
        functools.partial(spread_kernel, rows, first, height, width, last, len(passed)),
        out_shape=out_shape,
        in_specs=[smem()] * 5 + [vmem()] * ((2 if last else 1) + len(passed)),
        out_specs=(vmem(),) * 2 if last else vmem(),
        scratch_shapes=scratch,
        compiler_params=limits(52),
        cost_estimate=lasting(0.12 * rows),
        name="crop_backward",
    )(place, *parameters, keep, *passed, *([before] if last else []))


def natural_row(cell):
    k, i = divmod(cell, BINS)
    return i * BINS + k


def turn_kernel(
    counts,
    weight,
    sampled_far,
    second_far,
    out_far,
    bias_far,
    out,
    turned,
    tall,
    second,
    out_weight,
    hidden_bias,
    sampled,
    sems,
):
    held, lanes = weight.shape
    depth = second.shape[1]
    rows = out_weight.shape[0]
    half = PADDED // 2
    copies = [
        pltpu.make_async_copy(source, target, sems.at[at])
        for at, (source, target) in enumerate(
            (
                (second_far, second),
                (out_far, out_weight),
                (bias_far, hidden_bias),
                (sampled_far, sampled),
            )
        )
    ]
    for copy in copies:
        copy.start()
    for tile in range(CELLS):
        turned[tile * 128 : (tile + 1) * 128, 0:held] = jnp.transpose(
            weight[:, tile * 128 : (tile + 1) * 128]
        )
    for cell in range(CELLS):
        block = turned[pl.ds(natural_row(cell), 128, stride=CELLS), :]
        out[:, cell * 128 : (cell + 1) * 128] = jnp.transpose(block)[0:held].astype(BF16)
    for copy in copies:
        copy.wait()
    lane = lax.broadcasted_iota(jnp.int32, sampled.shape, 1)
    live = jnp.sum(
        jnp.where((lane < counts[0]) & (sampled[...] > 0), 1.0, 0.0), axis=1, keepdims=True
    )
    high = jnp.floor(live / 32.0)
    same = lax.broadcasted_iota(jnp.int32, (rows, rows), 0) == lax.broadcasted_iota(
        jnp.int32, (rows, rows), 1
    )
    biases = [
        jnp.sum(jnp.where(same, hidden_bias[at : at + 1, :], 0.0), axis=1, keepdims=True)
        for at in range(2)
    ]
    tall[...] = jnp.zeros_like(tall)
    tall[:, 0:WIDTH] = out_weight[...]
    column = lax.broadcasted_iota(jnp.int32, (rows, 128), 1) + (PADDED - 128)
    value = tall[:, PADDED - 128 : PADDED]
    for at, part in enumerate(
        (*biases, high, live - 32.0 * high)
    ):
        value = jnp.where(column == WIDTH + at, part, value)
    tall[:, PADDED - 128 : PADDED] = value
    out[:, lanes : lanes + depth] = second[...].astype(BF16)
    out[:, lanes + depth : lanes + depth + half] = jnp.concatenate(
        [tall[:, 0:half], tall[:, half:PADDED]], axis=0
    ).astype(BF16)


def turn_weight(counts, weight, sampled, second, out_weight, hidden_bias):
    held, lanes = weight.shape
    return pl.pallas_call(
        turn_kernel,
        out_shape=jax.ShapeDtypeStruct((held, lanes + second.shape[1] + PADDED // 2), BF16),
        in_specs=[smem(), vmem()] + [pl.BlockSpec(memory_space=pltpu.HBM)] * 4,
        out_specs=vmem(),
        scratch_shapes=[
            pltpu.VMEM((lanes, 128), F32),
            pltpu.VMEM((out_weight.shape[0], PADDED), F32),
            pltpu.VMEM(second.shape, F32),
            pltpu.VMEM(out_weight.shape, F32),
            pltpu.VMEM(hidden_bias.T.shape, F32),
            pltpu.VMEM((1, sampled.shape[0]), jnp.int32),
            pltpu.SemaphoreType.DMA((4,)),
        ],
        compiler_params=limits(62),
        cost_estimate=lasting(2.7),
        name="turn_weight",
    )(counts, weight, sampled[None], second, out_weight, hidden_bias.T)


def renew(weight, moment, average, grad, rate):
    step_value = grad + DECAY * weight
    moment_new = MOMENTUM * moment + step_value
    weight_new = weight - rate * (step_value + MOMENTUM * moment_new)
    average_new = AVERAGE * average + (1.0 - AVERAGE) * weight_new
    return (weight_new, moment_new, average_new)


def renew_kernel(rate, count, *refs):
    terms = refs[:count]
    kept = refs[count : count + 3]
    news = refs[count + 3 : count + 6]
    turned, *places = refs[count + 6 : count + 13]
    sems = refs[count + 13]
    held, lanes = terms[0].shape
    arrive = [
        pltpu.make_async_copy(kept[at], places[at], sems.at[at, 0]) for at in range(3)
    ]
    for copy in arrive:
        copy.start()
    for cell in range(CELLS):
        span = slice(cell * 128, (cell + 1) * 128)
        grad = terms[0][:, span].astype(F32)
        for term in terms[1:]:
            grad = grad + term[:, span].astype(F32)
        turned[pl.ds(natural_row(cell), 128, stride=CELLS), 0:held] = jnp.transpose(grad)
    for copy in arrive:
        copy.wait()
    leave = []
    for part in range(BINS):
        for tile in range(part * BINS, (part + 1) * BINS):
            span = slice(tile * 128, (tile + 1) * 128)
            grad = jnp.transpose(turned[span, :])[0:held]
            values = renew(*[place[:, span] for place in places[:3]], grad, rate)
            for at in range(3):
                places[3 + at][:, span] = values[at]
        span = pl.ds(part * BINS * 128, BINS * 128)
        for at in range(3):
            copy = pltpu.make_async_copy(
                places[3 + at].at[:, span], news[at].at[:, span], sems.at[at, 1 + part]
            )
            copy.start()
            leave.append(copy)
    for copy in leave:
        copy.wait()


def renew_first(terms, weight, moment, average, rate):
    held, lanes = weight.shape
    anywhere = pl.BlockSpec(memory_space=pl.ANY)
    return pl.pallas_call(
        functools.partial(renew_kernel, rate, len(terms)),
        out_shape=(jax.ShapeDtypeStruct(weight.shape, F32),) * 3,
        in_specs=[vmem()] * len(terms) + [anywhere] * 3,
        out_specs=(anywhere,) * 3,
        scratch_shapes=[pltpu.VMEM((lanes, 128), F32)]
        + [pltpu.VMEM((held, lanes), F32)] * 6
        + [pltpu.SemaphoreType.DMA((3, 1 + BINS))],
        compiler_params=limits(52),
        cost_estimate=lasting(6.5),
        name="renew_first",
    )(*terms, weight, moment, average)


def renew_small_kernel(rate, count, *refs):
    terms = refs[:count]
    second, tall, hidden, bias = (refs[count + 3 * at : count + 3 * at + 3] for at in range(4))
    second_new, tall_new, hidden_new, bias_new = (
        refs[count + 12 + 3 * at : count + 15 + 3 * at] for at in range(4)
    )
    loss = refs[count + 24]
    rows = tall[0].shape[0]
    depth = second[0].shape[1]
    half = PADDED // 2
    total = terms[0][...].astype(F32)
    for term in terms[1:]:
        total = total + term[...].astype(F32)

    def give(targets, sources, grad, rate):
        for target, value in zip(targets, renew(*[ref[...] for ref in sources], grad, rate)):
            target[...] = value

    give(second_new, second, total[:, :depth], rate)
    sums = jnp.concatenate([total[:rows, depth:], total[rows:, depth:]], axis=1)
    give(tall_new, tall, sums[:, :WIDTH], rate)
    same = lax.broadcasted_iota(jnp.int32, (rows, rows), 0) == lax.broadcasted_iota(
        jnp.int32, (rows, rows), 1
    )
    turned = [
        jnp.sum(jnp.where(same, sums[:, WIDTH + at : WIDTH + at + 1], 0.0), axis=0, keepdims=True)
        for at in range(2)
    ]
    give(hidden_new, hidden, jnp.concatenate(turned, axis=0), rate)
    spare = sums[:, PADDED - 128 : PADDED]
    start = BIAS_AT - (PADDED - 128)
    source = lax.broadcasted_iota(jnp.int32, (128, PADDED), 0)
    target = lax.broadcasted_iota(jnp.int32, (128, PADDED), 1)
    spread = jnp.dot(
        spare,
        jnp.where(source == start + target % 16, 1.0, 0.0),
        preferred_element_type=F32,
        precision=lax.Precision.HIGHEST,
    )
    row = lax.broadcasted_iota(jnp.int32, (rows, PADDED), 0)
    column = lax.broadcasted_iota(jnp.int32, (rows, PADDED), 1)
    line = jnp.sum(jnp.where(column // 16 == row, spread, 0.0), axis=0, keepdims=True)
    give(bias_new, bias, line[:, :WIDTH], 4.0)
    lane = lax.broadcasted_iota(jnp.int32, (rows, 128), 1) + (PADDED - 128)
    losses = jnp.where((lane >= LOSS_AT) & (lane < LOSS_AT + 3), spare, 0.0)
    loss[...] = jnp.sum(jnp.sum(losses, axis=1, keepdims=True), axis=0, keepdims=True)


def renew_small(terms, states, rate):
    states = [value for group in states for value in group]
    return pl.pallas_call(
        functools.partial(renew_small_kernel, rate, len(terms)),
        out_shape=tuple(jax.ShapeDtypeStruct(value.shape, F32) for value in states)
        + (jax.ShapeDtypeStruct((1, 1), F32),),
        in_specs=[vmem()] * (len(terms) + len(states)),
        out_specs=(vmem(),) * (len(states) + 1),
        compiler_params=limits(52),
        cost_estimate=lasting(2.0),
        name="renew_small",
    )(*terms, *states)


def map_sum_kernel(parts, own, *refs):
    passed, outs = refs[:parts], refs[parts:]
    ends = []
    for part in passed:
        ends.append((ends[-1] if ends else 0) + part.shape[0])
    start = 0
    for out in outs:
        end = start + out.shape[0]
        first = 0
        for part, last in zip(passed, ends):
            low, high = max(start, first), min(end, last)
            if low < high:
                out[low - start : high - start, :] = own[low:high, :] + part[
                    low - first : high - first, :
                ].astype(F32)
            first = last
        start = end


def map_sum(own, passed, maps):
    sizes = [level_map.shape[1] * level_map.shape[2] for level_map in maps]
    grads = pl.pallas_call(
        functools.partial(map_sum_kernel, len(passed)),
        out_shape=tuple(jax.ShapeDtypeStruct((size, own.shape[1]), F32) for size in sizes),
        in_specs=[vmem()] * (1 + len(passed)),
        out_specs=(vmem(),) * len(sizes),
        compiler_params=limits(52),
        cost_estimate=lasting(2.0),
        name="map_sum",
    )(own, *passed)
    return [grad.reshape(level_map.shape) for grad, level_map in zip(grads, maps)]


def gelu_parts(value):
    root = math.sqrt(2.0 / math.pi)
    square = value * value
    bend = jnp.tanh(root * (value + 0.044715 * square * value))
    half = 0.5 * (1.0 + bend)
    slope = half + 0.5 * value * (1.0 - bend * bend) * (
        root * (1.0 + 3.0 * 0.044715 * square)
    )
    return value * half, slope


def dot(left, right):
    return jnp.dot(left, right, preferred_element_type=F32)


def dot_last(left, right):
    return lax.dot_general(left, right, (((1,), (1,)), ((), ())), preferred_element_type=F32)


def middle_kernel(
    blocks,
    images,
    parts,
    order,
    *refs,
):
    pre_parts, refs = refs[: 2 * parts], refs[2 * parts :]
    middle_of(blocks, images, order, pre_parts, *refs)


def middle_of(
    blocks,
    images,
    order,
    pre_parts,
    second_turned_far,
    second_far,
    out_turned_far,
    out_weight,
    out_bias,
    slots,
    grad_own,
    grad_other,
    act_first,
    act_second,
    grad_second,
    grad_logits,
    losses,
    live_total,
    pre_first,
    slope_first,
    slope_second,
    grad_first,
    second_turned,
    second,
    out_turned,
    sems,
):
    copies = [
        pltpu.make_async_copy(source, target, sems.at[at])
        for at, (source, target) in enumerate(
            (
                (second_turned_far, second_turned),
                (out_turned_far, out_turned),
                (second_far, second),
            )
        )
    ]
    for copy in copies:
        copy.start()
    hidden, rows = pre_first.shape
    half = hidden // 2
    size = half // blocks
    own_start = order[3 * blocks] * half
    other_start = (1 - order[3 * blocks]) * half
    parts = len(pre_parts) // 2
    block = 0
    for own, other in zip(pre_parts[:parts], pre_parts[parts:]):
        for row in range(0, own.shape[0], size):
            at = pl.multiple_of(own_start + order[3 * blocks + 3 + block] * size, size)
            pre_first[pl.ds(at, size), :] = own[row : row + size, :]
            at = pl.multiple_of(other_start + order[3 * blocks + 3 + block] * size, size)
            pre_first[pl.ds(at, size), :] = other[row : row + size, :]
            block += 1
    spare = out_weight[:, PADDED - 128 : PADDED].astype(F32)
    at = WIDTH - (PADDED - 128)
    counted = 32.0 * spare[:, at + 2 : at + 3] + spare[:, at + 3 : at + 4]
    slots_total = jnp.sum(counted, axis=0, keepdims=True) * (images / hidden)
    live_total[...] = slots_total
    act, slope = gelu_parts(pre_first[...] + spare[:, at : at + 1])
    slope_first[...] = slope
    act_first[...] = act.astype(BF16)
    copies[0].wait()
    pre_second = (
        dot(second_turned[0], act_first[0:half, :])
        + dot(second_turned[1], act_first[half:hidden, :])
        + spare[:, at + 1 : at + 2]
    )
    act, slope = gelu_parts(pre_second)
    slope_second[...] = slope
    act_second[...] = act.astype(BF16)
    copies[1].wait()
    logits = dot(out_turned[...], act_second[...]) + out_bias[...]

    row = lax.broadcasted_iota(jnp.int32, logits.shape, 0)
    live = slots[0:1, :]
    scale = 1.0 / slots_total
    chosen = slots[2:3, :].astype(jnp.int32)
    foreground = jnp.where(chosen > 0, 1.0, 0.0)
    is_score = row < CLASSES
    top = jnp.max(jnp.where(is_score, logits, -jnp.inf), axis=0, keepdims=True)
    power = jnp.where(is_score, jnp.exp(logits - top), 0.0)
    total = jnp.sum(power, axis=0, keepdims=True)
    matches = row == chosen
    picked = jnp.sum(jnp.where(matches, logits, 0.0), axis=0, keepdims=True)
    value = jnp.log(total) + top - picked
    grad = power / total - jnp.where(matches, 1.0, 0.0)
    delta_row = CLASSES + 4 * (chosen - 1)
    smooth_total = jnp.zeros_like(live)
    for part in range(4):
        mine = (row == delta_row + part) & (chosen > 0)
        offset = jnp.sum(jnp.where(mine, logits, 0.0), axis=0, keepdims=True) - slots[
            3 + part : 4 + part, :
        ]
        size_of = jnp.abs(offset)
        near = size_of < SMOOTH
        smooth_total = smooth_total + jnp.where(
            near, 0.5 * offset * offset / SMOOTH, size_of - 0.5 * SMOOTH
        )
        slope = jnp.where(near, offset / SMOOTH, jnp.where(offset > 0.0, 1.0, -1.0))
        grad = jnp.where(mine, slope, grad)
    losses[...] = live * (value + foreground * smooth_total)
    grad_logits[...] = (grad * (live * scale)).astype(BF16)
    grad_second[...] = (dot(out_weight[...], grad_logits[...]) * slope_second[...]).astype(BF16)
    copies[2].wait()
    grad_first[...] = dot(second[...], grad_second[...]) * slope_first[...]
    for block in range(blocks):
        span = slice(block * size, (block + 1) * size)
        at = pl.multiple_of(own_start + order[block] * size, size)
        grad_own[span, :] = grad_first[pl.ds(at, size), :].astype(BF16)
        at = pl.multiple_of(other_start + order[block] * size, size)
        grad_other[span, :] = grad_first[pl.ds(at, size), :].astype(BF16)


def middle(blocks, images, order, pre_own, pre_other, *values):
    half, rows = (sum(part.shape[0] for part in pre_own), pre_own[0].shape[1])
    hidden = 2 * half
    low = lambda *shape: jax.ShapeDtypeStruct(shape, BF16)
    return pl.pallas_call(
        functools.partial(middle_kernel, blocks, images, len(pre_own)),
        out_shape=(
            low(half, rows),
            low(half, rows),
            low(hidden, rows),
            low(hidden, rows),
            low(hidden, rows),
            low(PADDED, rows),
            jax.ShapeDtypeStruct((1, rows), F32),
            jax.ShapeDtypeStruct((1, 1), F32),
        ),
        in_specs=[smem()]
        + [vmem()] * (2 * len(pre_own))
        + [pl.BlockSpec(memory_space=pl.ANY)] * 3
        + [vmem()] * (len(values) - 3),
        out_specs=(vmem(),) * 8,
        scratch_shapes=[pltpu.VMEM((hidden, rows), F32)] * 4
        + [pltpu.VMEM(value.shape, BF16) for value in values[:3]]
        + [pltpu.SemaphoreType.DMA((3,))],
        compiler_params=limits(52),
        cost_estimate=lasting(6.5),
        name="middle",
    )(order, *pre_own, *pre_other, *values)


def small_grads_kernel(
    blocks,
    parts,
    order,
    act_first,
    act_second,
    grad_second,
    grad_own,
    grad_other,
    grad_logits,
    losses,
    own,
    other,
    bias_out,
    second_sum,
    out_sum,
):
    hidden, rows = act_first.shape
    half = hidden // 2
    size = half // blocks
    section, fc, device = order[3 * blocks], order[3 * blocks + 1], order[3 * blocks + 2]
    for side in range(2):
        second_sum[side] = dot_last(
            grad_second[...], act_first[side * half : (side + 1) * half, :]
        ).astype(BF16)
    column = lax.broadcasted_iota(jnp.int32, (rows, PADDED), 1)
    value = dot_last(act_second[...], grad_logits[...])
    value = value + dot(grad_second[...], jnp.where(column == WIDTH + 1, 1.0, 0.0).astype(BF16))
    out_sum[...] = value
    ones = jnp.where(column == WIDTH, 1.0, 0.0).astype(BF16)
    for block in range(blocks):
        span = slice(block * size, (block + 1) * size)
        for values, where in ((grad_own, section), (grad_other, 1 - section)):
            at = pl.ds(pl.multiple_of(where * half + order[block] * size, size), size)
            out_sum[at, :] = out_sum[at, :] + dot(values[span, :], ones)
    bias = jnp.sum(grad_logits[...].astype(F32), axis=1, keepdims=True)
    bias_out[...] = bias
    part = size // 2
    if parts:
        tile = slice(PADDED - 128, PADDED)
        source = lax.broadcasted_iota(jnp.int32, (PADDED, 128), 0)
        target = lax.broadcasted_iota(jnp.int32, (PADDED, 128), 1) + (PADDED - 128)
        spread = jnp.where(target == BIAS_AT + source % 16, bias, 0.0).astype(BF16)
        row = lax.broadcasted_iota(jnp.int32, (hidden, PADDED), 0) % part
        pick = jnp.where(
            row == lax.broadcasted_iota(jnp.int32, (hidden, PADDED), 1) // 16, 1.0, 0.0
        ).astype(BF16)
        value = out_sum[:, tile] + dot(pick, spread)
        row = lax.broadcasted_iota(jnp.int32, (hidden, 128), 0) % part
        column = lax.broadcasted_iota(jnp.int32, (hidden, 128), 1) + (PADDED - 128)
        rest = jnp.sum(losses[...], axis=1, keepdims=True)
        for place in range(3):
            now = rest.astype(BF16).astype(F32)
            value = jnp.where((row == device) & (column == LOSS_AT + place), now, value)
            rest = rest - now
        out_sum[:, tile] = value
    for target, where in ((own, section), (other, 1 - section)):
        for near in range(2):
            lane = fc if near == 0 else 1 - fc
            for block in range(blocks):
                start = pl.multiple_of(where * half + order[blocks + block] * size, size)
                target[near, block * size : (block + 1) * size, 0:half] = second_sum[
                    lane, pl.ds(start, size), :
                ]
                at = pl.ds(pl.multiple_of(start + lane * part, part), part)
                for side in range(2):
                    target[
                        near,
                        block * size + side * part : block * size + (side + 1) * part,
                        half : half + PADDED // 2,
                    ] = out_sum[at, side * (PADDED // 2) : (side + 1) * (PADDED // 2)].astype(BF16)


def small_grads(
    blocks, parts, order, act_first, act_second, grad_second, grad_own, grad_other, grad_logits, losses
):
    hidden = act_first.shape[0]
    half = hidden // 2
    low = jax.ShapeDtypeStruct((2, half, half + PADDED // 2), BF16)
    return pl.pallas_call(
        functools.partial(small_grads_kernel, blocks, parts),
        out_shape=(low, low, jax.ShapeDtypeStruct((PADDED, 1), F32)),
        in_specs=[smem()] + [vmem()] * 7,
        out_specs=(vmem(),) * 3,
        scratch_shapes=[
            pltpu.VMEM((2, hidden, half), BF16),
            pltpu.VMEM((hidden, PADDED), F32),
        ],
        compiler_params=limits(52),
        cost_estimate=lasting(4.0),
        name="small_grads",
    )(order, act_first, act_second, grad_second, grad_own, grad_other, grad_logits, losses)


def assemble_kernel(blocks, order, *refs):
    sources, (second_turned, second, out_weight, out_turned) = refs[:-4], refs[-4:]
    hidden = second.shape[0]
    half = hidden // 2
    size = half // blocks
    part = size // 2
    section, fc = order[3 * blocks], order[3 * blocks + 1]
    first = 0
    for at in range(0, len(sources), 4):
        for index, source in enumerate(sources[at : at + 4]):
            where = section if index < 2 else 1 - section
            lane = fc if index % 2 == 0 else 1 - fc
            for block in range(source.shape[0] // size):
                rows = slice(block * size, (block + 1) * size)
                start = pl.multiple_of(
                    where * half + order[2 * blocks + first + block] * size, size
                )
                second_turned[lane, pl.ds(start, size), :] = source[rows, 0:half]
                target = pl.ds(pl.multiple_of(start + lane * part, part), part)
                for side in range(2):
                    out_weight[target, side * (PADDED // 2) : (side + 1) * (PADDED // 2)] = source[
                        block * size + side * part : block * size + (side + 1) * part,
                        half : half + PADDED // 2,
                    ]
        first += sources[at].shape[0] // size
    for side in range(2):
        second[side * half : (side + 1) * half, :] = jnp.transpose(second_turned[side])
    out_turned[...] = jnp.transpose(out_weight[...])


def assemble(blocks, order, groups):
    sources = [source for group in groups for source in group]
    half = sum(group[0].shape[0] for group in groups)
    hidden = 2 * half
    low = lambda *shape: jax.ShapeDtypeStruct(shape, BF16)
    return pl.pallas_call(
        functools.partial(assemble_kernel, blocks),
        out_shape=(low(2, hidden, half), low(hidden, hidden), low(hidden, PADDED), low(PADDED, hidden)),
        in_specs=[smem()] + [vmem()] * len(sources),
        out_specs=(vmem(),) * 4,
        compiler_params=limits(52),
        cost_estimate=lasting(5.0),
        name="assemble",
    )(order, *sources)


def lane_blocks(lanes):
    for parts in (7, 1):
        if lanes % (128 * parts) == 0:
            return parts, lanes // parts


def join_kernel(straight, passed_head, crossed, passed_tail, moving, cross):
    half = straight.shape[0] // 2
    moving[0:half, :] = (
        straight[0:half, :].astype(F32) + passed_head[...].astype(F32)
    ).astype(BF16)
    moving[half : 2 * half, :] = straight[half : 2 * half, :]
    cross[0:half, :] = crossed[0:half, :]
    cross[half : 2 * half, :] = (
        crossed[half : 2 * half, :].astype(F32) + passed_tail[...].astype(F32)
    ).astype(BF16)


def join(straight, passed_head, blocks, at, passed_tail):
    held, lanes = straight.shape
    return pl.pallas_call(
        join_kernel,
        out_shape=(jax.ShapeDtypeStruct(straight.shape, BF16),) * 2,
        grid=(1,),
        in_specs=[
            pl.BlockSpec((held, lanes), lambda step: (0, 0)),
            pl.BlockSpec((held // 2, lanes), lambda step: (0, 0)),
            pl.BlockSpec((held, lanes), lambda step: (at, 0)),
            pl.BlockSpec((held // 2, lanes), lambda step: (0, 0)),
        ],
        out_specs=(pl.BlockSpec((held, lanes), lambda step: (0, 0)),) * 2,
        compiler_params=limits(52),
        cost_estimate=lasting(1.5),
        name="join",
    )(straight, passed_head, blocks, passed_tail)


def input_grad_kernel(count, grad, *refs):
    weight = jnp.concatenate([ref[...] for ref in refs[:count]], axis=0)
    value = dot(grad[...], weight).astype(BF16)
    start = 0
    for out in refs[count:]:
        out[...] = value[start : start + out.shape[0]]
        start += out.shape[0]


def input_grad(grad, pieces, sizes, lanes):
    parts, size = lane_blocks(lanes)
    return pl.pallas_call(
        functools.partial(input_grad_kernel, len(pieces)),
        out_shape=tuple(jax.ShapeDtypeStruct((rows, lanes), BF16) for rows in sizes),
        grid=(parts,),
        in_specs=[pl.BlockSpec(grad.shape, lambda step: (0, 0))]
        + [pl.BlockSpec((piece.shape[0], size), lambda step: (0, step)) for piece in pieces],
        out_specs=tuple(pl.BlockSpec((rows, size), lambda step: (0, step)) for rows in sizes),
        compiler_params=limits(52),
        cost_estimate=lasting(5.0),
        name="input_grad",
    )(grad, *pieces)


def line_order(line):
    return (0, 1, 3, 2) if line == 4 else tuple(range(line))


def pair_swap(value, count):
    return lax.ppermute(value, "wide", [(at, at ^ 1) for at in range(count)])


def line_step(value, count, way=1):
    places = line_order(count // 2)
    steps = []
    for at, place in enumerate(places):
        target = places[(at + way) % len(places)]
        steps += [(2 * place + side, 2 * target + side) for side in range(2)]
    return lax.ppermute(value, "wide", sorted(steps))


def line_swap(value, count, bit):
    return lax.ppermute(value, "wide", [(at, at ^ (2 * bit)) for at in range(count)])


def swap(value, axis):
    return lax.ppermute(value, axis, [(0, 1), (1, 0)])


def together(*values):
    return lax.optimization_barrier(values)


def add(*terms):
    total = terms[0].astype(F32)
    for term in terms[1:]:
        total = total + term.astype(F32)
    return total.astype(BF16)


def ring_order(wide, line):
    places = line_order(line)
    here = sum((jnp.where(wide // 2 == place, at, 0) for at, place in enumerate(places)))
    table = lambda index: sum(
        (jnp.where(index == at, place, 0) for at, place in enumerate(places))
    )
    return [
        table((here - step) % line) * 2 + ((wide % 2) ^ side)
        for side in range(2)
        for step in range(line)
    ]


def swap_order(wide, line):
    return [
        ((wide // 2) ^ step) * 2 + ((wide % 2) ^ side) for side in range(2) for step in range(line)
    ]


def split_tall(terms, n_wide):
    sections, places, half, columns = terms.shape
    held = half // n_wide
    second = terms[..., : columns - PADDED // 2].reshape(sections, places, n_wide, held, -1)
    out = terms[..., columns - PADDED // 2 :].reshape(sections, places, 2, half // 2, PADDED // 2)
    out = jnp.transpose(out, (0, 1, 3, 2, 4)).reshape(sections, half, PADDED)
    out = out.reshape(sections, n_wide, places, held // places, 2, PADDED // 2)
    out = jnp.transpose(out, (0, 2, 1, 4, 3, 5)).reshape(sections, places, n_wide, held, -1)
    return jnp.concatenate([second, out], axis=-1)


def body(
    map_p2,
    map_p3,
    map_p4,
    map_p5,
    boxes,
    levels,
    classes,
    sampled,
    counts,
    targets,
    first_weight,
    second_weight,
    out_weight,
    hidden_bias,
    out_bias,
    first_moment,
    second_moment,
    out_moment,
    hidden_moment,
    bias_moment,
    first_average,
    second_average,
    out_average,
    hidden_average,
    bias_average,
):
    n_section = lax.axis_size("section")
    n_fc = lax.axis_size("fc")
    n_wide = lax.axis_size("wide")
    section = lax.axis_index("section")
    fc = lax.axis_index("fc")
    wide = lax.axis_index("wide")
    everywhere = ("section", "wide", "fc")
    maps = [map_p2, map_p3, map_p4, map_p5]
    channels = map_p2.shape[3]
    height = map_p2.shape[1] * n_section
    width = map_p2.shape[2]
    rows_dev = boxes.shape[0]
    rows_own = rows_dev // (n_section * n_fc)
    held = first_weight.shape[1]
    classes_out = out_weight.shape[1]
    place = section.astype(jnp.int32).reshape(1)

    ring = n_wide == 8
    line = n_wide // 2
    rows_tall = out_weight.shape[0]
    rows_fc = n_section * rows_own
    half_held = held // 2
    lanes = first_weight.shape[0]

    place = jnp.stack([section, fc]).astype(jnp.int32)

    turned = turn_weight(
        counts, first_weight.T, sampled, second_weight.T, out_weight, hidden_bias
    )
    slot_parts = (counts, boxes, levels, classes, sampled, targets)
    turned, maps, slot_parts = together(turned, maps, slot_parts)
    if ring:
        places = ring_order(wide, line)
        small_at = [0, 1, 3, 4, 2, 5, 7, 6]
        order = jnp.stack(
            places
            + swap_order(wide, line)
            + [places[at] for at in small_at]
            + [section, fc, (section * n_wide + wide) * n_fc + fc]
            + [places[at] for at in (0, 1, 2, 4, 5, 3, 6, 7)]
        ).astype(jnp.int32)
        blocks = n_wide
        straight = [turned, line_step(turned, n_wide)]
        crossed = [pair_swap(turned, n_wide)]
        last_small = line_step(turned[:, lanes:], n_wide, -1)
    else:
        zero = jnp.zeros_like(section)
        order = jnp.stack([zero, zero, zero, section, fc, zero, zero]).astype(jnp.int32)
        blocks = 1
    half_own = jnp.concatenate([level_map.reshape(-1, channels) for level_map in maps], axis=0)
    half_other = swap(half_own, "section")
    *parameters, slots = plan(place, *slot_parts, n_fc * rows_own, height, width)
    table = build_table(place, half_own, half_other, height, width)

    crops_mine = crop_forward(parameters, table, 0, rows_own)
    if ring:
        straight[1], crossed[0], last_small, table, crops_mine = together(
            straight[1], crossed[0], last_small, table, crops_mine
        )
        small_of = lambda piece: piece[:, lanes:]
        small_a = jnp.concatenate(
            [small_of(straight[0]), small_of(straight[1]), last_small, small_of(crossed[0])], axis=0
        )
        straight.append(line_step(straight[1], n_wide))
        crossed.append(pair_swap(straight[1], n_wide))
        last_crossed = pair_swap(last_small, n_wide)
        passed_a = swap(small_a, "fc")
    passed_mine = swap(crops_mine, "section")
    crops_theirs = crop_forward(parameters, table, rows_own, rows_own)

    if ring:
        straight[2], crossed, last_crossed, passed_mine, crops_theirs, small_a, passed_a = together(
            straight[2], crossed, last_crossed, passed_mine, crops_theirs, small_a, passed_a
        )
        straight.append(line_step(straight[2], n_wide))
        crossed.append(pair_swap(straight[2], n_wide))
        small_b = jnp.concatenate(
            [small_of(straight[2]), small_of(crossed[1]), last_crossed], axis=0
        )
        passed_b = swap(small_b, "fc")
        passed_theirs = swap(crops_theirs, "section")
        weight_of = lambda piece: piece[:, :lanes]
        early_weight = jnp.concatenate(
            [weight_of(piece) for piece in straight[:3] + crossed[:2]], axis=0
        )
        inputs_all = jnp.concatenate([crops_mine, passed_mine, crops_theirs, passed_theirs], axis=0)
        early = dot_last(early_weight, inputs_all)
        early, early_passed = early[:, :rows_fc], swap(early[:, rows_fc:].astype(BF16), "fc")
        straight[3], crossed[2], inputs_all, early, small_b, passed_b = together(
            straight[3], crossed[2], inputs_all, early, small_b, passed_b
        )
        tail = [
            pair_swap(straight[3][:half_held, :lanes], n_wide),
            line_step(crossed[2][half_held:, :lanes], n_wide),
        ]
        small_c = small_of(crossed[2])
        late = dot_last(
            jnp.concatenate([weight_of(straight[3]), weight_of(crossed[2])], axis=0), inputs_all
        )
        passed_c = swap(small_c, "fc")
        groups = [
            [small, passed, swap(small, "section"), swap(passed, "section")]
            for small, passed in ((small_a, passed_a), (small_b, passed_b))
        ]
        early = early + early_passed.astype(F32)
        tail, late, early, passed_c, inputs_all = together(tail, late, early, passed_c, inputs_all)
        last = jnp.concatenate(tail, axis=0)
        end = dot_last(last, inputs_all)
        late, late_passed = late[:, :rows_fc], swap(late[:, rows_fc:].astype(BF16), "fc")
        early_other = swap(early[:, rows_own:], "section")
        end_passed = end[:, rows_fc:].astype(BF16)
        end_passed, end, early, early_other, late, late_passed, groups = together(
            end_passed, end, early, early_other, late, late_passed, groups
        )
        end_passed = swap(end_passed, "fc")
        late = late + late_passed.astype(F32)
        late_other = swap(late[:, rows_own:], "section")
        groups.append([small_c, passed_c, swap(small_c, "section"), swap(passed_c, "section")])
        small_weights = assemble(blocks, order, groups)
        end_passed, small_weights, late, late_other = together(
            end_passed, small_weights, late, late_other
        )
        w_second_turned, w_second, w_out, w_out_turned = small_weights
        end = end[:, :rows_fc] + end_passed.astype(F32)
        end_other = swap(end[:, rows_own:], "section")
        pre_own = [part[:, :rows_own] for part in (early, late, end)]
        pre_other = [early_other, late_other, end_other]
        pieces = straight + crossed + [last]
    else:
        passed_theirs = swap(crops_theirs, "section")
        inputs_all = jnp.concatenate([crops_mine, passed_mine, crops_theirs, passed_theirs], axis=0)
        pieces = [lax.all_gather(turned[:, :lanes], "wide", axis=0, tiled=True)]
        pre = dot_last(pieces[0], inputs_all)
        pre = pre[:, :rows_fc] + swap(pre[:, rows_fc:], "fc")
        pre_own, pre_other = [pre[:, :rows_own]], [swap(pre[:, rows_own:], "section")]
        small = lax.all_gather(turned[:, lanes:], everywhere, axis=0, tiled=True)
        small = small.reshape(-1, n_fc, held, turned.shape[1] - lanes)
        w_second_turned = jnp.transpose(
            small[..., : second_weight.shape[0]], (1, 0, 2, 3)
        ).reshape(n_fc, -1, second_weight.shape[0])
        w_second = jnp.transpose(w_second_turned, (0, 2, 1)).reshape(
            -1, w_second_turned.shape[1]
        )
        w_out = small[..., second_weight.shape[0] :].reshape(-1, 2, rows_tall, PADDED // 2)
        w_out = jnp.transpose(w_out, (0, 2, 1, 3)).reshape(-1, PADDED)
        w_out_turned = w_out.T
    grad_own, grad_other, act_first, act_second, grad_second, grad_logits, losses, total = middle(
        blocks,
        n_wide,
        order,
        pre_own,
        pre_other,
        w_second_turned,
        w_second,
        w_out_turned,
        w_out,
        jnp.pad(out_bias, (0, PADDED - classes_out))[:, None],
        slots,
    )
    grad_passed = swap(grad_other, "section")
    grad_passed, grad_own, act_first = together(grad_passed, grad_own, act_first)
    grad_mine = jnp.concatenate([grad_own, grad_passed], axis=1)
    rate = 0.15 * math.sqrt(rows_dev * n_wide)
    back = lambda sent: swap(sent, "section")

    if ring:
        def all_slots(parts):
            mine = jnp.concatenate([grad_mine[at * held : (at + 1) * held] for at in parts], axis=0)
            return jnp.concatenate([mine, swap(mine, "fc")], axis=1)

        def block(values, at):
            return values[at * held : (at + 1) * held]

        rest_at = [0, 2, 3, line, line + 2, line + 3]
        first_grads = all_slots([1, line + 1])
        terms_own, terms_other, bias_terms = small_grads(
            blocks, True, order, act_first, act_second, grad_second, grad_own, grad_other, grad_logits, losses
        )
        first_grads, terms_own, terms_other = together(first_grads, terms_own, terms_other)
        first_terms = dot(first_grads, inputs_all).astype(BF16)
        rest_grads = all_slots(rest_at)
        first_terms, rest_grads, terms_other = together(first_terms, rest_grads, terms_other)
        moving, cross = block(first_terms, 0), block(first_terms, 1)
        tail = line_step(cross[half_held:], n_wide)
        head = pair_swap(cross[:half_held], n_wide)
        small = swap(terms_other, "section")
        rest = dot(rest_grads, inputs_all).astype(BF16)
        small = [add(terms_own[at], small[at]) for at in range(n_fc)]
        tail, head, rest, small, first_grads, rest_grads = together(
            tail, head, rest, small, first_grads, rest_grads
        )

        moving, cross = join(moving, head, rest, 4, tail)
        moving, cross, rest_grads = together(moving, cross, rest_grads)
        cross = pair_swap(cross, n_wide)
        moving = line_step(moving, n_wide)
        small_passed = swap(small[1], "fc")
        grad_all = jnp.concatenate(
            [
                block(rest_grads, 0),
                first_grads[:held],
                rest_grads[held : 3 * held],
                block(rest_grads, 3),
                first_grads[held:],
                rest_grads[4 * held :],
            ],
            axis=0,
        )
        keep_mine, send_mine, keep_theirs, send_theirs = input_grad(
            grad_all.T, pieces, [rows_own] * 4, lanes
        )
        sent_later = [block(rest, 5), block(rest, 3)]
        moving, cross, rest, sent_later, keep_mine, keep_theirs, send_mine, send_theirs, small_passed = together(
            moving, cross, rest, sent_later, keep_mine, keep_theirs, send_mine, send_theirs, small_passed
        )

        back_mine = [back(send_mine)]
        moving = add(block(rest, 1), cross, moving)
        moving, keep_mine = together(moving, keep_mine)
        moving = line_step(moving, n_wide)
        cross = pair_swap(sent_later[0], n_wide)
        before = crop_backward(place, parameters, keep_mine, back_mine, 0, height, width)
        small = add(small[0], small_passed)
        moving, cross, rest, sent_later, before, keep_theirs, send_theirs, small = together(
            moving, cross, rest, sent_later, before, keep_theirs, send_theirs, small
        )

        back_theirs = [back(send_theirs)]
        moving = add(block(rest, 2), cross, moving)
        moving, before = together(moving, before)
        moving = line_step(moving, n_wide)
        cut = small.shape[0] // 2
        cross = pair_swap(sent_later[1], n_wide)
        small_passed = pair_swap(small[cut:], n_wide)
        map_own, map_other = crop_backward(
            place, parameters, keep_theirs, back_theirs, rows_own, height, width, before
        )
        small_passed, map_own, map_other = together(small_passed, map_own, map_other)
        small = add(small[:cut], small_passed)
        small_terms = [small[:held]] + [
            line_swap(small[bits * held : (bits + 1) * held], n_wide, bits)
            for bits in range(1, line)
        ]
        cut = map_other.shape[0] // (2 * GROUP) * GROUP
        map_passed = [swap(map_other[:cut], "section"), swap(map_other[cut:], "section")]
        map_grads = map_sum(map_own, map_passed, maps)
        moving, cross, map_grads = together(moving, cross, map_grads)
        first_sums = [block(rest, 0), cross, moving]
    else:
        grad_all = jnp.concatenate([grad_mine, swap(grad_mine, "fc")], axis=1)
        first_sums = [
            lax.psum_scatter(
                dot(grad_all, inputs_all).astype(BF16), "wide", scatter_dimension=0, tiled=True
            )
        ]
        keep_mine, send_mine, keep_theirs, send_theirs = input_grad(
            grad_all.T, pieces, [rows_own] * 4, lanes
        )
        before = crop_backward(place, parameters, keep_mine, [back(send_mine)], 0, height, width)
        map_own, map_other = crop_backward(
            place, parameters, keep_theirs, [back(send_theirs)], rows_own, height, width, before
        )
        map_grads = map_sum(map_own, [swap(map_other, "section")], maps)
        terms_own, terms_other, bias_terms = small_grads(
            blocks, False, order, act_first, act_second, grad_second, grad_own, grad_other, grad_logits, losses
        )
        terms = jnp.stack(
            [jnp.where(section == at, terms_own, terms_other) for at in range(n_section)]
        )
        terms = jnp.where(fc == 0, terms, terms[:, ::-1])
        terms = jnp.transpose(split_tall(terms, n_wide), (0, 2, 1, 3, 4))
        small_sum = lax.psum_scatter(
            terms.reshape(-1, terms.shape[-1]), everywhere, scatter_dimension=0, tiled=True
        ).astype(F32)
    first_out = renew_first(first_sums, first_weight.T, first_moment.T, first_average.T, rate)
    if ring:
        first_out, small_terms = together(first_out, small_terms)
        small_out = renew_small(
            small_terms,
            (
                (second_weight.T, second_moment.T, second_average.T),
                (out_weight, out_moment, out_average),
                (hidden_bias.T, hidden_moment.T, hidden_average.T),
                (out_bias[None], bias_moment[None], bias_average[None]),
            ),
            rate,
        )
        *small_out, loss_sum = small_out
        loss_sum = loss_sum[0, 0]
        second_out = [value.T for value in small_out[:3]]
        out_out, hidden_out = small_out[3:6], [value.T for value in small_out[6:9]]
        bias_out = [value[0] for value in small_out[9:]]
    else:
        second_sum = small_sum[:, : second_weight.shape[0]]
        tall_sum = small_sum[:, second_weight.shape[0] :]
        tall_sum = jnp.concatenate([tall_sum[:rows_tall], tall_sum[rows_tall:]], axis=1)
        vector = jnp.concatenate([bias_terms[:classes_out, 0], jnp.sum(losses).reshape(1)])
        vector = lax.psum(vector, everywhere)
        loss_sum = vector[classes_out]
        second_out = renew(second_weight, second_moment, second_average, second_sum.T, rate)
        out_out = renew(out_weight, out_moment, out_average, tall_sum[:, :classes_out], rate)
        hidden_out = renew(
            hidden_bias,
            hidden_moment,
            hidden_average,
            tall_sum[:, classes_out : classes_out + 2],
            rate,
        )
        bias_out = renew(out_bias, bias_moment, bias_average, vector[:classes_out], 4.0)
    return (
        loss_sum,
        total[0, 0],
        map_grads[0],
        map_grads[1],
        map_grads[2],
        map_grads[3],
        first_out[0].T,
        first_out[1].T,
        first_out[2].T,
        *second_out,
        *out_out,
        *hidden_out,
        *bias_out,
    )


def solution(mesh):
    maps = P("wide", "section", None, "fc")
    wide_weight = P("fc", ("section", "wide"))
    tall_weight = P(("section", "wide", "fc"), None)
    in_specs = (
        (maps,) * 4
        + (P("wide", None), P("wide"), P("wide"), P("wide"), P("wide"), P("wide", None))
        + (wide_weight, wide_weight, tall_weight, tall_weight, P()) * 3
    )
    out_specs = (
        (P(), P())
        + (maps,) * 4
        + (wide_weight,) * 6
        + (tall_weight,) * 6
        + (P(),) * 3
    )
    return jax.shard_map(body, mesh=mesh, in_specs=in_specs, out_specs=out_specs, check_vma=False)
```
